32 devices in a mesh: dp: 2 (over x), seq: 8 (over z, core), tp: 2 (over y).
Axes of the slice: x: 2, y: 2, z: 4, core: 2. Of those that a mesh axis runs over, the one named last changes fastest.
Arguments:
- block_input: bfloat16 [8, 1024, 2048], P('dp', 'seq'), may hold values from -6 to 6
- initial_state: float32 [8, 32, 64, 64], P('dp', 'tp'), may hold values from -6 to 6
- norm_gains: bfloat16 [2, 2048], P(None, ('dp', 'seq')), may hold values from 0.5 to 1.5
- norm_biases: bfloat16 [2, 2048], P(None, ('dp', 'seq')), may hold values from -1.5 to 1.5
- mixing_coefficients: bfloat16 [8, 2048], P(None, ('dp', 'seq')), may hold values from 0 to 1
- mix_down: bfloat16 [2048, 160], P(('dp', 'seq')), may hold values from -0.125 to 0.125
- mixing_up_weight: bfloat16 [160, 2048], P(None, ('dp', 'seq')), may hold values from -0.5 to 0.5
- decay_down: bfloat16 [2048, 64], P(('dp', 'seq')), may hold values from -0.125 to 0.125
- decay_up: bfloat16 [64, 32, 64], P(None, 'tp', ('dp', 'seq')), may hold values from -0.5 to 0.5
- proj_weights: bfloat16 [4, 2048, 2048], P(None, ('dp', 'seq'), 'tp'), may hold values from -0.125 to 0.125
- out_weight: bfloat16 [2048, 2048], P('tp', ('dp', 'seq')), may hold values from -0.25 to 0.25
- time_decay: bfloat16 [32, 64], P('tp', ('dp', 'seq')), may hold values from -12 to -2
- time_first: bfloat16 [32, 64], P('tp', ('dp', 'seq')), may hold values from -0.5 to 1.5
- group_gain: bfloat16 [32, 64], P('tp', ('dp', 'seq')), may hold values from 0.5 to 1.5
- group_bias: bfloat16 [32, 64], P('tp', ('dp', 'seq')), may hold values from -1.5 to 1.5
- channel_key: bfloat16 [2048, 7168], P(None, 'tp'), may hold values from -0.125 to 0.125
- channel_value: bfloat16 [7168, 2048], P('tp'), may hold values from -0.0625 to 0.0625
- channel_recept: bfloat16 [2048, 2048], P(None, 'tp'), may hold values from -0.125 to 0.125
- out_grad: bfloat16 [8, 1024, 2048], P('dp', 'seq', 'tp'), may hold values from -6 to 6
Outputs:
- output: bfloat16 [8, 1024, 2048], P('dp', 'seq', 'tp')
- input_grad: float32 [8, 1024, 2048], P('dp', 'seq', 'tp')
- state_grad: float32 [8, 32, 64, 64], P('dp', 'tp')
- norm_gains_grad: float32 [2, 2048], P(None, ('dp', 'seq'))
- norm_biases_grad: float32 [2, 2048], P(None, ('dp', 'seq'))
- mix_coeffs_grad: float32 [7, 2048], P(None, ('dp', 'seq'))
- decay_coeff_grad: float32 [1, 2048], P(None, ('dp', 'seq'))
- mix_down_grad: float32 [2048, 160], P(('dp', 'seq'))
- mix_up_grad: float32 [160, 2048], P(None, ('dp', 'seq'))
- decay_down_grad: float32 [2048, 64], P(('dp', 'seq'))
- decay_up_grad: float32 [64, 32, 64], P(None, 'tp', ('dp', 'seq'))
- proj_weights_grad: float32 [4, 2048, 2048], P(None, ('dp', 'seq'), 'tp')
- out_weight_grad: float32 [2048, 2048], P('tp', ('dp', 'seq'))
- time_decay_grad: float32 [32, 64], P('tp', ('dp', 'seq'))
- time_first_grad: float32 [32, 64], P('tp', ('dp', 'seq'))
- group_gain_grad: float32 [32, 64], P('tp', ('dp', 'seq'))
- group_bias_grad: float32 [32, 64], P('tp', ('dp', 'seq'))
- channel_key_grad: float32 [2048, 7168], P(('dp', 'seq'), 'tp')
- channel_value_grad: float32 [7168, 2048], P('tp', ('dp', 'seq'))
- channel_recept_grad: float32 [2048, 2048], P(('dp', 'seq'), 'tp')
- decay_min: float32 [8, 32], P('dp', 'tp')
- decay_max: float32 [8, 32], P('dp', 'tp')
The draws below stay inside these ranges and needn't reach their ends.
All inputs are finite; a program needn't handle non-finite values.
Results may differ from the reference program's by a relative error of at most 0.015.
The reference program's roundings to bfloat16 on the way count: a program that leaves them out, or rounds other values in their place, can miss the bound.
Values may be sent and summed in bfloat16 or wider, within the bound.
A program may use at most 512 MiB of HBM per device.

```python
import jax
import jax.numpy as jnp
from jax import lax

HEADS = 32
HEAD = 64
MODEL_WIDTH = 2048
FF = 7168
MIXER_RANK = 32
DECR = 64
SPAN = 128
SEQUENCE_TOKENS = 1024
BATCH = 8


def level_of(own_key, extent, split, low, largest):
    level, own = 1.0, jax.random.fold_in(own_key, 6)
    for axis_at, shards_of in split:
        draws = jnp.exp(jax.random.uniform(jax.random.fold_in(own, axis_at), (shards_of,), jnp.float32, low / len(split), largest / len(split)))
        level = level * jnp.repeat(draws, extent[axis_at] // shards_of).reshape([-1 if axis == axis_at else 1 for axis in range(len(extent))])
    return level


def scatter_about(rng, extent, scale, most, cuts=(), kind=jnp.bfloat16):
    values = scale * jax.random.normal(rng, extent, jnp.float32)
    if cuts:
        values = values * level_of(rng, extent, cuts, -0.22, 0.18)
    return jnp.clip(values, -most, most).astype(kind)


def setup_inputs(seed: int = 0) -> dict:
    key_of = jax.random.split(jax.random.key(seed), 20)
    return {
        "block_input": scatter_about(key_of[0], (BATCH, SEQUENCE_TOKENS, MODEL_WIDTH), 1.0, 6.0, ((0, 2), (1, 8))),
        "initial_state": scatter_about(key_of[1], (BATCH, HEADS, HEAD, HEAD), 1.0, 6.0, ((0, 2), (1, 2)), jnp.float32),
        "norm_gains": jnp.clip(1.0 + 0.1 * jax.random.normal(key_of[2], (2, MODEL_WIDTH), jnp.float32), 0.5, 1.5).astype(jnp.bfloat16),
        "norm_biases": scatter_about(key_of[3], (2, MODEL_WIDTH), 0.3, 1.5, ((1, 16),)),
        "mixing_coefficients": jnp.clip(1.0 * jax.random.uniform(key_of[4], (8, MODEL_WIDTH), jnp.float32) ** level_of(key_of[4], (8, MODEL_WIDTH), ((1, 16),), -0.2, 0.2), 0.0, 1.0).astype(jnp.bfloat16),
        "mix_down": scatter_about(key_of[5], (MODEL_WIDTH, 5 * MIXER_RANK), MODEL_WIDTH ** -0.5, 0.125, ((0, 16),)),
        "mixing_up_weight": scatter_about(key_of[6], (5 * MIXER_RANK, MODEL_WIDTH), (4 * MIXER_RANK) ** -0.5, 0.5, ((1, 16),)),
        "decay_down": scatter_about(key_of[7], (MODEL_WIDTH, DECR), MODEL_WIDTH ** -0.5, 0.125, ((0, 16),)),
        "decay_up": scatter_about(key_of[8], (DECR, HEADS, HEAD), (2 * DECR) ** -0.5, 0.5, ((1, 2), (2, 16))),
        "proj_weights": scatter_about(key_of[9], (4, MODEL_WIDTH, MODEL_WIDTH), MODEL_WIDTH ** -0.5, 0.125, ((1, 16), (2, 2))),
        "out_weight": scatter_about(key_of[10], (MODEL_WIDTH, MODEL_WIDTH), (MODEL_WIDTH // 4) ** -0.5, 0.25, ((0, 2), (1, 16))),
        "time_decay": jnp.clip(-12.0 + 10.0 * jax.random.uniform(key_of[11], (HEADS, HEAD), jnp.float32) ** level_of(key_of[11], (HEADS, HEAD), ((0, 2), (1, 16)), -0.2, 0.2), -12.0, -2.0).astype(jnp.bfloat16),
        "time_first": jnp.clip(-0.5 + 2.0 * jax.random.uniform(key_of[12], (HEADS, HEAD), jnp.float32) ** level_of(key_of[12], (HEADS, HEAD), ((0, 2), (1, 16)), -0.2, 0.2), -0.5, 1.5).astype(jnp.bfloat16),
        "group_gain": jnp.clip(1.0 + 0.1 * jax.random.normal(key_of[13], (HEADS, HEAD), jnp.float32), 0.5, 1.5).astype(jnp.bfloat16),
        "group_bias": scatter_about(key_of[14], (HEADS, HEAD), 0.3, 1.5, ((0, 2), (1, 16))),
        "channel_key": scatter_about(key_of[15], (MODEL_WIDTH, FF), MODEL_WIDTH ** -0.5, 0.125, ((1, 2),)),
        "channel_value": scatter_about(key_of[16], (FF, MODEL_WIDTH), FF ** -0.5, 0.0625, ((0, 2),)),
        "channel_recept": scatter_about(key_of[17], (MODEL_WIDTH, MODEL_WIDTH), MODEL_WIDTH ** -0.5, 0.125, ((1, 2),)),
        "out_grad": scatter_about(key_of[18], (BATCH, SEQUENCE_TOKENS, MODEL_WIDTH), 1.0, 6.0, ((0, 2), (1, 8), (2, 2))),
    }


PRECISION_TOP = lax.Precision.HIGHEST
NORM_EPS = 1e-05
GROUP_EPS = 0.00064

@jax.custom_vjp
def low(v):
    return lax.optimization_barrier(v.astype(jnp.bfloat16)).astype(jnp.float32)

@jax.custom_vjp
def low_back(v):
    return v

def low_keep(v):
    return (low(v), None)

def low_pass(kept, grad):
    return (grad,)

def back_keep(v):
    return (v, None)

def back_low(kept, grad):
    return (low(grad),)
low.defvjp(low_keep, low_pass)
low_back.defvjp(back_keep, back_low)

def matmul_f32(left, right):
    return jnp.einsum('...i,ij->...j', left, right, precision=PRECISION_TOP, preferred_element_type=jnp.float32)

def layer_norm(values, scale_row, shift_row):
    mean_val = lax.optimization_barrier(jnp.mean(values, axis=-1, keepdims=True))
    centered = values - mean_val
    variance = lax.optimization_barrier(jnp.mean(centered * centered, axis=-1, keepdims=True))
    return centered * lax.rsqrt(variance + NORM_EPS) * scale_row + shift_row

def shifted(values):
    return jnp.concatenate([jnp.zeros_like(values[:, :1, :]), values[:, :-1, :]], axis=1)

def scaled_payload_series(acceptance_entries_list, lookup_array_entries, payload_array_entries, fading_multiplier, initial_reward_vector, starting_carry_tensor):
    batch_rows = acceptance_entries_list.shape[0]
    blocks = SEQUENCE_TOKENS // SPAN

    def to_blocks(rows):
        return jnp.transpose(rows, (1, 0, 2, 3)).reshape(blocks, SPAN, batch_rows, HEADS, HEAD)

    def token_step(handed_carry_tensor, token_rows):
        present_acceptance_vector, key_now, value_now, decay_now = token_rows
        tensor_pairing_result = key_now[..., :, None] * value_now[..., None, :]
        present_result_block = lax.optimization_barrier(jnp.sum(present_acceptance_vector[..., :, None] * (handed_carry_tensor + initial_reward_vector[None, :, :, None] * tensor_pairing_result), axis=-2))
        return (decay_now[..., None] * handed_carry_tensor + tensor_pairing_result, present_result_block)

    def block_step(handed_carry_tensor, block_rows):
        return lax.scan(token_step, handed_carry_tensor, block_rows)
    final_state, outputs = lax.scan(jax.checkpoint(block_step), starting_carry_tensor, (to_blocks(acceptance_entries_list), to_blocks(lookup_array_entries), to_blocks(payload_array_entries), to_blocks(fading_multiplier)))
    return jnp.transpose(outputs.reshape(SEQUENCE_TOKENS, batch_rows, HEADS, HEAD), (1, 0, 2, 3))

def forward(block_input, initial_state, norm_gains, norm_biases, mixing_coefficients, mix_down, mixing_up_weight, decay_down, decay_up, proj_weights, out_weight, time_decay, time_first, group_gain, group_bias, channel_key, channel_value, channel_recept):
    batch_rows = block_input.shape[0]
    normalized_first = layer_norm(block_input, norm_gains[0], norm_biases[0])
    shift_difference = shifted(normalized_first) - normalized_first
    base_value = normalized_first + shift_difference * mixing_coefficients[0]
    hidden_mixture = jnp.tanh(matmul_f32(base_value, mix_down))
    lowrank_map = jnp.einsum('azvw,vwg->vazg', hidden_mixture.reshape(batch_rows, SEQUENCE_TOKENS, 5, MIXER_RANK), mixing_up_weight.reshape(5, MIXER_RANK, MODEL_WIDTH), precision=PRECISION_TOP)
    mixed_input = [normalized_first + shift_difference * (mixing_coefficients[1 + branch_output] + lowrank_map[branch_output]) for branch_output in range(5)]
    hidden_decay = jnp.tanh(matmul_f32(mixed_input[0], decay_down))
    natural_log_fading = time_decay.reshape(MODEL_WIDTH) + matmul_f32(hidden_decay, decay_up.reshape(DECR, MODEL_WIDTH))
    fading_multiplier = jnp.exp(-jnp.exp(natural_log_fading))
    acceptance_entries_list = low_back(matmul_f32(low(mixed_input[3]), proj_weights[0]))
    lookup_array_entries = low_back(matmul_f32(low(mixed_input[1]), proj_weights[1]))
    payload_array_entries = low_back(matmul_f32(low(mixed_input[2]), proj_weights[2]))
    gate_pre = low_back(matmul_f32(low(mixed_input[4]), proj_weights[3]))

    def to_heads(rows):
        return rows.reshape(batch_rows, SEQUENCE_TOKENS, HEADS, HEAD)
    wkv = scaled_payload_series(to_heads(acceptance_entries_list), to_heads(lookup_array_entries), to_heads(payload_array_entries), to_heads(fading_multiplier), time_first, initial_state)
    mean_val = lax.optimization_barrier(jnp.mean(wkv, axis=-1, keepdims=True))
    centered = wkv - mean_val
    variance = lax.optimization_barrier(jnp.mean(centered * centered, axis=-1, keepdims=True))
    normed_heads = centered * lax.rsqrt(variance + GROUP_EPS) * group_gain + group_bias
    mixer_in = low(normed_heads.reshape(batch_rows, SEQUENCE_TOKENS, MODEL_WIDTH) * jax.nn.silu(gate_pre))
    residual = block_input + low_back(matmul_f32(mixer_in, out_weight))
    normed_two = layer_norm(residual, norm_gains[1], norm_biases[1])
    diff_two = shifted(normed_two) - normed_two
    chan_key = low(normed_two + diff_two * mixing_coefficients[6])
    chan_recept = low(normed_two + diff_two * mixing_coefficients[7])
    key_pre = low_back(matmul_f32(chan_key, channel_key))
    hidden = low(jnp.square(jnp.maximum(key_pre, 0.0)))
    kv_rows = low_back(matmul_f32(hidden, channel_value))
    recept_pre = low_back(matmul_f32(chan_recept, channel_recept))
    return (residual + jax.nn.sigmoid(recept_pre) * kv_rows, fading_multiplier)

def reference(block_input, initial_state, norm_gains, norm_biases, mixing_coefficients, mix_down, mixing_up_weight, decay_down, decay_up, proj_weights, out_weight, time_decay, time_first, group_gain, group_bias, channel_key, channel_value, channel_recept, out_grad):
    params = tuple((array.astype(jnp.float32) for array in (block_input, initial_state, norm_gains, norm_biases, mixing_coefficients, mix_down, mixing_up_weight, decay_down, decay_up, proj_weights, out_weight, time_decay, time_first, group_gain, group_bias, channel_key, channel_value, channel_recept)))
    result, backward, fading_multiplier = jax.vjp(forward, *params, has_aux=True)
    grads = backward(out_grad.astype(jnp.float32))
    by_head = fading_multiplier.reshape(fading_multiplier.shape[0], SEQUENCE_TOKENS, HEADS, HEAD)
    coeff_rows = jnp.concatenate([grads[4][:1], grads[4][2:]], axis=0)
    decay_row = grads[4][1:2]
    return (result.astype(jnp.bfloat16), grads[0], grads[1], grads[2], grads[3], coeff_rows, decay_row, grads[5], grads[6], grads[7], grads[8], grads[9], grads[10], grads[11], grads[12], grads[13], grads[14], grads[15], grads[16], grads[17], lax.optimization_barrier(jnp.min(by_head, axis=(1, 3))), lax.optimization_barrier(jnp.max(by_head, axis=(1, 3))))
```

```python
import jax
import jax.numpy as jnp
from jax import lax
from jax.sharding import PartitionSpec as P

PRECISION_TOP = lax.Precision.HIGHEST
NORM_EPS = 1e-05
GROUP_EPS = 0.00064


def from_behind(block, axis, distance):
    devices = range(lax.axis_size(axis))
    route = [(i - distance, i) for i in devices if i - distance in devices]
    return lax.ppermute(block, axis, route)


def for_sending(array):

    def short(part):
        return part.astype(jnp.bfloat16) if part.dtype == jnp.float32 else part

    return jax.tree.map(short, array)


def dense_single_float(left, right):
    return jnp.einsum(
        "...i,ij->...j", left, right, precision=PRECISION_TOP, preferred_element_type=jnp.float32
    )


def layer_norm(values, scale_row, shift_row):
    mean_val = jnp.mean(values, axis=-1, keepdims=True)
    centered = values - mean_val
    variance = jnp.mean(centered * centered, axis=-1, keepdims=True)
    return centered * lax.rsqrt(variance + NORM_EPS) * scale_row + shift_row


def group_norm(values, scale_rows, shift_rows):
    mean_val = jnp.mean(values, axis=-1, keepdims=True)
    centered = values - mean_val
    variance = jnp.mean(centered * centered, axis=-1, keepdims=True)
    return (
        centered * lax.rsqrt(variance + GROUP_EPS) * scale_rows[None, :, None, :]
        + shift_rows[None, :, None, :]
    )


def token_mixture(
    normalized_rows, preceding_row, shift_coefficient, lowrank_down, lowrank_up, decay_projection
):
    earlier = jnp.concatenate([preceding_row[:, None, :], normalized_rows[:, :-1, :]], axis=1)
    shift_difference = earlier - normalized_rows
    base_value = normalized_rows + shift_difference * shift_coefficient[0]
    hidden_mixture = jnp.tanh(dense_single_float(base_value, lowrank_down))
    seq_count, length, feature_columns = normalized_rows.shape
    rank_count = lowrank_up.shape[0] // 5
    lowrank_map = jnp.einsum(
        "stri,rid->rstd",
        hidden_mixture.reshape(seq_count, length, 5, rank_count),
        lowrank_up.reshape(5, rank_count, feature_columns),
        precision=PRECISION_TOP,
    )
    mixed_input = [
        normalized_rows
        + shift_difference * (shift_coefficient[1 + branch_output] + lowrank_map[branch_output])
        for branch_output in range(5)
    ]
    hidden_decay = jnp.tanh(dense_single_float(mixed_input[0], decay_projection))
    return (mixed_input[3], mixed_input[1], mixed_input[2], mixed_input[4], hidden_decay)


def decay_rates(hidden_decay, decay_lift, decay_base):
    return decay_base + dense_single_float(hidden_decay, decay_lift)


def channel_mix(normalized_rows, preceding_row, shift_coefficient):
    earlier = jnp.concatenate([preceding_row[:, None, :], normalized_rows[:, :-1, :]], axis=1)
    shift_difference = earlier - normalized_rows
    return (
        normalized_rows + shift_difference * shift_coefficient[6],
        normalized_rows + shift_difference * shift_coefficient[7],
    )


def span_totals(lookup_array_entries, payload_array_entries, natural_log_fading):
    cumulative = jnp.cumsum(-jnp.exp(natural_log_fading), axis=2)
    final_cum = cumulative[:, :, -1:, :]
    carried = jnp.einsum(
        "shtk,shtv->shkv",
        lookup_array_entries * jnp.exp(final_cum - cumulative),
        payload_array_entries,
        precision=PRECISION_TOP,
    )
    return (jnp.exp(final_cum[:, :, 0, :]), carried)


def segment_output(
    acceptance_entries_list,
    lookup_array_entries,
    payload_array_entries,
    natural_log_fading,
    initial_reward_vector,
    arriving_carry_tensor,
):
    decrement = -jnp.exp(natural_log_fading)
    cumulative = jnp.cumsum(decrement, axis=2)
    before = cumulative - decrement
    length = acceptance_entries_list.shape[2]
    middle = before[:, :, length // 2 : length // 2 + 1, :]
    carried = jnp.einsum(
        "shtk,shkv->shtv",
        acceptance_entries_list * jnp.exp(before),
        arriving_carry_tensor,
        precision=PRECISION_TOP,
    )
    scores = jnp.einsum(
        "shtk,shuk->shtu",
        acceptance_entries_list * jnp.exp(before - middle),
        lookup_array_entries * jnp.exp(middle - cumulative),
        precision=PRECISION_TOP,
    )
    positions = lax.broadcasted_iota(jnp.int32, (length, length), 0)
    sources = lax.broadcasted_iota(jnp.int32, (length, length), 1)
    scores = jnp.where(positions > sources, scores, 0.0)
    within = jnp.einsum("shtu,shuv->shtv", scores, payload_array_entries, precision=PRECISION_TOP)
    current = (
        jnp.sum(
            acceptance_entries_list
            * initial_reward_vector[None, :, None, :]
            * lookup_array_entries,
            axis=-1,
            keepdims=True,
        )
        * payload_array_entries
    )
    return carried + within + current


def packed_gather(pieces):
    flat = jnp.concatenate([part.reshape(-1) for part, _ in pieces])
    everything = lax.all_gather(flat, ("dp", "seq"))
    devices = everything.shape[0]
    out, at = [], 0
    for part, dim in pieces:
        piece = everything[:, at : at + part.size].reshape((devices,) + part.shape)
        at += part.size
        piece = jnp.moveaxis(piece, 0, dim)
        shape = list(part.shape)
        shape[dim] *= devices
        out.append(piece.reshape(shape))
    return out


def packed_scatter(pieces, devices):
    rows, shapes = [], []
    for whole, dim in pieces:
        shape = list(whole.shape)
        shape[dim] //= devices
        shapes.append(tuple(shape))
        cut = whole.reshape(whole.shape[:dim] + (devices, shape[dim]) + whole.shape[dim + 1 :])
        rows.append(jnp.moveaxis(cut, dim, 0).reshape(devices, -1))
    rows = jnp.concatenate(rows, axis=1)
    rows = jnp.pad(rows, ((0, 0), (0, -rows.shape[1] % 1024))).reshape(-1, 128)
    flat = lax.psum_scatter(rows, ("dp", "seq"), scatter_dimension=0, tiled=True).reshape(-1)
    out, at = [], 0
    for shape in shapes:
        size = 1
        for extent in shape:
            size *= extent
        out.append(flat[at : at + size].reshape(shape))
        at += size
    return out


def other_half(block):
    return lax.ppermute(block, "tp", [(0, 1), (1, 0)])


def big_scatter(whole, dim):
    return lax.psum_scatter(
        whole.astype(jnp.bfloat16), ("dp", "seq"), scatter_dimension=dim, tiled=True
    ).astype(jnp.float32)


def per_device(
    block_input,
    initial_state,
    norm_gains,
    norm_biases,
    mixing_coefficients,
    mix_down,
    mixing_up_weight,
    decay_down,
    decay_up,
    proj_weights,
    out_weight,
    time_decay,
    time_first,
    group_gain,
    group_bias,
    channel_key,
    channel_value,
    channel_recept,
    out_grad,
):
    blocks, place = lax.axis_size("seq"), lax.axis_index("seq")
    gathered = lax.axis_size("dp") * blocks
    half = lax.axis_index("tp")
    (
        gains_all,
        biases_all,
        shift_coefficient,
        lowrank_down,
        lowrank_up,
        decay_projection,
        decay_lift,
        decay_base,
        reward_array_entries,
        group_scale,
        group_shift,
    ) = [
        part.astype(jnp.float32)
        for part in packed_gather(
            [
                (norm_gains, 1),
                (norm_biases, 1),
                (mixing_coefficients, 1),
                (mix_down, 0),
                (mixing_up_weight, 1),
                (decay_down, 0),
                (decay_up, 2),
                (time_decay, 1),
                (time_first, 1),
                (group_gain, 1),
                (group_bias, 1),
            ]
        )
    ]
    projections = lax.all_gather(proj_weights, ("dp", "seq"), axis=1, tiled=True)
    out_proj = lax.all_gather(out_weight, ("dp", "seq"), axis=1, tiled=True)
    seq_count, length, feature_columns = block_input.shape
    heads_here, head_size = decay_base.shape
    head_cols = heads_here * head_size
    tokens = seq_count * length
    own_cols = channel_recept.shape[1]

    def split_heads(rows):
        return rows.reshape(seq_count, length, heads_here, head_size).transpose(0, 2, 1, 3)

    def join_heads(rows):
        return rows.transpose(0, 2, 1, 3).reshape(seq_count, length, head_cols)

    def both_halves(own):
        other = other_half(own)
        low = jnp.where(half == 0, own, other)
        high = jnp.where(half == 0, other, own)
        return jnp.concatenate([low, high], axis=-1)

    def own_half(rows):
        return lax.dynamic_slice_in_dim(rows, half * own_cols, own_cols, rows.ndim - 1)

    def half_sum(part):
        sent = lax.dynamic_slice_in_dim(part, (1 - half) * own_cols, own_cols, part.ndim - 1)
        return own_half(part) + other_half(sent.astype(jnp.bfloat16)).astype(jnp.float32)

    full_out = both_halves(out_grad)
    input_f = block_input.astype(jnp.float32)
    normalized_first, norm_one_back = jax.vjp(layer_norm, input_f, gains_all[0], biases_all[0])
    preceding_first = from_behind(normalized_first[:, -1, :].astype(jnp.bfloat16), "seq", 1).astype(
        jnp.float32
    )
    mixed_input, mix_back = jax.vjp(
        token_mixture,
        normalized_first,
        preceding_first,
        shift_coefficient,
        lowrank_down,
        lowrank_up,
        decay_projection,
    )
    log_rows, decay_back = jax.vjp(
        decay_rates,
        mixed_input[4],
        decay_lift.reshape(decay_lift.shape[0], head_cols),
        decay_base.reshape(head_cols),
    )
    stacked = jnp.stack(mixed_input[:4]).astype(jnp.bfloat16).reshape(4, tokens, feature_columns)
    projected = jnp.einsum("ntd,nde->nte", stacked, projections, preferred_element_type=jnp.float32)
    acceptance_entries_list = split_heads(projected[0])
    lookup_array_entries = split_heads(projected[1])
    payload_array_entries = split_heads(projected[2])
    gate_pre = projected[3].reshape(seq_count, length, head_cols)
    gate_act = jax.nn.silu(gate_pre)
    logarithm_heads = split_heads(log_rows)
    (decay_prod, carried), totals_back = jax.vjp(
        span_totals, lookup_array_entries, payload_array_entries, logarithm_heads
    )
    decay_heads = jnp.exp(-jnp.exp(logarithm_heads))
    stat_least = jnp.min(decay_heads, axis=(2, 3))
    stat_most = jnp.max(decay_heads, axis=(2, 3))
    small = jnp.concatenate(
        [decay_prod, stat_least[..., None], stat_most[..., None]], axis=-1
    )
    all_small = lax.all_gather(small, "seq")
    all_decay = all_small[..., :head_size]
    total_least = jnp.min(all_small[..., head_size], axis=0)
    total_most = jnp.max(all_small[..., head_size + 1], axis=0)
    all_carried = lax.all_gather(carried.astype(jnp.bfloat16), "seq")
    ahead = [jnp.ones_like(decay_prod)]
    for k in range(blocks):
        ahead.append(ahead[-1] * all_decay[k])
    prefix_decay = jnp.ones_like(decay_prod)
    prefix_state = jnp.zeros_like(carried)
    for k in range(blocks - 1):
        reached = k < place
        prefix_decay = jnp.where(reached, prefix_decay * all_decay[k], prefix_decay)
        prefix_state = jnp.where(
            reached,
            all_decay[k][..., None] * prefix_state + all_carried[k].astype(jnp.float32),
            prefix_state,
        )
    arriving_carry_tensor = prefix_decay[..., None] * initial_state + prefix_state
    wkv, output_back = jax.vjp(
        segment_output,
        acceptance_entries_list,
        lookup_array_entries,
        payload_array_entries,
        logarithm_heads,
        reward_array_entries,
        arriving_carry_tensor,
    )
    normed_heads, group_back = jax.vjp(group_norm, wkv, group_scale, group_shift)
    normed_rows = join_heads(normed_heads)
    mixer_in = (normed_rows * gate_act).astype(jnp.bfloat16)
    mixer_part = jnp.einsum("std,de->ste", mixer_in, out_proj, preferred_element_type=jnp.float32)
    residual = (
        input_f + mixer_part + other_half(mixer_part.astype(jnp.bfloat16)).astype(jnp.float32)
    )
    normed_two, norm_two_back = jax.vjp(layer_norm, residual, gains_all[1], biases_all[1])
    prev_two = from_behind(normed_two[:, -1, :].astype(jnp.bfloat16), "seq", 1).astype(jnp.float32)
    (chan_key, chan_recept), chan_back = jax.vjp(
        channel_mix, normed_two, prev_two, shift_coefficient
    )
    chan_key_b = chan_key.astype(jnp.bfloat16)
    chan_recept_b = chan_recept.astype(jnp.bfloat16)
    key_pre = jnp.einsum("std,df->stf", chan_key_b, channel_key, preferred_element_type=jnp.float32)
    hidden = jnp.square(jnp.maximum(key_pre, 0.0)).astype(jnp.bfloat16)
    value_part = jnp.einsum(
        "stf,fd->std", hidden, channel_value, preferred_element_type=jnp.float32
    )
    recept_pre = jnp.einsum(
        "std,de->ste", chan_recept_b, channel_recept, preferred_element_type=jnp.float32
    )
    kv_rows = half_sum(value_part)
    gate_chan = jax.nn.sigmoid(recept_pre)
    output = (own_half(residual) + gate_chan * kv_rows).astype(jnp.bfloat16)
    grad_out = out_grad.astype(jnp.float32)
    grad_value = (grad_out * gate_chan).astype(jnp.bfloat16)
    grad_recept = (grad_out * kv_rows * gate_chan * (1.0 - gate_chan)).astype(jnp.bfloat16)
    full_value = both_halves(grad_value)
    grad_hidden = jnp.einsum(
        "std,fd->stf", full_value, channel_value, preferred_element_type=jnp.float32
    )
    grad_key = (grad_hidden * 2.0 * jnp.maximum(key_pre, 0.0)).astype(jnp.bfloat16)
    part_key = jnp.einsum("stf,df->std", grad_key, channel_key, preferred_element_type=jnp.float32)
    part_recept = jnp.einsum(
        "ste,de->std", grad_recept, channel_recept, preferred_element_type=jnp.float32
    )
    part_normed_two, part_prev_two, grad_coeffs_chan = chan_back((part_key, part_recept))
    from_next_two = from_behind(for_sending(part_prev_two), "seq", -1).astype(jnp.float32)
    part_normed_two = part_normed_two.at[:, -1, :].add(from_next_two)
    grad_normed_two = part_normed_two + other_half(part_normed_two.astype(jnp.bfloat16)).astype(
        jnp.float32
    )
    grad_residual, grad_gain_two, grad_bias_two = norm_two_back(grad_normed_two)
    grad_residual = grad_residual + full_out.astype(jnp.float32)
    grad_branch = grad_residual.astype(jnp.bfloat16)
    out_weight_grad = jnp.einsum(
        "std,ste->de", mixer_in, grad_branch, preferred_element_type=jnp.float32
    )
    grad_mixer = jnp.einsum(
        "ste,de->std", grad_branch, out_proj, preferred_element_type=jnp.float32
    )
    grad_normed_rows = grad_mixer * gate_act
    gate_sig = jax.nn.sigmoid(gate_pre)
    grad_gate = grad_mixer * normed_rows * gate_sig * (1.0 + gate_pre * (1.0 - gate_sig))
    grad_wkv, group_gain_grad, group_bias_grad = group_back(split_heads(grad_normed_rows))
    (
        receptance_gradient,
        key_gradient_output,
        value_gradient_output,
        logarithm_gradient_output,
        reward_cotangent_term,
        incoming_gradient,
    ) = output_back(grad_wkv)
    all_incoming = lax.all_gather(incoming_gradient.astype(jnp.bfloat16), "seq")
    later_grad = jnp.zeros_like(incoming_gradient)
    state_grad = jnp.zeros_like(incoming_gradient)
    for k in range(blocks - 1, -1, -1):
        term = all_incoming[k].astype(jnp.float32)
        state_grad = state_grad + ahead[k][..., None] * term
        later_grad = jnp.where(k > place, all_decay[k][..., None] * later_grad + term, later_grad)
    grad_decay_prod = jnp.sum(later_grad * arriving_carry_tensor, axis=-1)
    grad_keys_tot, grad_values_tot, grad_logs_tot = totals_back((grad_decay_prod, later_grad))
    grad_proj = jnp.stack(
        [
            join_heads(receptance_gradient).reshape(tokens, head_cols),
            join_heads(key_gradient_output + grad_keys_tot).reshape(tokens, head_cols),
            join_heads(value_gradient_output + grad_values_tot).reshape(tokens, head_cols),
            grad_gate.reshape(tokens, head_cols),
        ]
    ).astype(jnp.bfloat16)
    proj_grad = jnp.einsum("ntd,nte->nde", stacked, grad_proj, preferred_element_type=jnp.float32)
    part_inputs = jnp.einsum(
        "nte,nde->ntd", grad_proj, projections, preferred_element_type=jnp.float32
    )
    part_hdec, lift_grad, base_grad = decay_back(join_heads(logarithm_gradient_output + grad_logs_tot))
    part_normed_one, part_prev_one, grad_coeffs_time, down_grad, up_grad, decay_proj_grad = mix_back(
        (
            part_inputs[0].reshape(seq_count, length, feature_columns),
            part_inputs[1].reshape(seq_count, length, feature_columns),
            part_inputs[2].reshape(seq_count, length, feature_columns),
            part_inputs[3].reshape(seq_count, length, feature_columns),
            part_hdec,
        )
    )
    from_next_one = from_behind(for_sending(part_prev_one), "seq", -1).astype(jnp.float32)
    part_normed_one = part_normed_one.at[:, -1, :].add(from_next_one)
    part_block, grad_gain_one, grad_bias_one = norm_one_back(part_normed_one)
    input_grad = own_half(grad_residual) + half_sum(part_block)
    value_weight_grad = jnp.einsum(
        "stf,std->fd", hidden, full_value, preferred_element_type=jnp.float32
    )
    key_weight_grad = jnp.einsum(
        "std,stf->df", chan_key_b, grad_key, preferred_element_type=jnp.float32
    )
    recept_weight_grad = jnp.einsum(
        "std,ste->de", chan_recept_b, grad_recept, preferred_element_type=jnp.float32
    )
    small_sums = packed_scatter(
        [
            (jnp.stack([grad_gain_one, 0.5 * grad_gain_two]), 1),
            (jnp.stack([grad_bias_one, 0.5 * grad_bias_two]), 1),
            (grad_coeffs_time + grad_coeffs_chan, 1),
            (down_grad, 0),
            (up_grad, 1),
            (decay_proj_grad, 0),
            (lift_grad.reshape(decay_lift.shape), 2),
            (base_grad.reshape(decay_base.shape), 1),
            (reward_cotangent_term, 1),
            (group_gain_grad, 1),
            (group_bias_grad, 1),
        ],
        gathered,
    )
    rest = [part + other_half(part) for part in small_sums[:6]] + small_sums[6:]
    proj_sum = big_scatter(proj_grad, 1)
    out_sum = big_scatter(out_weight_grad, 1)
    key_sum = big_scatter(key_weight_grad, 0)
    value_sum_rows = big_scatter(value_weight_grad, 1)
    recept_sum = big_scatter(recept_weight_grad, 0)
    coeff_rows = jnp.concatenate([rest[2][:1], rest[2][2:]], axis=0)
    decay_row = rest[2][1:2]
    return (
        output,
        input_grad,
        state_grad,
        rest[0],
        rest[1],
        coeff_rows,
        decay_row,
        rest[3],
        rest[4],
        rest[5],
        rest[6],
        proj_sum,
        out_sum,
        rest[7],
        rest[8],
        rest[9],
        rest[10],
        key_sum,
        value_sum_rows,
        recept_sum,
        total_least,
        total_most,
    )


def solution(mesh):
    return jax.shard_map(
        per_device,
        mesh=mesh,
        in_specs=(
            P("dp", "seq", None),
            P("dp", "tp", None, None),
            P(None, ("dp", "seq")),
            P(None, ("dp", "seq")),
            P(None, ("dp", "seq")),
            P(("dp", "seq"), None),
            P(None, ("dp", "seq")),
            P(("dp", "seq"), None),
            P(None, "tp", ("dp", "seq")),
            P(None, ("dp", "seq"), "tp"),
            P("tp", ("dp", "seq")),
            P("tp", ("dp", "seq")),
            P("tp", ("dp", "seq")),
            P("tp", ("dp", "seq")),
            P("tp", ("dp", "seq")),
            P(None, "tp"),
            P("tp", None),
            P(None, "tp"),
            P("dp", "seq", "tp"),
        ),
        out_specs=(
            P("dp", "seq", "tp"),
            P("dp", "seq", "tp"),
            P("dp", "tp", None, None),
            P(None, ("dp", "seq")),
            P(None, ("dp", "seq")),
            P(None, ("dp", "seq")),
            P(None, ("dp", "seq")),
            P(("dp", "seq"), None),
            P(None, ("dp", "seq")),
            P(("dp", "seq"), None),
            P(None, "tp", ("dp", "seq")),
            P(None, ("dp", "seq"), "tp"),
            P("tp", ("dp", "seq")),
            P("tp", ("dp", "seq")),
            P("tp", ("dp", "seq")),
            P("tp", ("dp", "seq")),
            P("tp", ("dp", "seq")),
            P(("dp", "seq"), "tp"),
            P("tp", ("dp", "seq")),
            P(("dp", "seq"), "tp"),
            P("dp", "tp"),
            P("dp", "tp"),
        ),
        check_vma=False,
    )
```

```python
import functools

import jax
import jax.numpy as jnp
from jax import lax
from jax.experimental import pallas as pl
from jax.experimental.pallas import tpu as pltpu
from jax.sharding import PartitionSpec as P

PRECISION_TOP = lax.Precision.HIGHEST
NORM_EPS = 1e-05
GROUP_EPS = 0.00064


def from_behind(block, axis, distance):
    devices = range(lax.axis_size(axis))
    route = [(i - distance, i) for i in devices if i - distance in devices]
    return lax.ppermute(block, axis, route)


def for_sending(array):

    def short(part):
        return part.astype(jnp.bfloat16) if part.dtype == jnp.float32 else part

    return jax.tree.map(short, array)


def dense_single_float(left, right):
    return jnp.einsum(
        "...i,ij->...j", left, right, precision=PRECISION_TOP, preferred_element_type=jnp.float32
    )


def layer_norm(values, scale_row, shift_row):
    mean_val = jnp.mean(values, axis=-1, keepdims=True)
    centered = values - mean_val
    variance = jnp.mean(centered * centered, axis=-1, keepdims=True)
    return centered * lax.rsqrt(variance + NORM_EPS) * scale_row + shift_row


def group_norm(values, scale_rows, shift_rows):
    mean_val = jnp.mean(values, axis=-1, keepdims=True)
    centered = values - mean_val
    variance = jnp.mean(centered * centered, axis=-1, keepdims=True)
    return (
        centered * lax.rsqrt(variance + GROUP_EPS) * scale_rows[None, :, None, :]
        + shift_rows[None, :, None, :]
    )


def token_mixture(
    normalized_rows, preceding_row, shift_coefficient, lowrank_down, lowrank_up, decay_projection
):
    earlier = jnp.concatenate([preceding_row[:, None, :], normalized_rows[:, :-1, :]], axis=1)
    shift_difference = earlier - normalized_rows
    base_value = normalized_rows + shift_difference * shift_coefficient[0]
    hidden_mixture = jnp.tanh(dense_single_float(base_value, lowrank_down))
    seq_count, length, feature_columns = normalized_rows.shape
    rank_count = lowrank_up.shape[0] // 5
    lowrank_map = jnp.einsum(
        "stri,rid->rstd",
        hidden_mixture.reshape(seq_count, length, 5, rank_count),
        lowrank_up.reshape(5, rank_count, feature_columns),
        precision=PRECISION_TOP,
    )
    mixed_input = [
        normalized_rows
        + shift_difference * (shift_coefficient[1 + branch_output] + lowrank_map[branch_output])
        for branch_output in range(5)
    ]
    hidden_decay = jnp.tanh(dense_single_float(mixed_input[0], decay_projection))
    return (mixed_input[3], mixed_input[1], mixed_input[2], mixed_input[4], hidden_decay)


def decay_rates(hidden_decay, decay_lift, decay_base):
    return decay_base + dense_single_float(hidden_decay, decay_lift)


def channel_mix(normalized_rows, preceding_row, shift_coefficient):
    earlier = jnp.concatenate([preceding_row[:, None, :], normalized_rows[:, :-1, :]], axis=1)
    shift_difference = earlier - normalized_rows
    return (
        normalized_rows + shift_difference * shift_coefficient[6],
        normalized_rows + shift_difference * shift_coefficient[7],
    )


def span_totals(lookup_array_entries, payload_array_entries, natural_log_fading):
    cumulative = jnp.cumsum(-jnp.exp(natural_log_fading), axis=2)
    final_cum = cumulative[:, :, -1:, :]
    carried = jnp.einsum(
        "shtk,shtv->shkv",
        lookup_array_entries * jnp.exp(final_cum - cumulative),
        payload_array_entries,
        precision=PRECISION_TOP,
    )
    return (jnp.exp(final_cum[:, :, 0, :]), carried)


def segment_output(
    acceptance_entries_list,
    lookup_array_entries,
    payload_array_entries,
    natural_log_fading,
    initial_reward_vector,
    arriving_carry_tensor,
):
    decrement = -jnp.exp(natural_log_fading)
    cumulative = jnp.cumsum(decrement, axis=2)
    before = cumulative - decrement
    length = acceptance_entries_list.shape[2]
    middle = before[:, :, length // 2 : length // 2 + 1, :]
    carried = jnp.einsum(
        "shtk,shkv->shtv",
        acceptance_entries_list * jnp.exp(before),
        arriving_carry_tensor,
        precision=PRECISION_TOP,
    )
    scores = jnp.einsum(
        "shtk,shuk->shtu",
        acceptance_entries_list * jnp.exp(before - middle),
        lookup_array_entries * jnp.exp(middle - cumulative),
        precision=PRECISION_TOP,
    )
    positions = lax.broadcasted_iota(jnp.int32, (length, length), 0)
    sources = lax.broadcasted_iota(jnp.int32, (length, length), 1)
    scores = jnp.where(positions > sources, scores, 0.0)
    within = jnp.einsum("shtu,shuv->shtv", scores, payload_array_entries, precision=PRECISION_TOP)
    current = (
        jnp.sum(
            acceptance_entries_list
            * initial_reward_vector[None, :, None, :]
            * lookup_array_entries,
            axis=-1,
            keepdims=True,
        )
        * payload_array_entries
    )
    return carried + within + current


def packed_gather(pieces):
    flat = jnp.concatenate([part.reshape(-1) for part, _ in pieces])
    everything = lax.all_gather(flat, ("dp", "seq"))
    devices = everything.shape[0]
    out, at = [], 0
    for part, dim in pieces:
        piece = everything[:, at : at + part.size].reshape((devices,) + part.shape)
        at += part.size
        piece = jnp.moveaxis(piece, 0, dim)
        shape = list(part.shape)
        shape[dim] *= devices
        out.append(piece.reshape(shape))
    return out


def packed_scatter(pieces, devices):
    rows, shapes = [], []
    for whole, dim in pieces:
        shape = list(whole.shape)
        shape[dim] //= devices
        shapes.append(tuple(shape))
        cut = whole.reshape(whole.shape[:dim] + (devices, shape[dim]) + whole.shape[dim + 1 :])
        rows.append(jnp.moveaxis(cut, dim, 0).reshape(devices, -1))
    rows = jnp.concatenate(rows, axis=1)
    rows = jnp.pad(rows, ((0, 0), (0, -rows.shape[1] % 1024))).reshape(-1, 128)
    flat = lax.psum_scatter(rows, ("dp", "seq"), scatter_dimension=0, tiled=True).reshape(-1)
    out, at = [], 0
    for shape in shapes:
        size = 1
        for extent in shape:
            size *= extent
        out.append(flat[at : at + size].reshape(shape))
        at += size
    return out


def other_half(block):
    return lax.ppermute(block, "tp", [(0, 1), (1, 0)])


CORES = 2


def ring_places(dp_size, seq_size):
    per_row = seq_size // CORES
    count = dp_size * per_row

    def chip(position):
        position = lax.rem(position + 2 * count, count)
        row = lax.div(position, per_row)
        column = lax.rem(position, per_row)
        column = jnp.where(lax.rem(row, 2) == 0, column, per_row - 1 - column)
        return row, column

    def own():
        row, column = lax.axis_index("dp"), lax.div(lax.axis_index("seq"), CORES)
        return row * per_row + jnp.where(lax.rem(row, 2) == 0, column, per_row - 1 - column)

    return count, chip, own


def cut_rings(widths, rings):
    each = sum(widths) // rings
    runs, product, column = [], 0, 0
    for _ in range(rings):
        run, left = [], each
        while left:
            take = min(left, widths[product] - column)
            run.append((product, column, take))
            left, column = left - take, column + take
            if column == widths[product]:
                product, column = product + 1, 0
        runs.append(run)
    return runs


def ring_kernel(dp_size, seq_size, rows, widths, runs, places, operands, *refs):
    products = len(widths)
    lefts = [(refs[left], lead) for left, _, lead in places]
    rights = [(refs[right], lead) for _, right, lead in places]
    totals, refs = refs[operands : operands + products], refs[operands + products :]
    rings = len(runs)
    mine, pair_out, pair_in, ring_out, ring_in = [
        refs[k * rings : (k + 1) * rings] for k in range(5)
    ]
    pair_send, pair_recv, pair_free, ring_send, ring_recv, ring_free = refs[5 * rings :]
    count, chip, own = ring_places(dp_size, seq_size)
    position, core = own(), lax.rem(lax.axis_index("seq"), CORES)

    def device(place, which):
        row, column = chip(place)
        return {"dp": row, "seq": column * CORES + which}

    sibling = device(position, 1 - core)
    after, before = device(position + 1, core), device(position - 1, core)
    barrier = pltpu.get_barrier_semaphore()
    for other in (sibling, after, before):
        pl.semaphore_signal(barrier, inc=1, device_id=other, device_id_type=pl.DeviceIdType.MESH)
    pl.semaphore_wait(barrier, 3)

    def pair_copy(ring):
        return pltpu.make_async_remote_copy(
            src_ref=pair_out[ring],
            dst_ref=pair_in[ring],
            send_sem=pair_send.at[ring],
            recv_sem=pair_recv.at[ring],
            device_id=sibling,
            device_id_type=pl.DeviceIdType.MESH,
        )

    def ring_copy(ring, slot):
        return pltpu.make_async_remote_copy(
            src_ref=ring_out[ring].at[slot],
            dst_ref=ring_in[ring].at[slot],
            send_sem=ring_send.at[ring, slot],
            recv_sem=ring_recv.at[ring, slot],
            device_id=after if ring % 2 == 0 else before,
            device_id_type=pl.DeviceIdType.MESH,
        )

    def part(ring, place, which, put):
        row, column = chip(place)
        start = (row * seq_size + column * CORES + which) * rows
        start = pl.multiple_of(start, rows)
        at = 0
        for product, first, wide in runs[ring]:
            ref, lead = lefts[product]
            if rows % 128 == 0:
                left = ref[(*lead, slice(None), pl.ds(start, rows))]
            else:
                left = ref[(*lead, pl.ds(start, rows), slice(None))]
            ref, lead = rights[product]
            right = ref[(*lead, slice(None), pl.ds(first, wide))]
            put(
                at,
                wide,
                lax.dot_general(
                    left,
                    right,
                    (((0 if rows % 128 == 0 else 1,), (0,)), ((), ())),
                    preferred_element_type=jnp.float32,
                ),
            )
            at += wide

    def turn(step, carry):
        slot = lax.rem(step, 2)
        last = 1 - slot
        for ring in range(rings):
            place = position - 1 - step if ring % 2 == 0 else position + 1 + step

            @pl.when(step >= 1)
            def _():
                pair_copy(ring).wait_send()

            def put_out(at, wide, value):
                pair_out[ring][:, at : at + wide] = value.astype(jnp.bfloat16)

            part(ring, place, 1 - core, put_out)

            @pl.when(step >= 1)
            def _():
                pl.semaphore_wait(pair_free.at[ring], 1)

            pair_copy(ring).start()

            def put_mine(at, wide, value):
                mine[ring][:, at : at + wide] = value

            part(ring, place, core, put_mine)
        for ring in range(rings):
            source = before if ring % 2 == 0 else after
            pair_copy(ring).wait_recv()

            @pl.when(step == 0)
            def _():
                ring_out[ring][slot] = (
                    mine[ring][...] + pair_in[ring][...].astype(jnp.float32)
                ).astype(jnp.bfloat16)

            @pl.when(step >= 1)
            def _():
                ring_copy(ring, last).wait_recv()

            @pl.when(jnp.logical_and(step >= 1, step < count - 1))
            def _():
                @pl.when(step >= 2)
                def _():
                    ring_copy(ring, slot).wait_send()

                ring_out[ring][slot] = (
                    mine[ring][...]
                    + pair_in[ring][...].astype(jnp.float32)
                    + ring_in[ring][last].astype(jnp.float32)
                ).astype(jnp.bfloat16)

            @pl.when(step == count - 1)
            def _():
                at = 0
                for product, first, wide in runs[ring]:
                    totals[product][:, first : first + wide] = (
                        mine[ring][:, at : at + wide]
                        + pair_in[ring][:, at : at + wide].astype(jnp.float32)
                        + ring_in[ring][last, :, at : at + wide].astype(jnp.float32)
                    )
                    at += wide

            @pl.when(step < count - 1)
            def _():
                @pl.when(step >= 2)
                def _():
                    pl.semaphore_wait(ring_free.at[ring], 1)

                ring_copy(ring, slot).start()
                pl.semaphore_signal(
                    pair_free.at[ring],
                    inc=1,
                    device_id=sibling,
                    device_id_type=pl.DeviceIdType.MESH,
                )

            @pl.when(jnp.logical_and(step >= 1, step < count - 2))
            def _():
                pl.semaphore_signal(
                    ring_free.at[ring],
                    inc=1,
                    device_id=source,
                    device_id_type=pl.DeviceIdType.MESH,
                )

        return carry

    lax.fori_loop(0, count, turn, 0)
    for ring in range(rings):
        pair_copy(ring).wait_send()
        for step in (count - 3, count - 2):
            ring_copy(ring, step % 2).wait_send()


def ring_sums(pairs, sizes, collective_id):
    dp_size, seq_size = sizes
    rows = pairs[0][0].shape[-1] // (dp_size * seq_size)
    tokens = pairs[0][1].shape[-2]
    operands, known, places = [], {}, []

    def place_of(array, turned):
        if id(array) not in known:
            known[id(array)] = len(operands)
            operands.append(jnp.swapaxes(array, -1, -2) if turned else array)
        return known[id(array)]

    for left, right, lead in pairs:
        places.append((place_of(left, rows % 128 != 0), place_of(right, False), lead))
    widths = [right.shape[-1] for _, right, _ in pairs]
    rings = 4
    runs = cut_rings(widths, rings)
    each = sum(widths) // rings
    low = jnp.bfloat16
    return pl.pallas_call(
        functools.partial(
            ring_kernel, dp_size, seq_size, rows, widths, runs, places, len(operands)
        ),
        out_shape=[jax.ShapeDtypeStruct((rows, wide), jnp.float32) for wide in widths],
        in_specs=[pl.BlockSpec(memory_space=pltpu.VMEM)] * len(operands),
        out_specs=[pl.BlockSpec(memory_space=pltpu.VMEM)] * len(pairs),
        scratch_shapes=[pltpu.VMEM((rows, each), jnp.float32)] * rings
        + [pltpu.VMEM((rows, each), low)] * (2 * rings)
        + [pltpu.VMEM((2, rows, each), low)] * (2 * rings)
        + [
            pltpu.SemaphoreType.DMA((rings,)),
            pltpu.SemaphoreType.DMA((rings,)),
            pltpu.SemaphoreType.REGULAR((rings,)),
            pltpu.SemaphoreType.DMA((rings, 2)),
            pltpu.SemaphoreType.DMA((rings, 2)),
            pltpu.SemaphoreType.REGULAR((rings,)),
        ],
        compiler_params=pltpu.CompilerParams(
            collective_id=collective_id, has_side_effects=True, vmem_limit_bytes=60 * 2**20
        ),
        cost_estimate=pl.CostEstimate(
            flops=2 * tokens * rows * dp_size * seq_size * sum(widths),
            bytes_accessed=2 * tokens * (2048 * len(pairs) + sum(widths)),
            transcendentals=0,
        ),
    )(*operands)


def per_device(
    block_input,
    initial_state,
    norm_gains,
    norm_biases,
    mixing_coefficients,
    mix_down,
    mixing_up_weight,
    decay_down,
    decay_up,
    proj_weights,
    out_weight,
    time_decay,
    time_first,
    group_gain,
    group_bias,
    channel_key,
    channel_value,
    channel_recept,
    out_grad,
):
    blocks, place = lax.axis_size("seq"), lax.axis_index("seq")
    gathered = lax.axis_size("dp") * blocks
    half = lax.axis_index("tp")
    (
        gains_all,
        biases_all,
        shift_coefficient,
        lowrank_down,
        lowrank_up,
        decay_projection,
        decay_lift,
        decay_base,
        reward_array_entries,
        group_scale,
        group_shift,
    ) = [
        part.astype(jnp.float32)
        for part in packed_gather(
            [
                (norm_gains, 1),
                (norm_biases, 1),
                (mixing_coefficients, 1),
                (mix_down, 0),
                (mixing_up_weight, 1),
                (decay_down, 0),
                (decay_up, 2),
                (time_decay, 1),
                (time_first, 1),
                (group_gain, 1),
                (group_bias, 1),
            ]
        )
    ]
    projections = lax.all_gather(proj_weights, ("dp", "seq"), axis=1, tiled=True)
    out_proj = lax.all_gather(out_weight, ("dp", "seq"), axis=1, tiled=True)
    seq_count, length, feature_columns = block_input.shape
    heads_here, head_size = decay_base.shape
    head_cols = heads_here * head_size
    tokens = seq_count * length
    own_cols = channel_recept.shape[1]

    def split_heads(rows):
        return rows.reshape(seq_count, length, heads_here, head_size).transpose(0, 2, 1, 3)

    def join_heads(rows):
        return rows.transpose(0, 2, 1, 3).reshape(seq_count, length, head_cols)

    def both_halves(own):
        other = other_half(own)
        low = jnp.where(half == 0, own, other)
        high = jnp.where(half == 0, other, own)
        return jnp.concatenate([low, high], axis=-1)

    def own_half(rows):
        return lax.dynamic_slice_in_dim(rows, half * own_cols, own_cols, rows.ndim - 1)

    def half_sum(part):
        sent = lax.dynamic_slice_in_dim(part, (1 - half) * own_cols, own_cols, part.ndim - 1)
        return own_half(part) + other_half(sent.astype(jnp.bfloat16)).astype(jnp.float32)

    full_out = both_halves(out_grad)
    input_f = block_input.astype(jnp.float32)
    normalized_first, norm_one_back = jax.vjp(layer_norm, input_f, gains_all[0], biases_all[0])
    preceding_first = from_behind(normalized_first[:, -1, :].astype(jnp.bfloat16), "seq", 1).astype(
        jnp.float32
    )
    mixed_input, mix_back = jax.vjp(
        token_mixture,
        normalized_first,
        preceding_first,
        shift_coefficient,
        lowrank_down,
        lowrank_up,
        decay_projection,
    )
    log_rows, decay_back = jax.vjp(
        decay_rates,
        mixed_input[4],
        decay_lift.reshape(decay_lift.shape[0], head_cols),
        decay_base.reshape(head_cols),
    )
    stacked = jnp.stack(mixed_input[:4]).astype(jnp.bfloat16).reshape(4, tokens, feature_columns)
    projected = jnp.einsum("ntd,nde->nte", stacked, projections, preferred_element_type=jnp.float32)
    acceptance_entries_list = split_heads(projected[0])
    lookup_array_entries = split_heads(projected[1])
    payload_array_entries = split_heads(projected[2])
    gate_pre = projected[3].reshape(seq_count, length, head_cols)
    gate_act = jax.nn.silu(gate_pre)
    logarithm_heads = split_heads(log_rows)
    (decay_prod, carried), totals_back = jax.vjp(
        span_totals, lookup_array_entries, payload_array_entries, logarithm_heads
    )
    decay_heads = jnp.exp(-jnp.exp(logarithm_heads))
    stat_least = jnp.min(decay_heads, axis=(2, 3))
    stat_most = jnp.max(decay_heads, axis=(2, 3))
    small = jnp.concatenate(
        [decay_prod, stat_least[..., None], stat_most[..., None]], axis=-1
    )
    all_small = lax.all_gather(small, "seq")
    all_decay = all_small[..., :head_size]
    total_least = jnp.min(all_small[..., head_size], axis=0)
    total_most = jnp.max(all_small[..., head_size + 1], axis=0)
    all_carried = lax.all_gather(carried.astype(jnp.bfloat16), "seq")
    ahead = [jnp.ones_like(decay_prod)]
    for k in range(blocks):
        ahead.append(ahead[-1] * all_decay[k])
    prefix_decay = jnp.ones_like(decay_prod)
    prefix_state = jnp.zeros_like(carried)
    for k in range(blocks - 1):
        reached = k < place
        prefix_decay = jnp.where(reached, prefix_decay * all_decay[k], prefix_decay)
        prefix_state = jnp.where(
            reached,
            all_decay[k][..., None] * prefix_state + all_carried[k].astype(jnp.float32),
            prefix_state,
        )
    arriving_carry_tensor = prefix_decay[..., None] * initial_state + prefix_state
    wkv, output_back = jax.vjp(
        segment_output,
        acceptance_entries_list,
        lookup_array_entries,
        payload_array_entries,
        logarithm_heads,
        reward_array_entries,
        arriving_carry_tensor,
    )
    normed_heads, group_back = jax.vjp(group_norm, wkv, group_scale, group_shift)
    normed_rows = join_heads(normed_heads)
    mixer_in = (normed_rows * gate_act).astype(jnp.bfloat16)
    mixer_part = jnp.einsum("std,de->ste", mixer_in, out_proj, preferred_element_type=jnp.float32)
    residual = (
        input_f + mixer_part + other_half(mixer_part.astype(jnp.bfloat16)).astype(jnp.float32)
    )
    normed_two, norm_two_back = jax.vjp(layer_norm, residual, gains_all[1], biases_all[1])
    prev_two = from_behind(normed_two[:, -1, :].astype(jnp.bfloat16), "seq", 1).astype(jnp.float32)
    (chan_key, chan_recept), chan_back = jax.vjp(
        channel_mix, normed_two, prev_two, shift_coefficient
    )
    chan_key_b = chan_key.astype(jnp.bfloat16)
    chan_recept_b = chan_recept.astype(jnp.bfloat16)
    key_pre = jnp.einsum("std,df->stf", chan_key_b, channel_key, preferred_element_type=jnp.float32)
    hidden = jnp.square(jnp.maximum(key_pre, 0.0)).astype(jnp.bfloat16)
    value_part = jnp.einsum(
        "stf,fd->std", hidden, channel_value, preferred_element_type=jnp.float32
    )
    recept_pre = jnp.einsum(
        "std,de->ste", chan_recept_b, channel_recept, preferred_element_type=jnp.float32
    )
    kv_rows = half_sum(value_part)
    gate_chan = jax.nn.sigmoid(recept_pre)
    output = (own_half(residual) + gate_chan * kv_rows).astype(jnp.bfloat16)
    grad_out = out_grad.astype(jnp.float32)
    grad_value = (grad_out * gate_chan).astype(jnp.bfloat16)
    grad_recept = (grad_out * kv_rows * gate_chan * (1.0 - gate_chan)).astype(jnp.bfloat16)
    full_value = both_halves(grad_value)
    grad_hidden = jnp.einsum(
        "std,fd->stf", full_value, channel_value, preferred_element_type=jnp.float32
    )
    grad_key = (grad_hidden * 2.0 * jnp.maximum(key_pre, 0.0)).astype(jnp.bfloat16)
    part_key = jnp.einsum("stf,df->std", grad_key, channel_key, preferred_element_type=jnp.float32)
    part_recept = jnp.einsum(
        "ste,de->std", grad_recept, channel_recept, preferred_element_type=jnp.float32
    )
    part_normed_two, part_prev_two, grad_coeffs_chan = chan_back((part_key, part_recept))
    from_next_two = from_behind(for_sending(part_prev_two), "seq", -1).astype(jnp.float32)
    part_normed_two = part_normed_two.at[:, -1, :].add(from_next_two)
    sizes = (lax.axis_size("dp"), blocks)
    flat_value = full_value.reshape(tokens, -1)
    key_sum, value_sum, recept_sum = ring_sums(
        [
            (chan_key_b.reshape(tokens, -1), grad_key.reshape(tokens, -1), ()),
            (flat_value, hidden.reshape(tokens, -1), ()),
            (chan_recept_b.reshape(tokens, -1), grad_recept.reshape(tokens, -1), ()),
        ],
        sizes,
        0,
    )
    grad_normed_two = part_normed_two + other_half(part_normed_two.astype(jnp.bfloat16)).astype(
        jnp.float32
    )
    grad_residual, grad_gain_two, grad_bias_two = norm_two_back(grad_normed_two)
    grad_residual = grad_residual + full_out.astype(jnp.float32)
    grad_branch = grad_residual.astype(jnp.bfloat16)
    grad_mixer = jnp.einsum(
        "ste,de->std", grad_branch, out_proj, preferred_element_type=jnp.float32
    )
    grad_normed_rows = grad_mixer * gate_act
    gate_sig = jax.nn.sigmoid(gate_pre)
    grad_gate = grad_mixer * normed_rows * gate_sig * (1.0 + gate_pre * (1.0 - gate_sig))
    grad_wkv, group_gain_grad, group_bias_grad = group_back(split_heads(grad_normed_rows))
    (
        receptance_gradient,
        key_gradient_output,
        value_gradient_output,
        logarithm_gradient_output,
        reward_cotangent_term,
        incoming_gradient,
    ) = output_back(grad_wkv)
    all_incoming = lax.all_gather(incoming_gradient.astype(jnp.bfloat16), "seq")
    later_grad = jnp.zeros_like(incoming_gradient)
    state_grad = jnp.zeros_like(incoming_gradient)
    for k in range(blocks - 1, -1, -1):
        term = all_incoming[k].astype(jnp.float32)
        state_grad = state_grad + ahead[k][..., None] * term
        later_grad = jnp.where(k > place, all_decay[k][..., None] * later_grad + term, later_grad)
    grad_decay_prod = jnp.sum(later_grad * arriving_carry_tensor, axis=-1)
    grad_keys_tot, grad_values_tot, grad_logs_tot = totals_back((grad_decay_prod, later_grad))
    grad_proj = jnp.stack(
        [
            join_heads(receptance_gradient).reshape(tokens, head_cols),
            join_heads(key_gradient_output + grad_keys_tot).reshape(tokens, head_cols),
            join_heads(value_gradient_output + grad_values_tot).reshape(tokens, head_cols),
            grad_gate.reshape(tokens, head_cols),
        ]
    ).astype(jnp.bfloat16)
    part_inputs = jnp.einsum(
        "nte,nde->ntd", grad_proj, projections, preferred_element_type=jnp.float32
    )
    part_hdec, lift_grad, base_grad = decay_back(join_heads(logarithm_gradient_output + grad_logs_tot))
    part_normed_one, part_prev_one, grad_coeffs_time, down_grad, up_grad, decay_proj_grad = mix_back(
        (
            part_inputs[0].reshape(seq_count, length, feature_columns),
            part_inputs[1].reshape(seq_count, length, feature_columns),
            part_inputs[2].reshape(seq_count, length, feature_columns),
            part_inputs[3].reshape(seq_count, length, feature_columns),
            part_hdec,
        )
    )
    from_next_one = from_behind(for_sending(part_prev_one), "seq", -1).astype(jnp.float32)
    part_normed_one = part_normed_one.at[:, -1, :].add(from_next_one)
    part_block, grad_gain_one, grad_bias_one = norm_one_back(part_normed_one)
    input_grad = own_half(grad_residual) + half_sum(part_block)
    small_sums = packed_scatter(
        [
            (jnp.stack([grad_gain_one, 0.5 * grad_gain_two]), 1),
            (jnp.stack([grad_bias_one, 0.5 * grad_bias_two]), 1),
            (grad_coeffs_time + grad_coeffs_chan, 1),
            (down_grad, 0),
            (up_grad, 1),
            (decay_proj_grad, 0),
            (lift_grad.reshape(decay_lift.shape), 2),
            (base_grad.reshape(decay_base.shape), 1),
            (reward_cotangent_term, 1),
            (group_gain_grad, 1),
            (group_bias_grad, 1),
        ],
        gathered,
    )
    rest = [part + other_half(part) for part in small_sums[:6]] + small_sums[6:]
    *proj_sums, out_sum = ring_sums(
        [(stacked, grad_proj, (branch,)) for branch in range(4)]
        + [(grad_branch.reshape(tokens, -1), mixer_in.reshape(tokens, -1), ())],
        sizes,
        1,
    )
    coeff_rows = jnp.concatenate([rest[2][:1], rest[2][2:]], axis=0)
    decay_row = rest[2][1:2]
    return (
        output,
        input_grad,
        state_grad,
        rest[0],
        rest[1],
        coeff_rows,
        decay_row,
        rest[3],
        rest[4],
        rest[5],
        rest[6],
        jnp.stack(proj_sums),
        out_sum.T,
        rest[7],
        rest[8],
        rest[9],
        rest[10],
        key_sum,
        value_sum.T,
        recept_sum,
        total_least,
        total_most,
    )


def solution(mesh):
    return jax.shard_map(
        per_device,
        mesh=mesh,
        in_specs=(
            P("dp", "seq", None),
            P("dp", "tp", None, None),
            P(None, ("dp", "seq")),
            P(None, ("dp", "seq")),
            P(None, ("dp", "seq")),
            P(("dp", "seq"), None),
            P(None, ("dp", "seq")),
            P(("dp", "seq"), None),
            P(None, "tp", ("dp", "seq")),
            P(None, ("dp", "seq"), "tp"),
            P("tp", ("dp", "seq")),
            P("tp", ("dp", "seq")),
            P("tp", ("dp", "seq")),
            P("tp", ("dp", "seq")),
            P("tp", ("dp", "seq")),
            P(None, "tp"),
            P("tp", None),
            P(None, "tp"),
            P("dp", "seq", "tp"),
        ),
        out_specs=(
            P("dp", "seq", "tp"),
            P("dp", "seq", "tp"),
            P("dp", "tp", None, None),
            P(None, ("dp", "seq")),
            P(None, ("dp", "seq")),
            P(None, ("dp", "seq")),
            P(None, ("dp", "seq")),
            P(("dp", "seq"), None),
            P(None, ("dp", "seq")),
            P(("dp", "seq"), None),
            P(None, "tp", ("dp", "seq")),
            P(None, ("dp", "seq"), "tp"),
            P("tp", ("dp", "seq")),
            P("tp", ("dp", "seq")),
            P("tp", ("dp", "seq")),
            P("tp", ("dp", "seq")),
            P("tp", ("dp", "seq")),
            P(("dp", "seq"), "tp"),
            P("tp", ("dp", "seq")),
            P(("dp", "seq"), "tp"),
            P("dp", "tp"),
            P("dp", "tp"),
        ),
        check_vma=False,
    )
```

```python
import functools

import jax
import jax.numpy as jnp
from jax import lax
from jax.experimental import pallas as pl
from jax.experimental.pallas import tpu as pltpu
from jax.sharding import PartitionSpec as P

NORM_EPS = 1e-05
GROUP_EPS = 0.00064


def from_behind(block, axis, distance):
    devices = range(lax.axis_size(axis))
    route = [(i - distance, i) for i in devices if i - distance in devices]
    return lax.ppermute(block, axis, route)


def for_sending(array):

    def short(part):
        return part.astype(jnp.bfloat16) if part.dtype == jnp.float32 else part

    return jax.tree.map(short, array)


def dense_single_float(left, right):
    return jnp.einsum(
        "...i,ij->...j", left, right, preferred_element_type=jnp.float32
    )


def layer_norm(values, scale_row, shift_row):
    mean_val = jnp.mean(values, axis=-1, keepdims=True)
    centered = values - mean_val
    variance = jnp.mean(centered * centered, axis=-1, keepdims=True)
    return centered * lax.rsqrt(variance + NORM_EPS) * scale_row + shift_row


def token_mixture(
    normalized_rows, preceding_row, shift_coefficient, lowrank_down, lowrank_up, decay_projection
):
    earlier = jnp.concatenate([preceding_row[:, None, :], normalized_rows[:, :-1, :]], axis=1)
    shift_difference = earlier - normalized_rows
    base_value = normalized_rows + shift_difference * shift_coefficient[0]
    hidden_mixture = jnp.tanh(dense_single_float(base_value, lowrank_down))
    seq_count, length, feature_columns = normalized_rows.shape
    rank_count = lowrank_up.shape[0] // 5
    lowrank_map = jnp.einsum(
        "stri,rid->rstd",
        hidden_mixture.reshape(seq_count, length, 5, rank_count),
        lowrank_up.reshape(5, rank_count, feature_columns),
    )
    mixed_input = [
        normalized_rows
        + shift_difference * (shift_coefficient[1 + branch_output] + lowrank_map[branch_output])
        for branch_output in range(5)
    ]
    hidden_decay = jnp.tanh(dense_single_float(mixed_input[0], decay_projection))
    return (mixed_input[3], mixed_input[1], mixed_input[2], mixed_input[4], hidden_decay)


def decay_rates(hidden_decay, decay_lift, decay_base):
    return decay_base + dense_single_float(hidden_decay, decay_lift)


def channel_mix(normalized_rows, preceding_row, shift_coefficient):
    earlier = jnp.concatenate([preceding_row[:, None, :], normalized_rows[:, :-1, :]], axis=1)
    shift_difference = earlier - normalized_rows
    return (
        normalized_rows + shift_difference * shift_coefficient[6],
        normalized_rows + shift_difference * shift_coefficient[7],
    )


WIDE = 256
PAIR = 128
EXTRA = 16


def halves_dot(left, right, dims):
    return lax.dot_general(
        left.astype(jnp.bfloat16),
        right.astype(jnp.bfloat16),
        (dims, ((), ())),
        preferred_element_type=jnp.float32,
    )


def exact_dot(ones, values):
    high = values.astype(jnp.bfloat16)
    rest = values - high.astype(jnp.float32)
    middle = rest.astype(jnp.bfloat16)
    low = (rest - middle.astype(jnp.float32)).astype(jnp.bfloat16)
    ones = ones.astype(jnp.bfloat16)
    dims = ((1,), (0,))
    return (
        halves_dot(ones, high, dims) + halves_dot(ones, middle, dims) + halves_dot(ones, low, dims)
    )


def iota(shape, dim):
    return lax.broadcasted_iota(jnp.int32, shape, dim)


def first_head(shape):
    return iota(shape, len(shape) - 1) < PAIR // 2


def compact(full):
    top, low = full[: PAIR // 2], full[PAIR // 2 :]
    return jnp.where(first_head(top.shape), top, low)


def spread(state):
    first = first_head(state.shape)
    return jnp.concatenate([jnp.where(first, state, 0.0), jnp.where(first, 0.0, state)], axis=0)


def head_sum(values):
    first = first_head(values.shape)
    a = jnp.sum(jnp.where(first, values, 0.0), axis=-1, keepdims=True)
    b = jnp.sum(jnp.where(first, 0.0, values), axis=-1, keepdims=True)
    return jnp.where(first, a, b)


def running_decay(log_rates):
    length = log_rates.shape[0]
    rates = -jnp.exp(log_rates)
    up_to = iota((length, length), 0) >= iota((length, length), 1)
    return rates, exact_dot(up_to.astype(jnp.float32), rates)


def two_parts(row):
    high = row.astype(jnp.bfloat16).astype(jnp.float32)
    return high, row - high


def totals_kernel(kv_ref, log_ref, packed_ref):
    for pair in range(WIDE // PAIR):
        lanes = slice(pair * PAIR, (pair + 1) * PAIR)
        keys, values = kv_ref[1, :, lanes], kv_ref[2, :, lanes]
        rates, total = running_decay(log_ref[:, lanes])
        length = rates.shape[0]
        final = total[length - 1 : length]
        state = compact(halves_dot(keys * jnp.exp(final - total), values, ((0,), (0,))))
        decay = jnp.exp(rates)
        rows = [
            *two_parts(jnp.exp(final)),
            *two_parts(jnp.min(decay, axis=0, keepdims=True)),
            *two_parts(jnp.max(decay, axis=0, keepdims=True)),
        ]
        row_at = iota((EXTRA, PAIR), 0)
        extra = jnp.zeros((EXTRA, PAIR), jnp.float32)
        for at, row in enumerate(rows):
            extra = jnp.where(row_at == at, row, extra)
        packed_ref[0, pair] = jnp.concatenate([state, extra], axis=0).astype(jnp.bfloat16)


def inner_scores(receive, keys, rates, total):
    length = receive.shape[0]
    before = total - rates
    middle = before[length // 2 : length // 2 + 1]
    up, down = jnp.exp(before - middle), jnp.exp(middle - total)
    rows, columns = receive * up, keys * down
    first = first_head(rows.shape)
    later = iota((length, length), 0) > iota((length, length), 1)
    columns = columns.astype(jnp.bfloat16)
    scores = [
        jnp.where(
            later, halves_dot(jnp.where(own, rows, 0.0), columns, ((1,), (1,))), 0.0
        ).astype(jnp.bfloat16)
        for own in (first, jnp.logical_not(first))
    ]
    return rows.astype(jnp.bfloat16), columns, scores, up, down, before


def heads_apply(left, right, side):
    first = first_head(right.shape)
    a = halves_dot(left[0], right, ((side,), (0,)))
    b = halves_dot(left[1], right, ((side,), (0,)))
    return jnp.where(first, a, b)


def inner_kernel(rkv_ref, log_ref, bonus_ref, inner_ref, decayed_ref):
    for pair in range(WIDE // PAIR):
        lanes = slice(pair * PAIR, (pair + 1) * PAIR)
        receive, keys, values = (rkv_ref[n, :, lanes] for n in range(3))
        rates, total = running_decay(log_ref[:, lanes])
        _, _, scores, _, _, before = inner_scores(receive, keys, rates, total)
        now = head_sum(receive * bonus_ref[:, lanes] * keys)
        inner_ref[:, lanes] = heads_apply(scores, values, 1) + now * values
        decayed_ref[:, lanes] = (receive * jnp.exp(before)).astype(jnp.bfloat16)


def block_decays(extra):
    blocks = extra.shape[0]
    flat = extra.astype(jnp.float32)
    columns = []
    for start in range(0, blocks, PAIR // EXTRA):
        some = flat[start : start + PAIR // EXTRA]
        some = some.reshape(some.shape[0] * EXTRA, PAIR)
        if some.shape[0] < PAIR:
            some = jnp.concatenate(
                [some, jnp.zeros((PAIR - some.shape[0], PAIR), jnp.float32)], axis=0
            )
        turned = some.T
        for k in range(min(PAIR // EXTRA, blocks - start)):
            both = turned[:, k * EXTRA : k * EXTRA + 1] + turned[:, k * EXTRA + 1 : k * EXTRA + 2]
            columns.append(compact(jnp.broadcast_to(both, (PAIR, PAIR))))
    return columns


def norm_heads(wkv, count):
    mean = head_sum(wkv) * (1.0 / count)
    centered = wkv - mean
    scale = lax.rsqrt(head_sum(centered * centered) * (1.0 / count) + GROUP_EPS)
    return centered * scale, scale


def join_kernel(
    place_ref, inner_ref, decayed_ref, gate_ref, packed_ref, start_ref, gain_ref, bias_ref, *outs
):
    wkv_ref, mixer_ref, state_ref = outs
    blocks = packed_ref.shape[0]
    place = place_ref[0]
    for pair in range(WIDE // PAIR):
        lanes = slice(pair * PAIR, (pair + 1) * PAIR)
        state = start_ref[0, pair]
        decays = block_decays(packed_ref[:, 0, pair, PAIR // 2 :, :])
        for k in range(blocks - 1):
            term = packed_ref[k, 0, pair, : PAIR // 2, :].astype(jnp.float32)
            state = jnp.where(k < place, decays[k] * state + term, state)
        state_ref[0, pair] = state
        wkv = inner_ref[:, lanes] + halves_dot(decayed_ref[:, lanes], spread(state), ((1,), (0,)))
        wkv_ref[:, lanes] = wkv
        normed, _ = norm_heads(wkv, PAIR // 2)
        normed = normed * gain_ref[:, lanes] + bias_ref[:, lanes]
        gate = gate_ref[0, :, lanes]
        mixer_ref[:, lanes] = (normed * gate * jax.nn.sigmoid(gate)).astype(jnp.bfloat16)


def put_rows(rows):
    row_at = iota((8, PAIR), 0)
    out = jnp.zeros((8, PAIR), jnp.float32)
    for at, row in enumerate(rows):
        out = jnp.where(row_at == at, row, out)
    return out


def back_join_kernel(grad_ref, wkv_ref, gate_ref, decayed_ref, gain_ref, bias_ref, *outs):
    grad_wkv_ref, grad_gate_ref, term_ref, sums_ref = outs
    for pair in range(WIDE // PAIR):
        lanes = slice(pair * PAIR, (pair + 1) * PAIR)
        grad, gate = grad_ref[:, lanes], gate_ref[0, :, lanes]
        gain = gain_ref[:, lanes]
        hat, scale = norm_heads(wkv_ref[:, lanes], PAIR // 2)
        sigmoid = jax.nn.sigmoid(gate)
        normed = hat * gain + bias_ref[:, lanes]
        grad_gate = grad * normed * sigmoid * (1.0 + gate * (1.0 - sigmoid))
        grad_gate_ref[:, lanes] = grad_gate.astype(jnp.bfloat16)
        grad_normed = grad * gate * sigmoid
        sums_ref[0, :, lanes] = put_rows(
            [
                jnp.sum(grad_normed * hat, axis=0, keepdims=True),
                jnp.sum(grad_normed, axis=0, keepdims=True),
            ]
        )
        q = grad_normed * gain
        each = 2.0 / PAIR
        grad_wkv = scale * (q - head_sum(q) * each - hat * (head_sum(q * hat) * each))
        grad_wkv_ref[:, lanes] = grad_wkv
        term_ref[0, pair] = compact(
            halves_dot(decayed_ref[:, lanes], grad_wkv, ((0,), (0,)))
        ).astype(jnp.bfloat16)


def back_inner_kernel(rkv_ref, log_ref, bonus_ref, grad_ref, state_ref, *outs):
    receive_ref, key_ref, value_ref, running_ref, sums_ref = outs
    for pair in range(WIDE // PAIR):
        lanes = slice(pair * PAIR, (pair + 1) * PAIR)
        receive, keys, values = (rkv_ref[n, :, lanes] for n in range(3))
        bonus, grad = bonus_ref[:, lanes], grad_ref[:, lanes]
        rates, total = running_decay(log_ref[:, lanes])
        rows, columns, scores, up, down, before = inner_scores(receive, keys, rates, total)
        length = receive.shape[0]
        first = first_head(values.shape)
        later = iota((length, length), 0) > iota((length, length), 1)
        low_values = values.astype(jnp.bfloat16)
        low_grad = grad.astype(jnp.bfloat16)
        grad_scores = [
            jnp.where(
                later, halves_dot(jnp.where(own, grad, 0.0), low_values, ((1,), (1,))), 0.0
            ).astype(jnp.bfloat16)
            for own in (first, jnp.logical_not(first))
        ]
        from_state = halves_dot(low_grad, spread(state_ref[0, pair]), ((1,), (1,)))
        far_receive = heads_apply(grad_scores, columns, 1) * up + jnp.exp(before) * from_state
        far_keys = heads_apply(grad_scores, rows, 0) * down
        meet = head_sum(grad * values)
        receive_ref[:, lanes] = (far_receive + bonus * keys * meet).astype(jnp.bfloat16)
        key_ref[:, lanes] = far_keys + bonus * receive * meet
        now = head_sum(receive * bonus * keys)
        value_ref[:, lanes] = heads_apply(scores, low_grad, 0) + now * grad
        moved = receive * far_receive
        moved = pltpu.roll(moved, length - 1, 0)
        moved = jnp.where(iota(moved.shape, 0) == length - 1, 0.0, moved)
        running_ref[:, lanes] = moved - keys * far_keys
        sums_ref[0, :, lanes] = put_rows([jnp.sum(receive * keys * meet, axis=0, keepdims=True)])


def back_outer_kernel(
    place_ref, kv_ref, log_ref, key_ref, value_ref, running_ref, state_ref, packed_ref, terms_ref, *outs
):
    grad_key_ref, grad_value_ref, grad_log_ref, start_ref, sums_ref = outs
    blocks = packed_ref.shape[0]
    place = place_ref[0]
    for pair in range(WIDE // PAIR):
        lanes = slice(pair * PAIR, (pair + 1) * PAIR)
        keys, values = kv_ref[1, :, lanes], kv_ref[2, :, lanes]
        rates, total = running_decay(log_ref[:, lanes])
        length = keys.shape[0]
        final = total[length - 1 : length]
        decays = block_decays(packed_ref[:, 0, pair, PAIR // 2 :, :])
        later = jnp.zeros((PAIR // 2, PAIR), jnp.float32)
        whole = jnp.zeros((PAIR // 2, PAIR), jnp.float32)
        for k in range(blocks - 1, -1, -1):
            term = terms_ref[k, 0, pair].astype(jnp.float32)
            later = jnp.where(k > place, decays[k] * later + term, later)
            whole = decays[k] * whole + term
        start_ref[0, pair] = whole
        spread_later = spread(later).astype(jnp.bfloat16)
        fade = jnp.exp(final - total)
        far_keys = fade * halves_dot(values, spread_later, ((1,), (1,)))
        grad_key_ref[:, lanes] = (key_ref[:, lanes] + far_keys).astype(jnp.bfloat16)
        grad_value_ref[:, lanes] = (
            value_ref[:, lanes] + halves_dot(keys * fade, spread_later, ((1,), (0,)))
        ).astype(jnp.bfloat16)
        moved = keys * far_keys
        met = spread(state_ref[0, pair] * later)
        high, low = two_parts(met)
        ones = jnp.ones((8, PAIR), jnp.bfloat16)
        met_row = (halves_dot(ones, high, ((1,), (1,))) + halves_dot(ones, low, ((1,), (1,))))[:1]
        last = jnp.sum(moved, axis=0, keepdims=True) + jnp.exp(final) * met_row
        running = running_ref[:, lanes] - moved
        running = running + jnp.where(iota(running.shape, 0) == length - 1, last, 0.0)
        onward = iota((length, length), 0) <= iota((length, length), 1)
        grad_log = exact_dot(onward.astype(jnp.float32), running) * rates
        grad_log_ref[:, lanes] = grad_log
        sums_ref[0, :, lanes] = put_rows([jnp.sum(grad_log, axis=0, keepdims=True)])


class Recurrence:
    def __init__(self, sequences, length, columns):
        self.sequences, self.length, self.columns = sequences, length, columns
        self.grid = (sequences, columns // WIDE)
        self.pairs = columns // PAIR
        self.tokens = pl.BlockSpec((length, WIDE), lambda s, p: (s, p))
        self.row = pl.BlockSpec((1, WIDE), lambda s, p: (0, p))
        self.stack = pl.BlockSpec((3, length, WIDE), lambda s, p: (0, s, p))
        self.gate = pl.BlockSpec((1, length, WIDE), lambda s, p: (3, s, p))
        self.state = pl.BlockSpec((1, WIDE // PAIR, PAIR // 2, PAIR), lambda s, p: (s, p, 0, 0))
        self.sums = pl.BlockSpec((1, 8, WIDE), lambda s, p: (s, 0, p))
        self.place = pl.BlockSpec(memory_space=pltpu.SMEM)

    def packed(self, blocks=None):
        rows = PAIR // 2 + EXTRA
        if blocks is None:
            return pl.BlockSpec((1, WIDE // PAIR, rows, PAIR), lambda s, p: (s, p, 0, 0))
        return pl.BlockSpec((blocks, 1, WIDE // PAIR, rows, PAIR), lambda s, p: (0, s, p, 0, 0))

    def terms(self, blocks):
        return pl.BlockSpec(
            (blocks, 1, WIDE // PAIR, PAIR // 2, PAIR), lambda s, p: (0, s, p, 0, 0)
        )

    def token_shape(self, kind):
        return jax.ShapeDtypeStruct((self.sequences * self.length, self.columns), kind)

    def state_shape(self, kind, rows=PAIR // 2):
        return jax.ShapeDtypeStruct((self.sequences, self.pairs, rows, PAIR), kind)

    def sums_shape(self):
        return jax.ShapeDtypeStruct((self.sequences, 8, self.columns), jnp.float32)

    def call(self, kernel, ins, outs, args, flops):
        size = sum(arg.size * arg.dtype.itemsize for arg in args)
        return pl.pallas_call(
            kernel,
            grid=self.grid,
            in_specs=ins,
            out_specs=[spec for spec, _ in outs],
            out_shape=[shape for _, shape in outs],
            compiler_params=pltpu.CompilerParams(vmem_limit_bytes=40 * 2**20),
            cost_estimate=pl.CostEstimate(
                flops=flops, bytes_accessed=size, transcendentals=6 * args[0].size
            ),
        )(*args)

    def totals(self, projected, log_rows):
        outs = [(self.packed(), self.state_shape(jnp.bfloat16, PAIR // 2 + EXTRA))]
        return self.call(
            totals_kernel, [self.stack, self.tokens], outs, (projected, log_rows), 10**9
        )[0]

    def inner(self, projected, log_rows, bonus):
        outs = [
            (self.tokens, self.token_shape(jnp.float32)),
            (self.tokens, self.token_shape(jnp.bfloat16)),
        ]
        ins = [self.stack, self.tokens, self.row]
        return self.call(inner_kernel, ins, outs, (projected, log_rows, bonus), 2 * 10**9)

    def join(self, place, inner, decayed, projected, packed, start, gain, bias):
        ins = [
            self.place,
            self.tokens,
            self.tokens,
            self.gate,
            self.packed(packed.shape[0]),
            self.state,
            self.row,
            self.row,
        ]
        outs = [
            (self.tokens, self.token_shape(jnp.float32)),
            (self.tokens, self.token_shape(jnp.bfloat16)),
            (self.state, self.state_shape(jnp.float32)),
        ]
        args = (place, inner, decayed, projected, packed, start, gain, bias)
        return self.call(join_kernel, ins, outs, args, 10**9)

    def back_join(self, grad, wkv, projected, decayed, gain, bias):
        ins = [self.tokens, self.tokens, self.gate, self.tokens, self.row, self.row]
        outs = [
            (self.tokens, self.token_shape(jnp.float32)),
            (self.tokens, self.token_shape(jnp.bfloat16)),
            (self.state, self.state_shape(jnp.bfloat16)),
            (self.sums, self.sums_shape()),
        ]
        args = (grad, wkv, projected, decayed, gain, bias)
        return self.call(back_join_kernel, ins, outs, args, 10**9)

    def back_inner(self, projected, log_rows, bonus, grad, state):
        ins = [self.stack, self.tokens, self.row, self.tokens, self.state]
        outs = [
            (self.tokens, self.token_shape(jnp.bfloat16)),
            (self.tokens, self.token_shape(jnp.float32)),
            (self.tokens, self.token_shape(jnp.float32)),
            (self.tokens, self.token_shape(jnp.float32)),
            (self.sums, self.sums_shape()),
        ]
        args = (projected, log_rows, bonus, grad, state)
        return self.call(back_inner_kernel, ins, outs, args, 4 * 10**9)

    def back_outer(self, place, projected, log_rows, keys, values, running, state, packed, terms):
        blocks = packed.shape[0]
        ins = [
            self.place,
            self.stack,
            self.tokens,
            self.tokens,
            self.tokens,
            self.tokens,
            self.state,
            self.packed(blocks),
            self.terms(blocks),
        ]
        outs = [
            (self.tokens, self.token_shape(jnp.bfloat16)),
            (self.tokens, self.token_shape(jnp.bfloat16)),
            (self.tokens, self.token_shape(jnp.float32)),
            (self.state, self.state_shape(jnp.float32)),
            (self.sums, self.sums_shape()),
        ]
        args = (place, projected, log_rows, keys, values, running, state, packed, terms)
        return self.call(back_outer_kernel, ins, outs, args, 3 * 10**9)


def paired_states(states):
    sequences, heads, size, _ = states.shape
    pairs = states.reshape(sequences, heads // 2, 2, size, size)
    return pairs.transpose(0, 1, 3, 2, 4).reshape(sequences, heads // 2, size, 2 * size)


def single_states(pairs):
    sequences, count, size, _ = pairs.shape
    heads = pairs.reshape(sequences, count, size, 2, size).transpose(0, 1, 3, 2, 4)
    return heads.reshape(sequences, 2 * count, size, size)


def packed_gather(pieces):
    flat = jnp.concatenate([part.reshape(-1) for part, _ in pieces])
    everything = lax.all_gather(flat, ("dp", "seq"))
    devices = everything.shape[0]
    out, at = [], 0
    for part, dim in pieces:
        piece = everything[:, at : at + part.size].reshape((devices,) + part.shape)
        at += part.size
        piece = jnp.moveaxis(piece, 0, dim)
        shape = list(part.shape)
        shape[dim] *= devices
        out.append(piece.reshape(shape))
    return out


def packed_scatter(pieces, devices):
    rows, shapes = [], []
    for whole, dim in pieces:
        shape = list(whole.shape)
        shape[dim] //= devices
        shapes.append(tuple(shape))
        cut = whole.reshape(whole.shape[:dim] + (devices, shape[dim]) + whole.shape[dim + 1 :])
        rows.append(jnp.moveaxis(cut, dim, 0).reshape(devices, -1))
    rows = jnp.concatenate(rows, axis=1)
    rows = jnp.pad(rows, ((0, 0), (0, -rows.shape[1] % 1024))).reshape(-1, 128)
    flat = lax.psum_scatter(rows, ("dp", "seq"), scatter_dimension=0, tiled=True).reshape(-1)
    out, at = [], 0
    for shape in shapes:
        size = 1
        for extent in shape:
            size *= extent
        out.append(flat[at : at + size].reshape(shape))
        at += size
    return out


def other_half(block):
    return lax.ppermute(block, "tp", [(0, 1), (1, 0)])


CORES = 2


def ring_places(dp_size, seq_size):
    per_row = seq_size // CORES
    count = dp_size * per_row

    def chip(position):
        position = lax.rem(position + 2 * count, count)
        row = lax.div(position, per_row)
        column = lax.rem(position, per_row)
        column = jnp.where(lax.rem(row, 2) == 0, column, per_row - 1 - column)
        return row, column

    def own():
        row, column = lax.axis_index("dp"), lax.div(lax.axis_index("seq"), CORES)
        return row * per_row + jnp.where(lax.rem(row, 2) == 0, column, per_row - 1 - column)

    return count, chip, own


def cut_rings(widths, rings):
    each = sum(widths) // rings
    runs, product, column = [], 0, 0
    for _ in range(rings):
        run, left = [], each
        while left:
            take = min(left, widths[product] - column)
            run.append((product, column, take))
            left, column = left - take, column + take
            if column == widths[product]:
                product, column = product + 1, 0
        runs.append(run)
    return runs


def ring_kernel(dp_size, seq_size, rows, widths, runs, places, operands, *refs):
    products = len(widths)
    lefts = [(refs[left], lead) for left, _, lead in places]
    rights = [(refs[right], lead) for _, right, lead in places]
    totals, refs = refs[operands : operands + products], refs[operands + products :]
    rings = len(runs)
    mine, pair_out, pair_in, ring_out, ring_in = [
        refs[k * rings : (k + 1) * rings] for k in range(5)
    ]
    pair_send, pair_recv, pair_free, ring_send, ring_recv, ring_free = refs[5 * rings :]
    count, chip, own = ring_places(dp_size, seq_size)
    position, core = own(), lax.rem(lax.axis_index("seq"), CORES)

    def device(place, which):
        row, column = chip(place)
        return {"dp": row, "seq": column * CORES + which}

    sibling = device(position, 1 - core)
    after, before = device(position + 1, core), device(position - 1, core)
    barrier = pltpu.get_barrier_semaphore()
    for other in (sibling, after, before):
        pl.semaphore_signal(barrier, inc=1, device_id=other, device_id_type=pl.DeviceIdType.MESH)
    pl.semaphore_wait(barrier, 3)

    def pair_copy(ring):
        return pltpu.make_async_remote_copy(
            src_ref=pair_out[ring],
            dst_ref=pair_in[ring],
            send_sem=pair_send.at[ring],
            recv_sem=pair_recv.at[ring],
            device_id=sibling,
            device_id_type=pl.DeviceIdType.MESH,
        )

    def ring_copy(ring, slot):
        return pltpu.make_async_remote_copy(
            src_ref=ring_out[ring].at[slot],
            dst_ref=ring_in[ring].at[slot],
            send_sem=ring_send.at[ring, slot],
            recv_sem=ring_recv.at[ring, slot],
            device_id=after if ring % 2 == 0 else before,
            device_id_type=pl.DeviceIdType.MESH,
        )

    def part(ring, place, which, put):
        row, column = chip(place)
        start = (row * seq_size + column * CORES + which) * rows
        start = pl.multiple_of(start, rows)
        at = 0
        for product, first, wide in runs[ring]:
            ref, lead = lefts[product]
            if rows % 128 == 0:
                left = ref[(*lead, slice(None), pl.ds(start, rows))]
            else:
                left = ref[(*lead, pl.ds(start, rows), slice(None))]
            ref, lead = rights[product]
            right = ref[(*lead, slice(None), pl.ds(first, wide))]
            put(
                at,
                wide,
                lax.dot_general(
                    left,
                    right,
                    (((0 if rows % 128 == 0 else 1,), (0,)), ((), ())),
                    preferred_element_type=jnp.float32,
                ),
            )
            at += wide

    def turn(step, carry):
        slot = lax.rem(step, 2)
        last = 1 - slot
        for ring in range(rings):
            place = position - 1 - step if ring % 2 == 0 else position + 1 + step

            @pl.when(step >= 1)
            def _():
                pair_copy(ring).wait_send()

            def put_out(at, wide, value):
                pair_out[ring][:, at : at + wide] = value.astype(jnp.bfloat16)

            part(ring, place, 1 - core, put_out)

            @pl.when(step >= 1)
            def _():
                pl.semaphore_wait(pair_free.at[ring], 1)

            pair_copy(ring).start()

            def put_mine(at, wide, value):
                mine[ring][:, at : at + wide] = value

            part(ring, place, core, put_mine)
        for ring in range(rings):
            source = before if ring % 2 == 0 else after
            pair_copy(ring).wait_recv()

            @pl.when(step == 0)
            def _():
                ring_out[ring][slot] = (
                    mine[ring][...] + pair_in[ring][...].astype(jnp.float32)
                ).astype(jnp.bfloat16)

            @pl.when(step >= 1)
            def _():
                ring_copy(ring, last).wait_recv()

            @pl.when(jnp.logical_and(step >= 1, step < count - 1))
            def _():
                @pl.when(step >= 2)
                def _():
                    ring_copy(ring, slot).wait_send()

                ring_out[ring][slot] = (
                    mine[ring][...]
                    + pair_in[ring][...].astype(jnp.float32)
                    + ring_in[ring][last].astype(jnp.float32)
                ).astype(jnp.bfloat16)

            @pl.when(step == count - 1)
            def _():
                at = 0
                for product, first, wide in runs[ring]:
                    totals[product][:, first : first + wide] = (
                        mine[ring][:, at : at + wide]
                        + pair_in[ring][:, at : at + wide].astype(jnp.float32)
                        + ring_in[ring][last, :, at : at + wide].astype(jnp.float32)
                    )
                    at += wide

            @pl.when(step < count - 1)
            def _():
                @pl.when(step >= 2)
                def _():
                    pl.semaphore_wait(ring_free.at[ring], 1)

                ring_copy(ring, slot).start()
                pl.semaphore_signal(
                    pair_free.at[ring],
                    inc=1,
                    device_id=sibling,
                    device_id_type=pl.DeviceIdType.MESH,
                )

            @pl.when(jnp.logical_and(step >= 1, step < count - 2))
            def _():
                pl.semaphore_signal(
                    ring_free.at[ring],
                    inc=1,
                    device_id=source,
                    device_id_type=pl.DeviceIdType.MESH,
                )

        return carry

    lax.fori_loop(0, count, turn, 0)
    for ring in range(rings):
        pair_copy(ring).wait_send()
        for step in (count - 3, count - 2):
            ring_copy(ring, step % 2).wait_send()


def ring_sums(pairs, sizes, collective_id):
    dp_size, seq_size = sizes
    rows = pairs[0][0].shape[-1] // (dp_size * seq_size)
    tokens = pairs[0][1].shape[-2]
    operands, known, places = [], {}, []

    def place_of(array, turned):
        if id(array) not in known:
            known[id(array)] = len(operands)
            operands.append(jnp.swapaxes(array, -1, -2) if turned else array)
        return known[id(array)]

    for left, right, lead in pairs:
        places.append((place_of(left, rows % 128 != 0), place_of(right, False), lead))
    widths = [right.shape[-1] for _, right, _ in pairs]
    rings = 4
    runs = cut_rings(widths, rings)
    each = sum(widths) // rings
    low = jnp.bfloat16
    return pl.pallas_call(
        functools.partial(
            ring_kernel, dp_size, seq_size, rows, widths, runs, places, len(operands)
        ),
        out_shape=[jax.ShapeDtypeStruct((rows, wide), jnp.float32) for wide in widths],
        in_specs=[pl.BlockSpec(memory_space=pltpu.VMEM)] * len(operands),
        out_specs=[pl.BlockSpec(memory_space=pltpu.VMEM)] * len(pairs),
        scratch_shapes=[pltpu.VMEM((rows, each), jnp.float32)] * rings
        + [pltpu.VMEM((rows, each), low)] * (2 * rings)
        + [pltpu.VMEM((2, rows, each), low)] * (2 * rings)
        + [
            pltpu.SemaphoreType.DMA((rings,)),
            pltpu.SemaphoreType.DMA((rings,)),
            pltpu.SemaphoreType.REGULAR((rings,)),
            pltpu.SemaphoreType.DMA((rings, 2)),
            pltpu.SemaphoreType.DMA((rings, 2)),
            pltpu.SemaphoreType.REGULAR((rings,)),
        ],
        compiler_params=pltpu.CompilerParams(
            collective_id=collective_id, has_side_effects=True, vmem_limit_bytes=60 * 2**20
        ),
        cost_estimate=pl.CostEstimate(
            flops=2 * tokens * rows * dp_size * seq_size * sum(widths),
            bytes_accessed=2 * tokens * (2048 * len(pairs) + sum(widths)),
            transcendentals=0,
        ),
    )(*operands)


def per_device(
    block_input,
    initial_state,
    norm_gains,
    norm_biases,
    mixing_coefficients,
    mix_down,
    mixing_up_weight,
    decay_down,
    decay_up,
    proj_weights,
    out_weight,
    time_decay,
    time_first,
    group_gain,
    group_bias,
    channel_key,
    channel_value,
    channel_recept,
    out_grad,
):
    blocks, place = lax.axis_size("seq"), lax.axis_index("seq")
    gathered = lax.axis_size("dp") * blocks
    half = lax.axis_index("tp")
    (
        gains_all,
        biases_all,
        shift_coefficient,
        lowrank_down,
        lowrank_up,
        decay_projection,
        decay_lift,
        decay_base,
        reward_array_entries,
        group_scale,
        group_shift,
    ) = [
        part.astype(jnp.float32)
        for part in packed_gather(
            [
                (norm_gains, 1),
                (norm_biases, 1),
                (mixing_coefficients, 1),
                (mix_down, 0),
                (mixing_up_weight, 1),
                (decay_down, 0),
                (decay_up, 2),
                (time_decay, 1),
                (time_first, 1),
                (group_gain, 1),
                (group_bias, 1),
            ]
        )
    ]
    projections = lax.all_gather(proj_weights, ("dp", "seq"), axis=1, tiled=True)
    out_proj = lax.all_gather(out_weight, ("dp", "seq"), axis=1, tiled=True)
    seq_count, length, feature_columns = block_input.shape
    heads_here, head_size = decay_base.shape
    head_cols = heads_here * head_size
    tokens = seq_count * length
    own_cols = channel_recept.shape[1]

    def both_halves(own):
        other = other_half(own)
        low = jnp.where(half == 0, own, other)
        high = jnp.where(half == 0, other, own)
        return jnp.concatenate([low, high], axis=-1)

    def own_half(rows):
        return lax.dynamic_slice_in_dim(rows, half * own_cols, own_cols, rows.ndim - 1)

    def half_sum(part):
        sent = lax.dynamic_slice_in_dim(part, (1 - half) * own_cols, own_cols, part.ndim - 1)
        return own_half(part) + other_half(sent.astype(jnp.bfloat16)).astype(jnp.float32)

    full_out = both_halves(out_grad)
    input_f = block_input.astype(jnp.float32)
    normalized_first, norm_one_back = jax.vjp(layer_norm, input_f, gains_all[0], biases_all[0])
    preceding_first = from_behind(normalized_first[:, -1, :].astype(jnp.bfloat16), "seq", 1).astype(
        jnp.float32
    )
    mixed_input, mix_back = jax.vjp(
        token_mixture,
        normalized_first,
        preceding_first,
        shift_coefficient,
        lowrank_down,
        lowrank_up,
        decay_projection,
    )
    log_rows, decay_back = jax.vjp(
        decay_rates,
        mixed_input[4],
        decay_lift.reshape(decay_lift.shape[0], head_cols),
        decay_base.reshape(head_cols),
    )
    stacked = jnp.stack(mixed_input[:4]).astype(jnp.bfloat16).reshape(4, tokens, feature_columns)
    projected = jnp.einsum("ntd,nde->nte", stacked, projections, preferred_element_type=jnp.float32)
    recurrence = Recurrence(seq_count, length, head_cols)
    log_flat = log_rows.reshape(tokens, head_cols)
    bonus = reward_array_entries.reshape(1, head_cols)
    group_scale, group_shift = group_scale.reshape(1, -1), group_shift.reshape(1, -1)
    where_here = place.astype(jnp.int32).reshape(1)
    all_packed = lax.all_gather(recurrence.totals(projected, log_flat), "seq")
    inner, decayed = recurrence.inner(projected, log_flat, bonus)
    wkv, mixer_rows, state = recurrence.join(
        where_here,
        inner,
        decayed,
        projected,
        all_packed,
        paired_states(initial_state),
        group_scale,
        group_shift,
    )
    mixer_in = mixer_rows.reshape(seq_count, length, head_cols)
    extra = all_packed[..., head_size : head_size + 6, :].astype(jnp.float32)
    extra = extra.reshape(blocks, seq_count, heads_here // 2, 3, 2, 2, head_size).sum(axis=4)
    total_least = jnp.min(extra[:, :, :, 1], axis=(0, 4)).reshape(seq_count, heads_here)
    total_most = jnp.max(extra[:, :, :, 2], axis=(0, 4)).reshape(seq_count, heads_here)
    mixer_part = jnp.einsum("std,de->ste", mixer_in, out_proj, preferred_element_type=jnp.float32)
    residual = (
        input_f + mixer_part + other_half(mixer_part.astype(jnp.bfloat16)).astype(jnp.float32)
    )
    normed_two, norm_two_back = jax.vjp(layer_norm, residual, gains_all[1], biases_all[1])
    prev_two = from_behind(normed_two[:, -1, :].astype(jnp.bfloat16), "seq", 1).astype(jnp.float32)
    (chan_key, chan_recept), chan_back = jax.vjp(
        channel_mix, normed_two, prev_two, shift_coefficient
    )
    chan_key_b = chan_key.astype(jnp.bfloat16)
    chan_recept_b = chan_recept.astype(jnp.bfloat16)
    key_pre = jnp.einsum("std,df->stf", chan_key_b, channel_key, preferred_element_type=jnp.float32)
    hidden = jnp.square(jnp.maximum(key_pre, 0.0)).astype(jnp.bfloat16)
    value_part = jnp.einsum(
        "stf,fd->std", hidden, channel_value, preferred_element_type=jnp.float32
    )
    recept_pre = jnp.einsum(
        "std,de->ste", chan_recept_b, channel_recept, preferred_element_type=jnp.float32
    )
    kv_rows = half_sum(value_part)
    gate_chan = jax.nn.sigmoid(recept_pre)
    output = (own_half(residual) + gate_chan * kv_rows).astype(jnp.bfloat16)
    grad_out = out_grad.astype(jnp.float32)
    grad_value = (grad_out * gate_chan).astype(jnp.bfloat16)
    grad_recept = (grad_out * kv_rows * gate_chan * (1.0 - gate_chan)).astype(jnp.bfloat16)
    full_value = both_halves(grad_value)

    def weight_terms(left, right):
        return jnp.einsum(
            "td,tf->df",
            left.reshape(tokens, -1),
            right.reshape(tokens, -1),
            preferred_element_type=jnp.float32,
        ).astype(jnp.bfloat16)

    def scattered(whole):
        return lax.psum_scatter(whole, ("dp", "seq"), scatter_dimension=0, tiled=True).astype(
            jnp.float32
        )

    full_value, value_whole = lax.optimization_barrier(
        (full_value, weight_terms(full_value, hidden))
    )
    value_sum = scattered(value_whole)
    grad_hidden = jnp.einsum(
        "std,fd->stf", full_value, channel_value, preferred_element_type=jnp.float32
    )
    grad_key = (grad_hidden * 2.0 * jnp.maximum(key_pre, 0.0)).astype(jnp.bfloat16)
    part_key = jnp.einsum("stf,df->std", grad_key, channel_key, preferred_element_type=jnp.float32)
    part_recept = jnp.einsum(
        "ste,de->std", grad_recept, channel_recept, preferred_element_type=jnp.float32
    )
    part_normed_two, part_prev_two, grad_coeffs_chan = chan_back((part_key, part_recept))
    from_next_two = from_behind(for_sending(part_prev_two), "seq", -1).astype(jnp.float32)
    part_normed_two = part_normed_two.at[:, -1, :].add(from_next_two)
    sizes = (lax.axis_size("dp"), blocks)
    key_whole = weight_terms(chan_key_b, grad_key)
    grad_normed_two = part_normed_two + other_half(part_normed_two.astype(jnp.bfloat16)).astype(
        jnp.float32
    )
    grad_residual, grad_gain_two, grad_bias_two = norm_two_back(grad_normed_two)
    grad_residual = grad_residual + full_out.astype(jnp.float32)
    grad_residual, key_whole = lax.optimization_barrier((grad_residual, key_whole))
    key_sum = scattered(key_whole)
    grad_branch = grad_residual.astype(jnp.bfloat16)
    grad_mixer = jnp.einsum(
        "ste,de->std", grad_branch, out_proj, preferred_element_type=jnp.float32
    )
    grad_wkv, grad_gate, block_term, group_sums = recurrence.back_join(
        grad_mixer.reshape(tokens, head_cols), wkv, projected, decayed, group_scale, group_shift
    )
    all_terms = lax.all_gather(block_term, "seq")
    grad_receive, near_key, near_value, running, bonus_sums = recurrence.back_inner(
        projected, log_flat, bonus, grad_wkv, state
    )
    grad_keys, grad_values, grad_log, start_pairs, rate_sums = recurrence.back_outer(
        where_here,
        projected,
        log_flat,
        near_key,
        near_value,
        running,
        state,
        all_packed,
        all_terms,
    )
    state_grad = single_states(start_pairs)

    def head_rows(sums, row):
        return jnp.sum(sums[:, row], axis=0).reshape(heads_here, head_size)

    group_gain_grad, group_bias_grad = head_rows(group_sums, 0), head_rows(group_sums, 1)
    reward_cotangent_term, base_grad = head_rows(bonus_sums, 0), head_rows(rate_sums, 0)
    grad_proj = jnp.stack([grad_receive, grad_keys, grad_values, grad_gate])
    grad_proj, value_sum = lax.optimization_barrier((grad_proj, value_sum))
    part_inputs = jnp.einsum(
        "nte,nde->ntd", grad_proj, projections, preferred_element_type=jnp.float32
    )
    part_hdec, lift_grad, _ = decay_back(grad_log.reshape(seq_count, length, head_cols))
    part_normed_one, part_prev_one, grad_coeffs_time, down_grad, up_grad, decay_proj_grad = mix_back(
        (
            part_inputs[0].reshape(seq_count, length, feature_columns),
            part_inputs[1].reshape(seq_count, length, feature_columns),
            part_inputs[2].reshape(seq_count, length, feature_columns),
            part_inputs[3].reshape(seq_count, length, feature_columns),
            part_hdec,
        )
    )
    from_next_one = from_behind(for_sending(part_prev_one), "seq", -1).astype(jnp.float32)
    part_normed_one = part_normed_one.at[:, -1, :].add(from_next_one)
    part_block, grad_gain_one, grad_bias_one = norm_one_back(part_normed_one)
    input_grad = own_half(grad_residual) + half_sum(part_block)
    small_sums = packed_scatter(
        [
            (jnp.stack([grad_gain_one, 0.5 * grad_gain_two]), 1),
            (jnp.stack([grad_bias_one, 0.5 * grad_bias_two]), 1),
            (grad_coeffs_time + grad_coeffs_chan, 1),
            (down_grad, 0),
            (up_grad, 1),
            (decay_proj_grad, 0),
            (lift_grad.reshape(decay_lift.shape), 2),
            (base_grad.reshape(decay_base.shape), 1),
            (reward_cotangent_term, 1),
            (group_gain_grad, 1),
            (group_bias_grad, 1),
        ],
        gathered,
    )
    rest = [part + other_half(part) for part in small_sums[:6]] + small_sums[6:]
    last_branch, key_sum = lax.optimization_barrier((grad_branch, key_sum))
    *proj_sums, out_sum, recept_sum = ring_sums(
        [(stacked, grad_proj, (branch,)) for branch in range(4)]
        + [
            (last_branch.reshape(tokens, -1), mixer_in.reshape(tokens, -1), ()),
            (chan_recept_b.reshape(tokens, -1), grad_recept.reshape(tokens, -1), ()),
        ],
        sizes,
        0,
    )
    coeff_rows = jnp.concatenate([rest[2][:1], rest[2][2:]], axis=0)
    decay_row = rest[2][1:2]
    return (
        output,
        input_grad,
        state_grad,
        rest[0],
        rest[1],
        coeff_rows,
        decay_row,
        rest[3],
        rest[4],
        rest[5],
        rest[6],
        jnp.stack(proj_sums),
        out_sum.T,
        rest[7],
        rest[8],
        rest[9],
        rest[10],
        key_sum,
        value_sum.T,
        recept_sum,
        total_least,
        total_most,
    )


def solution(mesh):
    return jax.shard_map(
        per_device,
        mesh=mesh,
        in_specs=(
            P("dp", "seq", None),
            P("dp", "tp", None, None),
            P(None, ("dp", "seq")),
            P(None, ("dp", "seq")),
            P(None, ("dp", "seq")),
            P(("dp", "seq"), None),
            P(None, ("dp", "seq")),
            P(("dp", "seq"), None),
            P(None, "tp", ("dp", "seq")),
            P(None, ("dp", "seq"), "tp"),
            P("tp", ("dp", "seq")),
            P("tp", ("dp", "seq")),
            P("tp", ("dp", "seq")),
            P("tp", ("dp", "seq")),
            P("tp", ("dp", "seq")),
            P(None, "tp"),
            P("tp", None),
            P(None, "tp"),
            P("dp", "seq", "tp"),
        ),
        out_specs=(
            P("dp", "seq", "tp"),
            P("dp", "seq", "tp"),
            P("dp", "tp", None, None),
            P(None, ("dp", "seq")),
            P(None, ("dp", "seq")),
            P(None, ("dp", "seq")),
            P(None, ("dp", "seq")),
            P(("dp", "seq"), None),
            P(None, ("dp", "seq")),
            P(("dp", "seq"), None),
            P(None, "tp", ("dp", "seq")),
            P(None, ("dp", "seq"), "tp"),
            P("tp", ("dp", "seq")),
            P("tp", ("dp", "seq")),
            P("tp", ("dp", "seq")),
            P("tp", ("dp", "seq")),
            P("tp", ("dp", "seq")),
            P(("dp", "seq"), "tp"),
            P("tp", ("dp", "seq")),
            P(("dp", "seq"), "tp"),
            P("dp", "tp"),
            P("dp", "tp"),
        ),
        check_vma=False,
    )
```

```python
import functools

import jax
import jax.numpy as jnp
from jax import lax
from jax.experimental import pallas as pl
from jax.experimental.pallas import tpu as pltpu
from jax.sharding import PartitionSpec as P

NORM_EPS = 1e-05
GROUP_EPS = 0.00064


def from_behind(block, axis, distance):
    devices = range(lax.axis_size(axis))
    route = [(i - distance, i) for i in devices if i - distance in devices]
    return lax.ppermute(block, axis, route)


def for_sending(array):

    def short(part):
        return part.astype(jnp.bfloat16) if part.dtype == jnp.float32 else part

    return jax.tree.map(short, array)


def layer_norm(values, scale_row, shift_row):
    mean_val = jnp.mean(values, axis=-1, keepdims=True)
    centered = values - mean_val
    variance = jnp.mean(centered * centered, axis=-1, keepdims=True)
    return centered * lax.rsqrt(variance + NORM_EPS) * scale_row + shift_row


def channel_mix(normalized_rows, preceding_row, shift_coefficient):
    earlier = jnp.concatenate([preceding_row[:, None, :], normalized_rows[:, :-1, :]], axis=1)
    shift_difference = earlier - normalized_rows
    return (
        normalized_rows + shift_difference * shift_coefficient[6],
        normalized_rows + shift_difference * shift_coefficient[7],
    )


WIDE = 256
PAIR = 128
EXTRA = 16


def halves_dot(left, right, dims):
    return lax.dot_general(
        left.astype(jnp.bfloat16),
        right.astype(jnp.bfloat16),
        (dims, ((), ())),
        preferred_element_type=jnp.float32,
    )


def exact_dot(ones, values):
    high = values.astype(jnp.bfloat16)
    rest = values - high.astype(jnp.float32)
    middle = rest.astype(jnp.bfloat16)
    low = (rest - middle.astype(jnp.float32)).astype(jnp.bfloat16)
    ones = ones.astype(jnp.bfloat16)
    dims = ((1,), (0,))
    return (
        halves_dot(ones, high, dims) + halves_dot(ones, middle, dims) + halves_dot(ones, low, dims)
    )


def iota(shape, dim):
    return lax.broadcasted_iota(jnp.int32, shape, dim)


def first_head(shape):
    return iota(shape, len(shape) - 1) < PAIR // 2


def compact(full):
    top, low = full[: PAIR // 2], full[PAIR // 2 :]
    return jnp.where(first_head(top.shape), top, low)


def spread(state):
    first = first_head(state.shape)
    return jnp.concatenate([jnp.where(first, state, 0.0), jnp.where(first, 0.0, state)], axis=0)


def head_sum(values):
    first = first_head(values.shape)
    a = jnp.sum(jnp.where(first, values, 0.0), axis=-1, keepdims=True)
    b = jnp.sum(jnp.where(first, 0.0, values), axis=-1, keepdims=True)
    return jnp.where(first, a, b)


def running_decay(log_rates):
    length = log_rates.shape[0]
    rates = -jnp.exp(log_rates)
    up_to = iota((length, length), 0) >= iota((length, length), 1)
    return rates, exact_dot(up_to.astype(jnp.float32), rates)


def two_parts(row):
    high = row.astype(jnp.bfloat16).astype(jnp.float32)
    return high, row - high


def totals_kernel(kv_ref, log_ref, packed_ref):
    for pair in range(WIDE // PAIR):
        lanes = slice(pair * PAIR, (pair + 1) * PAIR)
        keys, values = kv_ref[1, :, lanes], kv_ref[2, :, lanes]
        rates, total = running_decay(log_ref[:, lanes])
        length = rates.shape[0]
        final = total[length - 1 : length]
        state = compact(halves_dot(keys * jnp.exp(final - total), values, ((0,), (0,))))
        decay = jnp.exp(rates)
        rows = [
            *two_parts(jnp.exp(final)),
            *two_parts(jnp.min(decay, axis=0, keepdims=True)),
            *two_parts(jnp.max(decay, axis=0, keepdims=True)),
        ]
        row_at = iota((EXTRA, PAIR), 0)
        extra = jnp.zeros((EXTRA, PAIR), jnp.float32)
        for at, row in enumerate(rows):
            extra = jnp.where(row_at == at, row, extra)
        packed_ref[0, pair] = jnp.concatenate([state, extra], axis=0).astype(jnp.bfloat16)


def inner_scores(receive, keys, rates, total):
    length = receive.shape[0]
    before = total - rates
    middle = before[length // 2 : length // 2 + 1]
    up, down = jnp.exp(before - middle), jnp.exp(middle - total)
    rows, columns = receive * up, keys * down
    first = first_head(rows.shape)
    later = iota((length, length), 0) > iota((length, length), 1)
    columns = columns.astype(jnp.bfloat16)
    scores = [
        jnp.where(
            later, halves_dot(jnp.where(own, rows, 0.0), columns, ((1,), (1,))), 0.0
        ).astype(jnp.bfloat16)
        for own in (first, jnp.logical_not(first))
    ]
    return rows.astype(jnp.bfloat16), columns, scores, up, down, before


def heads_apply(left, right, side):
    first = first_head(right.shape)
    a = halves_dot(left[0], right, ((side,), (0,)))
    b = halves_dot(left[1], right, ((side,), (0,)))
    return jnp.where(first, a, b)


def inner_kernel(rkv_ref, log_ref, bonus_ref, inner_ref, decayed_ref):
    for pair in range(WIDE // PAIR):
        lanes = slice(pair * PAIR, (pair + 1) * PAIR)
        receive, keys, values = (rkv_ref[n, :, lanes] for n in range(3))
        rates, total = running_decay(log_ref[:, lanes])
        _, _, scores, _, _, before = inner_scores(receive, keys, rates, total)
        now = head_sum(receive * bonus_ref[:, lanes] * keys)
        inner_ref[:, lanes] = heads_apply(scores, values, 1) + now * values
        decayed_ref[:, lanes] = (receive * jnp.exp(before)).astype(jnp.bfloat16)


def block_decays(extra):
    blocks = extra.shape[0]
    flat = extra.astype(jnp.float32)
    columns = []
    for start in range(0, blocks, PAIR // EXTRA):
        some = flat[start : start + PAIR // EXTRA]
        some = some.reshape(some.shape[0] * EXTRA, PAIR)
        if some.shape[0] < PAIR:
            some = jnp.concatenate(
                [some, jnp.zeros((PAIR - some.shape[0], PAIR), jnp.float32)], axis=0
            )
        turned = some.T
        for k in range(min(PAIR // EXTRA, blocks - start)):
            both = turned[:, k * EXTRA : k * EXTRA + 1] + turned[:, k * EXTRA + 1 : k * EXTRA + 2]
            columns.append(compact(jnp.broadcast_to(both, (PAIR, PAIR))))
    return columns


def norm_heads(wkv, count):
    mean = head_sum(wkv) * (1.0 / count)
    centered = wkv - mean
    scale = lax.rsqrt(head_sum(centered * centered) * (1.0 / count) + GROUP_EPS)
    return centered * scale, scale


def join_kernel(
    place_ref, inner_ref, decayed_ref, gate_ref, packed_ref, start_ref, gain_ref, bias_ref, *outs
):
    wkv_ref, mixer_ref, state_ref, range_ref = outs
    blocks = packed_ref.shape[0]
    place = place_ref[0]
    for pair in range(WIDE // PAIR):
        lanes = slice(pair * PAIR, (pair + 1) * PAIR)
        state = start_ref[0, pair]
        extra = packed_ref[:, 0, pair, PAIR // 2 :, :]
        decays = block_decays(extra)
        extra = extra.astype(jnp.float32)
        range_ref[0, :, lanes] = put_rows(
            [
                jnp.min(extra[:, 2] + extra[:, 3], axis=0, keepdims=True),
                jnp.max(extra[:, 4] + extra[:, 5], axis=0, keepdims=True),
            ]
        )
        for k in range(blocks - 1):
            term = packed_ref[k, 0, pair, : PAIR // 2, :].astype(jnp.float32)
            state = jnp.where(k < place, decays[k] * state + term, state)
        state_ref[0, pair] = state
        wkv = inner_ref[:, lanes] + halves_dot(decayed_ref[:, lanes], spread(state), ((1,), (0,)))
        wkv_ref[:, lanes] = wkv
        normed, _ = norm_heads(wkv, PAIR // 2)
        normed = normed * gain_ref[:, lanes] + bias_ref[:, lanes]
        gate = gate_ref[0, :, lanes]
        mixer_ref[:, lanes] = (normed * gate * jax.nn.sigmoid(gate)).astype(jnp.bfloat16)


def put_rows(rows):
    row_at = iota((8, PAIR), 0)
    out = jnp.zeros((8, PAIR), jnp.float32)
    for at, row in enumerate(rows):
        out = jnp.where(row_at == at, row, out)
    return out


def back_join_kernel(grad_ref, wkv_ref, gate_ref, decayed_ref, gain_ref, bias_ref, *outs):
    grad_wkv_ref, grad_gate_ref, term_ref, sums_ref = outs
    for pair in range(WIDE // PAIR):
        lanes = slice(pair * PAIR, (pair + 1) * PAIR)
        grad, gate = grad_ref[:, lanes], gate_ref[0, :, lanes]
        gain = gain_ref[:, lanes]
        hat, scale = norm_heads(wkv_ref[:, lanes], PAIR // 2)
        sigmoid = jax.nn.sigmoid(gate)
        normed = hat * gain + bias_ref[:, lanes]
        grad_gate = grad * normed * sigmoid * (1.0 + gate * (1.0 - sigmoid))
        grad_gate_ref[:, lanes] = grad_gate.astype(jnp.bfloat16)
        grad_normed = grad * gate * sigmoid
        sums_ref[0, :, lanes] = put_rows(
            [
                jnp.sum(grad_normed * hat, axis=0, keepdims=True),
                jnp.sum(grad_normed, axis=0, keepdims=True),
            ]
        )
        q = grad_normed * gain
        each = 2.0 / PAIR
        grad_wkv = scale * (q - head_sum(q) * each - hat * (head_sum(q * hat) * each))
        grad_wkv_ref[:, lanes] = grad_wkv
        term_ref[0, pair] = compact(
            halves_dot(decayed_ref[:, lanes], grad_wkv, ((0,), (0,)))
        ).astype(jnp.bfloat16)


def back_inner_kernel(rkv_ref, log_ref, bonus_ref, grad_ref, state_ref, *outs):
    receive_ref, key_ref, value_ref, running_ref, sums_ref = outs
    for pair in range(WIDE // PAIR):
        lanes = slice(pair * PAIR, (pair + 1) * PAIR)
        receive, keys, values = (rkv_ref[n, :, lanes] for n in range(3))
        bonus, grad = bonus_ref[:, lanes], grad_ref[:, lanes]
        rates, total = running_decay(log_ref[:, lanes])
        rows, columns, scores, up, down, before = inner_scores(receive, keys, rates, total)
        length = receive.shape[0]
        first = first_head(values.shape)
        later = iota((length, length), 0) > iota((length, length), 1)
        low_values = values.astype(jnp.bfloat16)
        low_grad = grad.astype(jnp.bfloat16)
        grad_scores = [
            jnp.where(
                later, halves_dot(jnp.where(own, grad, 0.0), low_values, ((1,), (1,))), 0.0
            ).astype(jnp.bfloat16)
            for own in (first, jnp.logical_not(first))
        ]
        from_state = halves_dot(low_grad, spread(state_ref[0, pair]), ((1,), (1,)))
        far_receive = heads_apply(grad_scores, columns, 1) * up + jnp.exp(before) * from_state
        far_keys = heads_apply(grad_scores, rows, 0) * down
        meet = head_sum(grad * values)
        receive_ref[:, lanes] = (far_receive + bonus * keys * meet).astype(jnp.bfloat16)
        key_ref[:, lanes] = far_keys + bonus * receive * meet
        now = head_sum(receive * bonus * keys)
        value_ref[:, lanes] = heads_apply(scores, low_grad, 0) + now * grad
        moved = receive * far_receive
        moved = pltpu.roll(moved, length - 1, 0)
        moved = jnp.where(iota(moved.shape, 0) == length - 1, 0.0, moved)
        running_ref[:, lanes] = moved - keys * far_keys
        sums_ref[0, :, lanes] = put_rows([jnp.sum(receive * keys * meet, axis=0, keepdims=True)])


def back_outer_kernel(
    place_ref, kv_ref, log_ref, key_ref, value_ref, running_ref, state_ref, packed_ref, terms_ref, *outs
):
    grad_key_ref, grad_value_ref, grad_log_ref, start_ref, sums_ref = outs
    blocks = packed_ref.shape[0]
    place = place_ref[0]
    for pair in range(WIDE // PAIR):
        lanes = slice(pair * PAIR, (pair + 1) * PAIR)
        keys, values = kv_ref[1, :, lanes], kv_ref[2, :, lanes]
        rates, total = running_decay(log_ref[:, lanes])
        length = keys.shape[0]
        final = total[length - 1 : length]
        decays = block_decays(packed_ref[:, 0, pair, PAIR // 2 :, :])
        later = jnp.zeros((PAIR // 2, PAIR), jnp.float32)
        whole = jnp.zeros((PAIR // 2, PAIR), jnp.float32)
        for k in range(blocks - 1, -1, -1):
            term = terms_ref[k, 0, pair].astype(jnp.float32)
            later = jnp.where(k > place, decays[k] * later + term, later)
            whole = decays[k] * whole + term
        start_ref[0, pair] = whole
        spread_later = spread(later).astype(jnp.bfloat16)
        fade = jnp.exp(final - total)
        far_keys = fade * halves_dot(values, spread_later, ((1,), (1,)))
        grad_key_ref[:, lanes] = (key_ref[:, lanes] + far_keys).astype(jnp.bfloat16)
        grad_value_ref[:, lanes] = (
            value_ref[:, lanes] + halves_dot(keys * fade, spread_later, ((1,), (0,)))
        ).astype(jnp.bfloat16)
        moved = keys * far_keys
        met = spread(state_ref[0, pair] * later)
        high, low = two_parts(met)
        ones = jnp.ones((8, PAIR), jnp.bfloat16)
        met_row = (halves_dot(ones, high, ((1,), (1,))) + halves_dot(ones, low, ((1,), (1,))))[:1]
        last = jnp.sum(moved, axis=0, keepdims=True) + jnp.exp(final) * met_row
        running = running_ref[:, lanes] - moved
        running = running + jnp.where(iota(running.shape, 0) == length - 1, last, 0.0)
        onward = iota((length, length), 0) <= iota((length, length), 1)
        grad_log = exact_dot(onward.astype(jnp.float32), running) * rates
        grad_log_ref[:, lanes] = grad_log
        sums_ref[0, :, lanes] = put_rows([jnp.sum(grad_log, axis=0, keepdims=True)])


class Recurrence:
    def __init__(self, sequences, length, columns):
        self.sequences, self.length, self.columns = sequences, length, columns
        self.grid = (sequences, columns // WIDE)
        self.pairs = columns // PAIR
        self.tokens = pl.BlockSpec((length, WIDE), lambda s, p: (s, p))
        self.row = pl.BlockSpec((1, WIDE), lambda s, p: (0, p))
        self.stack = pl.BlockSpec((3, length, WIDE), lambda s, p: (0, s, p))
        self.gate = pl.BlockSpec((1, length, WIDE), lambda s, p: (3, s, p))
        self.state = pl.BlockSpec((1, WIDE // PAIR, PAIR // 2, PAIR), lambda s, p: (s, p, 0, 0))
        self.sums = pl.BlockSpec((1, 8, WIDE), lambda s, p: (s, 0, p))
        self.place = pl.BlockSpec(memory_space=pltpu.SMEM)

    def packed(self, blocks=None):
        rows = PAIR // 2 + EXTRA
        if blocks is None:
            return pl.BlockSpec((1, WIDE // PAIR, rows, PAIR), lambda s, p: (s, p, 0, 0))
        return pl.BlockSpec((blocks, 1, WIDE // PAIR, rows, PAIR), lambda s, p: (0, s, p, 0, 0))

    def terms(self, blocks):
        return pl.BlockSpec(
            (blocks, 1, WIDE // PAIR, PAIR // 2, PAIR), lambda s, p: (0, s, p, 0, 0)
        )

    def token_shape(self, kind):
        return jax.ShapeDtypeStruct((self.sequences * self.length, self.columns), kind)

    def state_shape(self, kind, rows=PAIR // 2):
        return jax.ShapeDtypeStruct((self.sequences, self.pairs, rows, PAIR), kind)

    def sums_shape(self):
        return jax.ShapeDtypeStruct((self.sequences, 8, self.columns), jnp.float32)

    def call(self, kernel, ins, outs, args, flops):
        size = sum(arg.size * arg.dtype.itemsize for arg in args)
        return pl.pallas_call(
            kernel,
            grid=self.grid,
            in_specs=ins,
            out_specs=[spec for spec, _ in outs],
            out_shape=[shape for _, shape in outs],
            compiler_params=pltpu.CompilerParams(vmem_limit_bytes=40 * 2**20),
            cost_estimate=pl.CostEstimate(
                flops=flops, bytes_accessed=size, transcendentals=6 * args[0].size
            ),
        )(*args)

    def totals(self, projected, log_rows):
        outs = [(self.packed(), self.state_shape(jnp.bfloat16, PAIR // 2 + EXTRA))]
        return self.call(
            totals_kernel, [self.stack, self.tokens], outs, (projected, log_rows), 14 * 10**9
        )[0]

    def inner(self, projected, log_rows, bonus):
        outs = [
            (self.tokens, self.token_shape(jnp.float32)),
            (self.tokens, self.token_shape(jnp.bfloat16)),
        ]
        ins = [self.stack, self.tokens, self.row]
        return self.call(inner_kernel, ins, outs, (projected, log_rows, bonus), 16 * 10**9)

    def join(self, place, inner, decayed, projected, packed, start, gain, bias):
        ins = [
            self.place,
            self.tokens,
            self.tokens,
            self.gate,
            self.packed(packed.shape[0]),
            self.state,
            self.row,
            self.row,
        ]
        outs = [
            (self.tokens, self.token_shape(jnp.float32)),
            (self.tokens, self.token_shape(jnp.bfloat16)),
            (self.state, self.state_shape(jnp.float32)),
            (self.sums, self.sums_shape()),
        ]
        args = (place, inner, decayed, projected, packed, start, gain, bias)
        return self.call(join_kernel, ins, outs, args, 21 * 10**9)

    def back_join(self, grad, wkv, projected, decayed, gain, bias):
        ins = [self.tokens, self.tokens, self.gate, self.tokens, self.row, self.row]
        outs = [
            (self.tokens, self.token_shape(jnp.float32)),
            (self.tokens, self.token_shape(jnp.bfloat16)),
            (self.state, self.state_shape(jnp.bfloat16)),
            (self.sums, self.sums_shape()),
        ]
        args = (grad, wkv, projected, decayed, gain, bias)
        return self.call(back_join_kernel, ins, outs, args, 15 * 10**9)

    def back_inner(self, projected, log_rows, bonus, grad, state):
        ins = [self.stack, self.tokens, self.row, self.tokens, self.state]
        outs = [
            (self.tokens, self.token_shape(jnp.bfloat16)),
            (self.tokens, self.token_shape(jnp.float32)),
            (self.tokens, self.token_shape(jnp.float32)),
            (self.tokens, self.token_shape(jnp.float32)),
            (self.sums, self.sums_shape()),
        ]
        args = (projected, log_rows, bonus, grad, state)
        return self.call(back_inner_kernel, ins, outs, args, 22 * 10**9)

    def back_outer(self, place, projected, log_rows, keys, values, running, state, packed, terms):
        blocks = packed.shape[0]
        ins = [
            self.place,
            self.stack,
            self.tokens,
            self.tokens,
            self.tokens,
            self.tokens,
            self.state,
            self.packed(blocks),
            self.terms(blocks),
        ]
        outs = [
            (self.tokens, self.token_shape(jnp.bfloat16)),
            (self.tokens, self.token_shape(jnp.bfloat16)),
            (self.tokens, self.token_shape(jnp.float32)),
            (self.state, self.state_shape(jnp.float32)),
            (self.sums, self.sums_shape()),
        ]
        args = (place, projected, log_rows, keys, values, running, state, packed, terms)
        return self.call(back_outer_kernel, ins, outs, args, 24 * 10**9)


def paired_states(states):
    sequences, heads, size, _ = states.shape
    pairs = states.reshape(sequences, heads // 2, 2, size, size)
    return pairs.transpose(0, 1, 3, 2, 4).reshape(sequences, heads // 2, size, 2 * size)


def single_states(pairs):
    sequences, count, size, _ = pairs.shape
    heads = pairs.reshape(sequences, count, size, 2, size).transpose(0, 1, 3, 2, 4)
    return heads.reshape(sequences, 2 * count, size, size)


BRANCHES = (3, 1, 2, 4)
STRIP = 512


def mix_back_kernel(
    x_ref,
    before_ref,
    grad_ref,
    log_ref,
    hidden_ref,
    decay_ref,
    proj_ref,
    coeff_ref,
    norm_ref,
    down_ref,
    up_ref,
    decay_down_ref,
    decay_up_ref,
    block_ref,
    edge_ref,
    sums_ref,
    grad_up_ref,
    grad_down_ref,
    grad_decay_down_ref,
    grad_decay_up_ref,
    hat_ref,
    grad_diff_ref,
    grad_all_ref,
):
    length, columns = x_ref.shape[1:]
    ranks = up_ref.shape[0] // 5
    strips = columns // STRIP
    low = jnp.bfloat16
    last = length - 1

    @pl.when(pl.program_id(0) == 0)
    def _():
        for ref in (sums_ref, grad_up_ref, grad_down_ref, grad_decay_down_ref, grad_decay_up_ref):
            ref[...] = jnp.zeros_like(ref)

    x = x_ref[0].astype(jnp.float32)
    mean = jnp.mean(x, axis=-1, keepdims=True)
    variance = jnp.mean((x - mean) * (x - mean), axis=-1, keepdims=True)
    scale = lax.rsqrt(variance + NORM_EPS)
    hidden, hidden_decay = hidden_ref[...], decay_ref[...]
    low_hidden, low_decay = hidden.astype(low), hidden_decay.astype(low)
    grad_log = log_ref[...].astype(low)
    grad_decay = halves_dot(grad_log, decay_up_ref[...], ((1,), (1,)))
    grad_decay = grad_decay * (1.0 - hidden_decay * hidden_decay)
    low_grad_decay = grad_decay.astype(low)
    grad_decay_up_ref[...] += halves_dot(low_decay, grad_log, ((0,), (0,)))

    def strip_of(strip):
        return pl.ds(pl.multiple_of(strip * STRIP, STRIP), STRIP)

    def normed_and_diff(at, hat):
        normed = hat * norm_ref[0:1, at] + norm_ref[1:2, at]
        earlier = pltpu.roll(normed, 1, 0)
        earlier = jnp.where(iota(normed.shape, 0) == 0, before_ref[0, :, at], earlier)
        return normed, earlier - normed

    def first(strip, grad_pre):
        at = strip_of(strip)
        hat = (x_ref[0, :, at].astype(jnp.float32) - mean) * scale
        hat_ref[:, at] = hat
        normed, diff = normed_and_diff(at, hat)
        grad_diff = jnp.zeros_like(diff)
        grad_all = jnp.zeros_like(diff)
        parts = []
        for branch in range(5):
            rows = slice(branch * ranks, (branch + 1) * ranks)
            up = up_ref[rows, at]
            weight = coeff_ref[1 + branch : 2 + branch, at] + halves_dot(
                low_hidden[:, rows], up, ((1,), (0,))
            )
            if branch == 0:
                mixed = normed + diff * weight
                grad_decay_down_ref[:, at] += halves_dot(low_grad_decay, mixed, ((0,), (0,)))
                grad = halves_dot(low_grad_decay, decay_down_ref[:, at], ((1,), (0,)))
            else:
                n = BRANCHES.index(branch)
                grad = halves_dot(grad_ref[n], proj_ref[n, at, :], ((1,), (1,)))
            grad_all += grad
            grad_diff += grad * weight
            moved = grad * diff
            sums_ref[1 + branch : 2 + branch, at] += jnp.sum(moved, axis=0, keepdims=True)
            moved = moved.astype(low)
            grad_up_ref[rows, at] += halves_dot(low_hidden[:, rows], moved, ((0,), (0,)))
            parts.append(halves_dot(moved, up, ((1,), (1,))))
        grad_diff_ref[:, at] = grad_diff
        grad_all_ref[:, at] = grad_all
        return grad_pre + jnp.concatenate(parts, axis=1)

    grad_pre = lax.fori_loop(0, strips, first, jnp.zeros(hidden.shape, jnp.float32))
    grad_pre = (grad_pre * (1.0 - hidden * hidden)).astype(low)

    def second(strip, carry):
        total, against = carry
        at = strip_of(strip)
        hat = hat_ref[:, at]
        normed, diff = normed_and_diff(at, hat)
        coeff = coeff_ref[0:1, at]
        grad_base = halves_dot(grad_pre, down_ref[:, at], ((1,), (0,)))
        grad_down_ref[:, at] += halves_dot(grad_pre, normed + diff * coeff, ((0,), (0,)))
        sums_ref[0:1, at] += jnp.sum(grad_base * diff, axis=0, keepdims=True)
        grad_diff = grad_diff_ref[:, at] + grad_base * coeff
        edge_ref[0, :, at] = grad_diff[0:1]
        onward = pltpu.roll(grad_diff, last, 0)
        onward = jnp.where(iota(onward.shape, 0) == last, 0.0, onward)
        grad = grad_base + grad_all_ref[:, at] - grad_diff + onward
        sums_ref[6:7, at] += jnp.sum(grad * hat, axis=0, keepdims=True)
        sums_ref[7:8, at] += jnp.sum(grad, axis=0, keepdims=True)
        q = grad * norm_ref[0:1, at]
        grad_all_ref[:, at] = q
        total += jnp.sum(q, axis=-1, keepdims=True)
        against += jnp.sum(q * hat, axis=-1, keepdims=True)
        return total, against

    zero = jnp.zeros((length, 1), jnp.float32)
    total, against = lax.fori_loop(0, strips, second, (zero, zero))
    total, against = total * (1.0 / columns), against * (1.0 / columns)

    def third(strip, carry):
        at = strip_of(strip)
        block_ref[0, :, at] = scale * (grad_all_ref[:, at] - total - hat_ref[:, at] * against)
        return carry

    lax.fori_loop(0, strips, third, 0)


def mix_back(
    block_input,
    before,
    grad_proj,
    grad_log,
    hidden,
    hidden_decay,
    projections,
    coeffs,
    norm,
    down,
    up,
    decay_down,
    decay_up,
):
    sequences, length, columns = block_input.shape
    heads = grad_proj.shape[-1]
    ranks, decay_ranks = up.shape[0], decay_up.shape[0]

    def whole(array):
        return pl.BlockSpec(array.shape, lambda s: (0,) * array.ndim)

    def kept(shape):
        return pl.BlockSpec(shape, lambda s: (0, 0)), jax.ShapeDtypeStruct(shape, jnp.float32)

    block = pl.BlockSpec((1, length, columns), lambda s: (s, 0, 0))
    edge = pl.BlockSpec((1, 1, columns), lambda s: (s, 0, 0))
    outs = [
        (block, jax.ShapeDtypeStruct(block_input.shape, jnp.float32)),
        (edge, jax.ShapeDtypeStruct((sequences, 1, columns), jnp.float32)),
        kept((8, columns)),
        kept((ranks, columns)),
        kept((ranks, columns)),
        kept((decay_ranks, columns)),
        kept((decay_ranks, heads)),
    ]
    args = (
        block_input,
        before,
        grad_proj,
        grad_log,
        hidden,
        hidden_decay,
        projections,
        coeffs,
        norm,
        down,
        up,
        decay_down,
        decay_up,
    )
    return pl.pallas_call(
        mix_back_kernel,
        grid=(sequences,),
        in_specs=[
            block,
            edge,
            pl.BlockSpec((4, length, heads), lambda s: (0, s, 0)),
            pl.BlockSpec((length, heads), lambda s: (s, 0)),
            pl.BlockSpec((length, hidden.shape[1]), lambda s: (s, 0)),
            pl.BlockSpec((length, decay_ranks), lambda s: (s, 0)),
            pl.BlockSpec(projections.shape, lambda s: (0, 0, 0), pipeline_mode=pl.Buffered(1)),
        ]
        + [whole(array) for array in args[7:]],
        out_specs=[spec for spec, _ in outs],
        out_shape=[shape for _, shape in outs],
        scratch_shapes=[pltpu.VMEM((length, columns), jnp.float32)] * 3,
        compiler_params=pltpu.CompilerParams(vmem_limit_bytes=58 * 2**20),
        cost_estimate=pl.CostEstimate(
            flops=7 * 10**10, bytes_accessed=40 * 2**20, transcendentals=0
        ),
    )(*args)


def sum_columns(rows):
    shards = lax.axis_size("dp") * lax.axis_size("seq")
    parts = rows.reshape(rows.shape[0], shards, -1).transpose(1, 0, 2)
    return lax.psum_scatter(
        parts.reshape(-1, parts.shape[2]), ("dp", "seq"), scatter_dimension=0, tiled=True
    )


def other_half(block):
    return lax.ppermute(block, "tp", [(0, 1), (1, 0)])


CORES = 2


def ring_places(dp_size, seq_size):
    per_row = seq_size // CORES
    count = dp_size * per_row

    def chip(position):
        position = lax.rem(position + 2 * count, count)
        row = lax.div(position, per_row)
        column = lax.rem(position, per_row)
        column = jnp.where(lax.rem(row, 2) == 0, column, per_row - 1 - column)
        return row, column

    def own():
        row, column = lax.axis_index("dp"), lax.div(lax.axis_index("seq"), CORES)
        return row * per_row + jnp.where(lax.rem(row, 2) == 0, column, per_row - 1 - column)

    return count, chip, own


def cut_rings(widths, rings):
    each = sum(widths) // rings
    runs, product, column = [], 0, 0
    for _ in range(rings):
        run, left = [], each
        while left:
            take = min(left, widths[product] - column)
            run.append((product, column, take))
            left, column = left - take, column + take
            if column == widths[product]:
                product, column = product + 1, 0
        runs.append(run)
    return runs


def ring_kernel(dp_size, seq_size, rows, widths, runs, places, operands, *refs):
    products = len(widths)
    lefts = [(refs[left], lead) for left, _, lead in places]
    rights = [(refs[right], lead) for _, right, lead in places]
    totals, refs = refs[operands : operands + products], refs[operands + products :]
    rings = len(runs)
    mine, pair_out, pair_in, ring_out, ring_in = [
        refs[k * rings : (k + 1) * rings] for k in range(5)
    ]
    pair_send, pair_recv, pair_free, ring_send, ring_recv, ring_free = refs[5 * rings :]
    count, chip, own = ring_places(dp_size, seq_size)
    position, core = own(), lax.rem(lax.axis_index("seq"), CORES)

    def device(place, which):
        row, column = chip(place)
        return {"dp": row, "seq": column * CORES + which}

    sibling = device(position, 1 - core)
    after, before = device(position + 1, core), device(position - 1, core)
    barrier = pltpu.get_barrier_semaphore()
    for other in (sibling, after, before):
        pl.semaphore_signal(barrier, inc=1, device_id=other, device_id_type=pl.DeviceIdType.MESH)
    pl.semaphore_wait(barrier, 3)

    def pair_copy(ring):
        return pltpu.make_async_remote_copy(
            src_ref=pair_out[ring],
            dst_ref=pair_in[ring],
            send_sem=pair_send.at[ring],
            recv_sem=pair_recv.at[ring],
            device_id=sibling,
            device_id_type=pl.DeviceIdType.MESH,
        )

    def ring_copy(ring, slot):
        return pltpu.make_async_remote_copy(
            src_ref=ring_out[ring].at[slot],
            dst_ref=ring_in[ring].at[slot],
            send_sem=ring_send.at[ring, slot],
            recv_sem=ring_recv.at[ring, slot],
            device_id=after if ring % 2 == 0 else before,
            device_id_type=pl.DeviceIdType.MESH,
        )

    def part(ring, place, which, put):
        row, column = chip(place)
        start = (row * seq_size + column * CORES + which) * rows
        start = pl.multiple_of(start, rows)
        at = 0
        for product, first, wide in runs[ring]:
            ref, lead = lefts[product]
            if rows % 128 == 0:
                left = ref[(*lead, slice(None), pl.ds(start, rows))]
            else:
                left = ref[(*lead, pl.ds(start, rows), slice(None))]
            ref, lead = rights[product]
            right = ref[(*lead, slice(None), pl.ds(first, wide))]
            put(
                at,
                wide,
                lax.dot_general(
                    left,
                    right,
                    (((0 if rows % 128 == 0 else 1,), (0,)), ((), ())),
                    preferred_element_type=jnp.float32,
                ),
            )
            at += wide

    def turn(step, carry):
        slot = lax.rem(step, 2)
        last = 1 - slot
        for ring in range(rings):
            place = position - 1 - step if ring % 2 == 0 else position + 1 + step

            @pl.when(step >= 1)
            def _():
                pair_copy(ring).wait_send()

            def put_out(at, wide, value):
                pair_out[ring][:, at : at + wide] = value.astype(jnp.bfloat16)

            part(ring, place, 1 - core, put_out)

            @pl.when(step >= 1)
            def _():
                pl.semaphore_wait(pair_free.at[ring], 1)

            pair_copy(ring).start()

            def put_mine(at, wide, value):
                mine[ring][:, at : at + wide] = value

            part(ring, place, core, put_mine)
        for ring in range(rings):
            source = before if ring % 2 == 0 else after
            pair_copy(ring).wait_recv()

            @pl.when(step == 0)
            def _():
                ring_out[ring][slot] = (
                    mine[ring][...] + pair_in[ring][...].astype(jnp.float32)
                ).astype(jnp.bfloat16)

            @pl.when(step >= 1)
            def _():
                ring_copy(ring, last).wait_recv()

            @pl.when(jnp.logical_and(step >= 1, step < count - 1))
            def _():
                @pl.when(step >= 2)
                def _():
                    ring_copy(ring, slot).wait_send()

                ring_out[ring][slot] = (
                    mine[ring][...]
                    + pair_in[ring][...].astype(jnp.float32)
                    + ring_in[ring][last].astype(jnp.float32)
                ).astype(jnp.bfloat16)

            @pl.when(step == count - 1)
            def _():
                at = 0
                for product, first, wide in runs[ring]:
                    totals[product][:, first : first + wide] = (
                        mine[ring][:, at : at + wide]
                        + pair_in[ring][:, at : at + wide].astype(jnp.float32)
                        + ring_in[ring][last, :, at : at + wide].astype(jnp.float32)
                    )
                    at += wide

            @pl.when(step < count - 1)
            def _():
                @pl.when(step >= 2)
                def _():
                    pl.semaphore_wait(ring_free.at[ring], 1)

                ring_copy(ring, slot).start()
                pl.semaphore_signal(
                    pair_free.at[ring],
                    inc=1,
                    device_id=sibling,
                    device_id_type=pl.DeviceIdType.MESH,
                )

            @pl.when(jnp.logical_and(step >= 1, step < count - 2))
            def _():
                pl.semaphore_signal(
                    ring_free.at[ring],
                    inc=1,
                    device_id=source,
                    device_id_type=pl.DeviceIdType.MESH,
                )

        return carry

    lax.fori_loop(0, count, turn, 0)
    for ring in range(rings):
        pair_copy(ring).wait_send()
        for step in (count - 3, count - 2):
            ring_copy(ring, step % 2).wait_send()


def ring_sums(pairs, sizes, collective_id):
    dp_size, seq_size = sizes
    rows = pairs[0][0].shape[-1] // (dp_size * seq_size)
    tokens = pairs[0][1].shape[-2]
    operands, known, places = [], {}, []

    def place_of(array, turned):
        if id(array) not in known:
            known[id(array)] = len(operands)
            operands.append(jnp.swapaxes(array, -1, -2) if turned else array)
        return known[id(array)]

    for left, right, lead in pairs:
        places.append((place_of(left, rows % 128 != 0), place_of(right, False), lead))
    widths = [right.shape[-1] for _, right, _ in pairs]
    rings = 4
    runs = cut_rings(widths, rings)
    each = sum(widths) // rings
    low = jnp.bfloat16
    return pl.pallas_call(
        functools.partial(
            ring_kernel, dp_size, seq_size, rows, widths, runs, places, len(operands)
        ),
        out_shape=[jax.ShapeDtypeStruct((rows, wide), jnp.float32) for wide in widths],
        in_specs=[pl.BlockSpec(memory_space=pltpu.VMEM)] * len(operands),
        out_specs=[pl.BlockSpec(memory_space=pltpu.VMEM)] * len(pairs),
        scratch_shapes=[pltpu.VMEM((rows, each), jnp.float32)] * rings
        + [pltpu.VMEM((rows, each), low)] * (2 * rings)
        + [pltpu.VMEM((2, rows, each), low)] * (2 * rings)
        + [
            pltpu.SemaphoreType.DMA((rings,)),
            pltpu.SemaphoreType.DMA((rings,)),
            pltpu.SemaphoreType.REGULAR((rings,)),
            pltpu.SemaphoreType.DMA((rings, 2)),
            pltpu.SemaphoreType.DMA((rings, 2)),
            pltpu.SemaphoreType.REGULAR((rings,)),
        ],
        compiler_params=pltpu.CompilerParams(
            collective_id=collective_id, has_side_effects=True, vmem_limit_bytes=60 * 2**20
        ),
        cost_estimate=pl.CostEstimate(
            flops=int(28 * 10**6 * sum(widths)),
            bytes_accessed=2 * tokens * (2048 * len(pairs) + sum(widths)),
            transcendentals=0,
        ),
    )(*operands)


def spread_kernel(dp_size, seq_size, part_ref, whole_ref, local, send, recv, pair_send, pair_recv):
    count = dp_size * seq_size // CORES
    per_row, width = seq_size // CORES, part_ref.shape[1]
    row, core = lax.axis_index("dp"), lax.rem(lax.axis_index("seq"), CORES)
    position = row * per_row + lax.div(lax.axis_index("seq"), CORES)

    def device(place, which):
        place = lax.rem(place + count, count)
        return {"dp": lax.div(place, per_row), "seq": lax.rem(place, per_row) * CORES + which}

    def columns(place, which):
        place = lax.rem(place + count, count)
        return pl.ds(pl.multiple_of((place * CORES + which) * width, width), width)

    barrier = pltpu.get_barrier_semaphore()
    sibling = device(position, 1 - core)
    for other in [sibling] + [device(position + k, core) for k in range(1, count)]:
        pl.semaphore_signal(barrier, inc=1, device_id=other, device_id_type=pl.DeviceIdType.MESH)
    pl.semaphore_wait(barrier, count)

    own = whole_ref.at[:, columns(position, core)]
    keep = pltpu.make_async_copy(part_ref, own, local)
    keep.start()
    copies = [
        pltpu.make_async_remote_copy(
            src_ref=part_ref,
            dst_ref=own,
            send_sem=send.at[k],
            recv_sem=recv.at[k],
            device_id=device(position + k, core),
            device_id_type=pl.DeviceIdType.MESH,
        )
        for k in range(1, count)
    ]
    passed = []
    for k in range(count):
        at = whole_ref.at[:, columns(position - k, core)]
        passed.append(
            pltpu.make_async_remote_copy(
                src_ref=part_ref if k == 0 else at,
                dst_ref=at,
                send_sem=pair_send.at[k],
                recv_sem=pair_recv.at[k],
                device_id=sibling,
                device_id_type=pl.DeviceIdType.MESH,
            )
        )
    for copy in copies:
        copy.start()
    passed[0].start()
    for k in range(1, count):
        copies[k - 1].wait_recv()
        passed[k].start()
    keep.wait()
    for copy in copies:
        copy.wait_send()
    for copy in passed:
        copy.wait()


def spread_columns(part, sizes, collective_id):
    if part.shape[1] % 128:
        return lax.all_gather(part, ("dp", "seq"), axis=1, tiled=True)
    dp_size, seq_size = sizes
    count = dp_size * seq_size // CORES
    rows, width = part.shape
    return pl.pallas_call(
        functools.partial(spread_kernel, dp_size, seq_size),
        out_shape=jax.ShapeDtypeStruct((rows, width * dp_size * seq_size), part.dtype),
        in_specs=[pl.BlockSpec(memory_space=pltpu.VMEM)],
        out_specs=pl.BlockSpec(memory_space=pltpu.VMEM),
        scratch_shapes=[pltpu.SemaphoreType.DMA(())] + [pltpu.SemaphoreType.DMA((count,))] * 4,
        compiler_params=pltpu.CompilerParams(
            collective_id=collective_id, has_side_effects=True, vmem_limit_bytes=16 * 2**20
        ),
        cost_estimate=pl.CostEstimate(
            flops=50 * 10**9, bytes_accessed=4 * 2**20, transcendentals=0
        ),
    )(part)


def mix_kernel(
    x_ref,
    before_ref,
    coeff_ref,
    norm_ref,
    down_ref,
    up_ref,
    decay_down_ref,
    decay_up_ref,
    base_ref,
    mixed_ref,
    hidden_ref,
    decay_ref,
    log_ref,
):
    length, columns = x_ref.shape[1:]
    ranks = up_ref.shape[0] // 5
    strips = columns // STRIP
    x = x_ref[0].astype(jnp.float32)
    mean = jnp.mean(x, axis=-1, keepdims=True)
    variance = jnp.mean((x - mean) * (x - mean), axis=-1, keepdims=True)
    scale = lax.rsqrt(variance + NORM_EPS)

    def normed_and_diff(strip):
        at = pl.ds(pl.multiple_of(strip * STRIP, STRIP), STRIP)
        hat = (x_ref[0, :, at].astype(jnp.float32) - mean) * scale
        normed = hat * norm_ref[0:1, at] + norm_ref[1:2, at]
        earlier = pltpu.roll(normed, 1, 0)
        earlier = jnp.where(iota(normed.shape, 0) == 0, before_ref[0, :, at], earlier)
        return at, normed, earlier - normed

    def first(strip, hidden):
        at, normed, diff = normed_and_diff(strip)
        return hidden + halves_dot(normed + diff * coeff_ref[0:1, at], down_ref[:, at], ((1,), (1,)))

    hidden = lax.fori_loop(0, strips, first, jnp.zeros(hidden_ref.shape, jnp.float32))
    hidden = jnp.tanh(hidden)
    hidden_ref[...] = hidden
    hidden = hidden.astype(jnp.bfloat16)

    def second(strip, decay):
        at, normed, diff = normed_and_diff(strip)
        for branch in range(5):
            rows = slice(branch * ranks, (branch + 1) * ranks)
            weight = coeff_ref[1 + branch : 2 + branch, at] + halves_dot(
                hidden[:, rows], up_ref[rows, at], ((1,), (0,))
            )
            mixed = (normed + diff * weight).astype(jnp.bfloat16)
            if branch == 0:
                decay += halves_dot(mixed, decay_down_ref[:, at], ((1,), (1,)))
            else:
                mixed_ref[BRANCHES.index(branch), :, at] = mixed
        return decay

    decay = lax.fori_loop(0, strips, second, jnp.zeros(decay_ref.shape, jnp.float32))
    decay = jnp.tanh(decay)
    decay_ref[...] = decay
    log_ref[...] = base_ref[...] + halves_dot(decay, decay_up_ref[...], ((1,), (0,)))


def mix_forward(block_input, before, coeffs, norm, down, up, decay_down, decay_up, base):
    sequences, length, columns = block_input.shape
    heads, tokens = decay_up.shape[1], sequences * length
    args = (block_input, before, coeffs, norm, down, up, decay_down, decay_up, base)

    def rows(wide):
        return pl.BlockSpec((length, wide), lambda s: (s, 0))

    outs = [(down.shape[0], jnp.float32), (decay_up.shape[0], jnp.float32), (heads, jnp.float32)]
    return pl.pallas_call(
        mix_kernel,
        grid=(sequences,),
        in_specs=[
            pl.BlockSpec((1, length, columns), lambda s: (s, 0, 0)),
            pl.BlockSpec((1, 1, columns), lambda s: (s, 0, 0)),
        ]
        + [pl.BlockSpec(array.shape, lambda s: (0, 0)) for array in args[2:]],
        out_specs=[pl.BlockSpec((4, length, columns), lambda s: (0, s, 0))]
        + [rows(wide) for wide, _ in outs],
        out_shape=[jax.ShapeDtypeStruct((4, tokens, columns), jnp.bfloat16)]
        + [jax.ShapeDtypeStruct((tokens, wide), kind) for wide, kind in outs],
        compiler_params=pltpu.CompilerParams(vmem_limit_bytes=40 * 2**20),
        cost_estimate=pl.CostEstimate(
            flops=17 * 10**9, bytes_accessed=16 * 2**20, transcendentals=10**5
        ),
    )(*args)


def per_device(
    block_input,
    initial_state,
    norm_gains,
    norm_biases,
    mixing_coefficients,
    mix_down,
    mixing_up_weight,
    decay_down,
    decay_up,
    proj_weights,
    out_weight,
    time_decay,
    time_first,
    group_gain,
    group_bias,
    channel_key,
    channel_value,
    channel_recept,
    out_grad,
):
    blocks, place = lax.axis_size("seq"), lax.axis_index("seq")
    half = lax.axis_index("tp")
    sizes = (lax.axis_size("dp"), blocks)
    width = norm_gains.shape[1]
    heads_here, each = time_decay.shape
    head_size = initial_state.shape[-1]
    head_cols = heads_here * head_size
    ranks, decay_ranks = mix_down.shape[1], decay_down.shape[1]

    def narrow_rows(part):
        part = part.reshape(-1, heads_here * each)
        return jnp.pad(part, ((0, 0), (0, width - part.shape[1])))

    up_at = 16
    down_at = up_at + ranks
    decay_at = down_at + ranks
    narrow_at = decay_at + decay_ranks
    own_rows = jnp.concatenate(
        [
            norm_gains,
            norm_biases,
            mixing_coefficients,
            jnp.zeros((4, width), jnp.bfloat16),
            mixing_up_weight,
            mix_down.T,
            decay_down.T,
            narrow_rows(decay_up),
            narrow_rows(time_decay),
            narrow_rows(time_first),
            narrow_rows(group_gain),
            narrow_rows(group_bias),
            jnp.zeros((12, width), jnp.bfloat16),
        ]
    )
    spread_rows = spread_columns(own_rows, sizes, 1)
    channel = jnp.arange(head_cols)
    lane = (channel % head_size) // each * width + channel // head_size * each + channel % each
    choose = (jnp.arange(spread_rows.shape[1])[:, None] == lane[None, :]).astype(jnp.bfloat16)
    narrow_all = jnp.dot(
        spread_rows[narrow_at:], choose, preferred_element_type=jnp.float32
    )
    gains_all, biases_all = (spread_rows[k : k + 2].astype(jnp.float32) for k in (0, 2))
    shift_coefficient = spread_rows[4:12].astype(jnp.float32)
    lowrank_up = spread_rows[up_at:down_at]
    lowrank_down = spread_rows[down_at:decay_at]
    decay_projection = spread_rows[decay_at:narrow_at]
    lift_rows = narrow_all[:decay_ranks].astype(jnp.bfloat16)
    base_row, bonus, group_scale, group_shift = (
        narrow_all[decay_ranks + k : decay_ranks + k + 1] for k in range(4)
    )
    projections = lax.all_gather(proj_weights, ("dp", "seq"), axis=1, tiled=True)
    out_proj = lax.all_gather(out_weight, ("dp", "seq"), axis=1, tiled=True)
    seq_count, length, feature_columns = block_input.shape
    tokens = seq_count * length
    own_cols = channel_recept.shape[1]

    def both_halves(own):
        other = other_half(own)
        low = jnp.where(half == 0, own, other)
        high = jnp.where(half == 0, other, own)
        return jnp.concatenate([low, high], axis=-1)

    def own_half(rows):
        return lax.dynamic_slice_in_dim(rows, half * own_cols, own_cols, rows.ndim - 1)

    def half_sum(part):
        sent = lax.dynamic_slice_in_dim(part, (1 - half) * own_cols, own_cols, part.ndim - 1)
        return own_half(part) + other_half(sent.astype(jnp.bfloat16)).astype(jnp.float32)

    full_out = both_halves(out_grad)
    input_f = block_input.astype(jnp.float32)
    last_one = layer_norm(input_f[:, -1], gains_all[0], biases_all[0])
    preceding_first = from_behind(last_one.astype(jnp.bfloat16), "seq", 1)
    preceding_first = preceding_first.astype(jnp.float32)[:, None, :]
    norm_one = jnp.stack([gains_all[0], biases_all[0]])
    stacked, hidden_mixture, hidden_decay, log_flat = mix_forward(
        block_input,
        preceding_first,
        shift_coefficient,
        norm_one,
        lowrank_down,
        lowrank_up,
        decay_projection,
        lift_rows,
        base_row,
    )
    projected = jnp.einsum("ntd,nde->nte", stacked, projections, preferred_element_type=jnp.float32)
    recurrence = Recurrence(seq_count, length, head_cols)
    where_here = place.astype(jnp.int32).reshape(1)
    all_packed = lax.all_gather(recurrence.totals(projected, log_flat), "seq")
    inner, decayed = recurrence.inner(projected, log_flat, bonus)
    wkv, mixer_rows, state, decay_range = recurrence.join(
        where_here,
        inner,
        decayed,
        projected,
        all_packed,
        paired_states(initial_state),
        group_scale,
        group_shift,
    )
    mixer_in = mixer_rows.reshape(seq_count, length, head_cols)
    decay_range = decay_range[:, :2].reshape(seq_count, 2, heads_here, head_size)
    total_least = jnp.min(decay_range[:, 0], axis=-1)
    total_most = jnp.max(decay_range[:, 1], axis=-1)
    mixer_part = jnp.einsum("std,de->ste", mixer_in, out_proj, preferred_element_type=jnp.float32)
    residual = (
        input_f + mixer_part + other_half(mixer_part.astype(jnp.bfloat16)).astype(jnp.float32)
    )
    normed_two, norm_two_back = jax.vjp(layer_norm, residual, gains_all[1], biases_all[1])
    prev_two = from_behind(normed_two[:, -1, :].astype(jnp.bfloat16), "seq", 1).astype(jnp.float32)
    (chan_key, chan_recept), chan_back = jax.vjp(
        channel_mix, normed_two, prev_two, shift_coefficient
    )
    chan_key_b = chan_key.astype(jnp.bfloat16)
    chan_recept_b = chan_recept.astype(jnp.bfloat16)
    key_pre = jnp.einsum("std,df->stf", chan_key_b, channel_key, preferred_element_type=jnp.float32)
    hidden = jnp.square(jnp.maximum(key_pre, 0.0)).astype(jnp.bfloat16)
    value_part = jnp.einsum(
        "stf,fd->std", hidden, channel_value, preferred_element_type=jnp.float32
    )
    recept_pre = jnp.einsum(
        "std,de->ste", chan_recept_b, channel_recept, preferred_element_type=jnp.float32
    )
    kv_rows = half_sum(value_part)
    gate_chan = jax.nn.sigmoid(recept_pre)
    output = (own_half(residual) + gate_chan * kv_rows).astype(jnp.bfloat16)
    grad_out = out_grad.astype(jnp.float32)
    grad_value = (grad_out * gate_chan).astype(jnp.bfloat16)
    grad_recept = (grad_out * kv_rows * gate_chan * (1.0 - gate_chan)).astype(jnp.bfloat16)
    full_value = both_halves(grad_value)

    def weight_terms(left, right):
        return jnp.einsum(
            "td,tf->df",
            left.reshape(tokens, -1),
            right.reshape(tokens, -1),
            preferred_element_type=jnp.float32,
        ).astype(jnp.bfloat16)

    def scattered(whole):
        return lax.psum_scatter(whole, ("dp", "seq"), scatter_dimension=0, tiled=True).astype(
            jnp.float32
        )

    full_value, value_whole = lax.optimization_barrier(
        (full_value, weight_terms(full_value, hidden))
    )
    value_sum = scattered(value_whole)
    grad_hidden = jnp.einsum(
        "std,fd->stf", full_value, channel_value, preferred_element_type=jnp.float32
    )
    grad_key = (grad_hidden * 2.0 * jnp.maximum(key_pre, 0.0)).astype(jnp.bfloat16)
    part_key = jnp.einsum("stf,df->std", grad_key, channel_key, preferred_element_type=jnp.float32)
    part_recept = jnp.einsum(
        "ste,de->std", grad_recept, channel_recept, preferred_element_type=jnp.float32
    )
    part_normed_two, part_prev_two, grad_coeffs_chan = chan_back((part_key, part_recept))
    from_next_two = from_behind(for_sending(part_prev_two), "seq", -1).astype(jnp.float32)
    part_normed_two = part_normed_two.at[:, -1, :].add(from_next_two)
    sizes = (lax.axis_size("dp"), blocks)
    grad_key_rows = grad_key.reshape(tokens, -1)
    key_cut = grad_key_rows.shape[1] * 4 // 7
    key_whole = weight_terms(chan_key_b, grad_key_rows[:, :key_cut])
    grad_normed_two = part_normed_two + other_half(part_normed_two.astype(jnp.bfloat16)).astype(
        jnp.float32
    )
    grad_residual, grad_gain_two, grad_bias_two = norm_two_back(grad_normed_two)
    grad_residual = grad_residual + full_out.astype(jnp.float32)
    grad_residual, key_whole = lax.optimization_barrier((grad_residual, key_whole))
    key_sum = scattered(key_whole)
    grad_branch = grad_residual.astype(jnp.bfloat16)
    grad_mixer = jnp.einsum(
        "ste,de->std", grad_branch, out_proj, preferred_element_type=jnp.float32
    )
    grad_wkv, grad_gate, block_term, group_sums = recurrence.back_join(
        grad_mixer.reshape(tokens, head_cols), wkv, projected, decayed, group_scale, group_shift
    )
    all_terms = lax.all_gather(block_term, "seq")
    grad_wkv, value_sum = lax.optimization_barrier((grad_wkv, value_sum))
    grad_receive, near_key, near_value, running, bonus_sums = recurrence.back_inner(
        projected, log_flat, bonus, grad_wkv, state
    )
    grad_keys, grad_values, grad_log, start_pairs, rate_sums = recurrence.back_outer(
        where_here,
        projected,
        log_flat,
        near_key,
        near_value,
        running,
        state,
        all_packed,
        all_terms,
    )
    state_grad = single_states(start_pairs)

    grad_proj = jnp.stack([grad_receive, grad_keys, grad_values, grad_gate])
    part_block, edge, mix_sums, up_grad, down_grad, decay_down_grad, lift_grad = mix_back(
        block_input,
        preceding_first,
        grad_proj,
        grad_log,
        hidden_mixture,
        hidden_decay,
        projections,
        shift_coefficient,
        norm_one,
        lowrank_down,
        lowrank_up,
        decay_projection,
        lift_rows,
    )
    from_next_one = from_behind(edge[:, 0].astype(jnp.bfloat16), "seq", -1).astype(jnp.float32)
    _, last_back = jax.vjp(layer_norm, input_f[:, -1], gains_all[0], biases_all[0])
    part_last, gain_last, bias_last = last_back(from_next_one)
    part_block = part_block.at[:, -1].add(part_last)
    head_rows = jnp.concatenate(
        [
            lift_grad,
            jnp.sum(rate_sums[:, :1], axis=0),
            jnp.sum(bonus_sums[:, :1], axis=0),
            jnp.sum(group_sums[:, :2], axis=0),
            jnp.zeros((12, head_cols), jnp.float32),
        ]
    )
    head_rows = lax.dot_general(
        head_rows,
        choose.astype(jnp.float32),
        (((1,), (1,)), ((), ())),
        precision=lax.Precision.HIGHEST,
    )
    small_rows = jnp.concatenate(
        [
            jnp.stack([mix_sums[6] + gain_last, 0.5 * grad_gain_two]),
            jnp.stack([mix_sums[7] + bias_last, 0.5 * grad_bias_two]),
            mix_sums[:6],
            grad_coeffs_chan[6:],
            jnp.zeros((4, feature_columns), jnp.float32),
            up_grad,
            down_grad,
            decay_down_grad,
            head_rows,
        ]
    )
    half_block = half_sum(part_block)
    small_sums = sum_columns(small_rows)
    input_grad = own_half(grad_residual) + half_block
    *proj_sums, out_sum, recept_sum, key_rest = ring_sums(
        [(stacked, grad_proj, (branch,)) for branch in range(4)]
        + [
            (grad_branch.reshape(tokens, -1), mixer_in.reshape(tokens, -1), ()),
            (chan_recept_b.reshape(tokens, -1), grad_recept.reshape(tokens, -1), ()),
            (chan_key_b.reshape(tokens, -1), grad_key_rows[:, key_cut:], ()),
        ],
        sizes,
        0,
    )
    shared = small_sums[:narrow_at] + other_half(small_sums[:narrow_at])
    narrow = small_sums[narrow_at:, : heads_here * each]
    head_sums = [
        narrow[decay_ranks + k].reshape(heads_here, each) for k in range(4)
    ]
    return (
        output,
        input_grad,
        state_grad,
        shared[:2],
        shared[2:4],
        jnp.concatenate([shared[4:5], shared[6:12]], axis=0),
        shared[5:6],
        shared[down_at:decay_at].T,
        shared[up_at:down_at],
        shared[decay_at:].T,
        narrow[:decay_ranks].reshape(decay_ranks, heads_here, each),
        jnp.stack(proj_sums),
        out_sum.T,
        *head_sums,
        jnp.concatenate([key_sum, key_rest], axis=1),
        value_sum.T,
        recept_sum,
        total_least,
        total_most,
    )


def solution(mesh):
    return jax.shard_map(
        per_device,
        mesh=mesh,
        in_specs=(
            P("dp", "seq", None),
            P("dp", "tp", None, None),
            P(None, ("dp", "seq")),
            P(None, ("dp", "seq")),
            P(None, ("dp", "seq")),
            P(("dp", "seq"), None),
            P(None, ("dp", "seq")),
            P(("dp", "seq"), None),
            P(None, "tp", ("dp", "seq")),
            P(None, ("dp", "seq"), "tp"),
            P("tp", ("dp", "seq")),
            P("tp", ("dp", "seq")),
            P("tp", ("dp", "seq")),
            P("tp", ("dp", "seq")),
            P("tp", ("dp", "seq")),
            P(None, "tp"),
            P("tp", None),
            P(None, "tp"),
            P("dp", "seq", "tp"),
        ),
        out_specs=(
            P("dp", "seq", "tp"),
            P("dp", "seq", "tp"),
            P("dp", "tp", None, None),
            P(None, ("dp", "seq")),
            P(None, ("dp", "seq")),
            P(None, ("dp", "seq")),
            P(None, ("dp", "seq")),
            P(("dp", "seq"), None),
            P(None, ("dp", "seq")),
            P(("dp", "seq"), None),
            P(None, "tp", ("dp", "seq")),
            P(None, ("dp", "seq"), "tp"),
            P("tp", ("dp", "seq")),
            P("tp", ("dp", "seq")),
            P("tp", ("dp", "seq")),
            P("tp", ("dp", "seq")),
            P("tp", ("dp", "seq")),
            P(("dp", "seq"), "tp"),
            P("tp", ("dp", "seq")),
            P(("dp", "seq"), "tp"),
            P("dp", "tp"),
            P("dp", "tp"),
        ),
        check_vma=False,
    )
```

```python
import functools

import jax
import jax.numpy as jnp
from jax import lax
from jax.experimental import pallas as pl
from jax.experimental.pallas import tpu as pltpu
from jax.sharding import PartitionSpec as P

NORM_EPS = 1e-05
GROUP_EPS = 0.00064


def from_behind(block, axis, distance):
    devices = range(lax.axis_size(axis))
    route = [(i - distance, i) for i in devices if i - distance in devices]
    return lax.ppermute(block, axis, route)


def for_sending(array):

    def short(part):
        return part.astype(jnp.bfloat16) if part.dtype == jnp.float32 else part

    return jax.tree.map(short, array)


def layer_norm(values, scale_row, shift_row):
    mean_val = jnp.mean(values, axis=-1, keepdims=True)
    centered = values - mean_val
    variance = jnp.mean(centered * centered, axis=-1, keepdims=True)
    return centered * lax.rsqrt(variance + NORM_EPS) * scale_row + shift_row


def channel_mix(normalized_rows, preceding_row, shift_coefficient):
    earlier = jnp.concatenate([preceding_row[:, None, :], normalized_rows[:, :-1, :]], axis=1)
    shift_difference = earlier - normalized_rows
    return (
        normalized_rows + shift_difference * shift_coefficient[6],
        normalized_rows + shift_difference * shift_coefficient[7],
    )


WIDE = 256
PAIR = 128
EXTRA = 16


def halves_dot(left, right, dims):
    return lax.dot_general(
        left.astype(jnp.bfloat16),
        right.astype(jnp.bfloat16),
        (dims, ((), ())),
        preferred_element_type=jnp.float32,
    )


def exact_dot(ones, values):
    high = values.astype(jnp.bfloat16)
    rest = values - high.astype(jnp.float32)
    middle = rest.astype(jnp.bfloat16)
    low = (rest - middle.astype(jnp.float32)).astype(jnp.bfloat16)
    ones = ones.astype(jnp.bfloat16)
    dims = ((1,), (0,))
    return (
        halves_dot(ones, high, dims) + halves_dot(ones, middle, dims) + halves_dot(ones, low, dims)
    )


def iota(shape, dim):
    return lax.broadcasted_iota(jnp.int32, shape, dim)


def first_head(shape):
    return iota(shape, len(shape) - 1) < PAIR // 2


def compact(full):
    top, low = full[: PAIR // 2], full[PAIR // 2 :]
    return jnp.where(first_head(top.shape), top, low)


def spread(state):
    first = first_head(state.shape)
    return jnp.concatenate([jnp.where(first, state, 0.0), jnp.where(first, 0.0, state)], axis=0)


def head_sum(values):
    first = first_head(values.shape)
    a = jnp.sum(jnp.where(first, values, 0.0), axis=-1, keepdims=True)
    b = jnp.sum(jnp.where(first, 0.0, values), axis=-1, keepdims=True)
    return jnp.where(first, a, b)


def running_decay(log_rates):
    length = log_rates.shape[0]
    rates = -jnp.exp(log_rates)
    up_to = iota((length, length), 0) >= iota((length, length), 1)
    return rates, exact_dot(up_to.astype(jnp.float32), rates)


def two_parts(row):
    high = row.astype(jnp.bfloat16).astype(jnp.float32)
    return high, row - high


def totals_kernel(kv_ref, log_ref, packed_ref):
    for pair in range(WIDE // PAIR):
        lanes = slice(pair * PAIR, (pair + 1) * PAIR)
        keys, values = kv_ref[1, :, lanes], kv_ref[2, :, lanes]
        rates, total = running_decay(log_ref[:, lanes])
        length = rates.shape[0]
        final = total[length - 1 : length]
        state = compact(halves_dot(keys * jnp.exp(final - total), values, ((0,), (0,))))
        decay = jnp.exp(rates)
        rows = [
            *two_parts(jnp.exp(final)),
            *two_parts(jnp.min(decay, axis=0, keepdims=True)),
            *two_parts(jnp.max(decay, axis=0, keepdims=True)),
        ]
        row_at = iota((EXTRA, PAIR), 0)
        extra = jnp.zeros((EXTRA, PAIR), jnp.float32)
        for at, row in enumerate(rows):
            extra = jnp.where(row_at == at, row, extra)
        packed_ref[0, pair] = jnp.concatenate([state, extra], axis=0).astype(jnp.bfloat16)


def inner_scores(receive, keys, rates, total):
    length = receive.shape[0]
    before = total - rates
    middle = before[length // 2 : length // 2 + 1]
    up, down = jnp.exp(before - middle), jnp.exp(middle - total)
    rows, columns = receive * up, keys * down
    first = first_head(rows.shape)
    later = iota((length, length), 0) > iota((length, length), 1)
    columns = columns.astype(jnp.bfloat16)
    scores = [
        jnp.where(
            later, halves_dot(jnp.where(own, rows, 0.0), columns, ((1,), (1,))), 0.0
        ).astype(jnp.bfloat16)
        for own in (first, jnp.logical_not(first))
    ]
    return rows.astype(jnp.bfloat16), columns, scores, up, down, before


def heads_apply(left, right, side):
    first = first_head(right.shape)
    a = halves_dot(left[0], right, ((side,), (0,)))
    b = halves_dot(left[1], right, ((side,), (0,)))
    return jnp.where(first, a, b)


def inner_kernel(rkv_ref, log_ref, bonus_ref, inner_ref, decayed_ref):
    for pair in range(WIDE // PAIR):
        lanes = slice(pair * PAIR, (pair + 1) * PAIR)
        receive, keys, values = (rkv_ref[n, :, lanes] for n in range(3))
        rates, total = running_decay(log_ref[:, lanes])
        _, _, scores, _, _, before = inner_scores(receive, keys, rates, total)
        now = head_sum(receive * bonus_ref[:, lanes] * keys)
        inner_ref[:, lanes] = heads_apply(scores, values, 1) + now * values
        decayed_ref[:, lanes] = (receive * jnp.exp(before)).astype(jnp.bfloat16)


def block_decays(extra):
    blocks = extra.shape[0]
    flat = extra.astype(jnp.float32)
    columns = []
    for start in range(0, blocks, PAIR // EXTRA):
        some = flat[start : start + PAIR // EXTRA]
        some = some.reshape(some.shape[0] * EXTRA, PAIR)
        if some.shape[0] < PAIR:
            some = jnp.concatenate(
                [some, jnp.zeros((PAIR - some.shape[0], PAIR), jnp.float32)], axis=0
            )
        turned = some.T
        for k in range(min(PAIR // EXTRA, blocks - start)):
            both = turned[:, k * EXTRA : k * EXTRA + 1] + turned[:, k * EXTRA + 1 : k * EXTRA + 2]
            columns.append(compact(jnp.broadcast_to(both, (PAIR, PAIR))))
    return columns


def norm_heads(wkv, count):
    mean = head_sum(wkv) * (1.0 / count)
    centered = wkv - mean
    scale = lax.rsqrt(head_sum(centered * centered) * (1.0 / count) + GROUP_EPS)
    return centered * scale, scale


def join_kernel(
    place_ref, inner_ref, decayed_ref, gate_ref, packed_ref, start_ref, gain_ref, bias_ref, *outs
):
    wkv_ref, mixer_ref, state_ref, range_ref = outs
    blocks = packed_ref.shape[0]
    place = place_ref[0]
    for pair in range(WIDE // PAIR):
        lanes = slice(pair * PAIR, (pair + 1) * PAIR)
        state = jnp.concatenate([start_ref[0, 2 * pair], start_ref[0, 2 * pair + 1]], axis=1)
        extra = packed_ref[:, 0, pair, PAIR // 2 :, :]
        decays = block_decays(extra)
        extra = extra.astype(jnp.float32)
        range_ref[0, :, lanes] = put_rows(
            [
                jnp.min(extra[:, 2] + extra[:, 3], axis=0, keepdims=True),
                jnp.max(extra[:, 4] + extra[:, 5], axis=0, keepdims=True),
            ]
        )
        for k in range(blocks - 1):
            term = packed_ref[k, 0, pair, : PAIR // 2, :].astype(jnp.float32)
            state = jnp.where(k < place, decays[k] * state + term, state)
        state_ref[0, pair] = state
        wkv = inner_ref[:, lanes] + halves_dot(decayed_ref[:, lanes], spread(state), ((1,), (0,)))
        wkv_ref[:, lanes] = wkv
        normed, _ = norm_heads(wkv, PAIR // 2)
        normed = normed * gain_ref[:, lanes] + bias_ref[:, lanes]
        gate = gate_ref[0, :, lanes]
        mixer_ref[:, lanes] = (normed * gate * jax.nn.sigmoid(gate)).astype(jnp.bfloat16)


def put_rows(rows):
    row_at = iota((8, PAIR), 0)
    out = jnp.zeros((8, PAIR), jnp.float32)
    for at, row in enumerate(rows):
        out = jnp.where(row_at == at, row, out)
    return out


def back_join_kernel(grad_ref, wkv_ref, gate_ref, decayed_ref, gain_ref, bias_ref, *outs):
    grad_wkv_ref, grad_gate_ref, term_ref, sums_ref = outs
    for pair in range(WIDE // PAIR):
        lanes = slice(pair * PAIR, (pair + 1) * PAIR)
        grad, gate = grad_ref[:, lanes], gate_ref[0, :, lanes]
        gain = gain_ref[:, lanes]
        hat, scale = norm_heads(wkv_ref[:, lanes], PAIR // 2)
        sigmoid = jax.nn.sigmoid(gate)
        normed = hat * gain + bias_ref[:, lanes]
        grad_gate = grad * normed * sigmoid * (1.0 + gate * (1.0 - sigmoid))
        grad_gate_ref[:, lanes] = grad_gate.astype(jnp.bfloat16)
        grad_normed = grad * gate * sigmoid
        sums_ref[0, :, lanes] = put_rows(
            [
                jnp.sum(grad_normed * hat, axis=0, keepdims=True),
                jnp.sum(grad_normed, axis=0, keepdims=True),
            ]
        )
        q = grad_normed * gain
        each = 2.0 / PAIR
        grad_wkv = scale * (q - head_sum(q) * each - hat * (head_sum(q * hat) * each))
        grad_wkv_ref[:, lanes] = grad_wkv
        term_ref[0, pair] = compact(
            halves_dot(decayed_ref[:, lanes], grad_wkv, ((0,), (0,)))
        ).astype(jnp.bfloat16)


def back_inner_kernel(rkv_ref, log_ref, bonus_ref, grad_ref, state_ref, *outs):
    receive_ref, key_ref, value_ref, running_ref, sums_ref = outs
    for pair in range(WIDE // PAIR):
        lanes = slice(pair * PAIR, (pair + 1) * PAIR)
        receive, keys, values = (rkv_ref[n, :, lanes] for n in range(3))
        bonus, grad = bonus_ref[:, lanes], grad_ref[:, lanes]
        rates, total = running_decay(log_ref[:, lanes])
        rows, columns, scores, up, down, before = inner_scores(receive, keys, rates, total)
        length = receive.shape[0]
        first = first_head(values.shape)
        later = iota((length, length), 0) > iota((length, length), 1)
        low_values = values.astype(jnp.bfloat16)
        low_grad = grad.astype(jnp.bfloat16)
        grad_scores = [
            jnp.where(
                later, halves_dot(jnp.where(own, grad, 0.0), low_values, ((1,), (1,))), 0.0
            ).astype(jnp.bfloat16)
            for own in (first, jnp.logical_not(first))
        ]
        from_state = halves_dot(low_grad, spread(state_ref[0, pair]), ((1,), (1,)))
        far_receive = heads_apply(grad_scores, columns, 1) * up + jnp.exp(before) * from_state
        far_keys = heads_apply(grad_scores, rows, 0) * down
        meet = head_sum(grad * values)
        receive_ref[:, lanes] = (far_receive + bonus * keys * meet).astype(jnp.bfloat16)
        key_ref[:, lanes] = far_keys + bonus * receive * meet
        now = head_sum(receive * bonus * keys)
        value_ref[:, lanes] = heads_apply(scores, low_grad, 0) + now * grad
        moved = receive * far_receive
        moved = pltpu.roll(moved, length - 1, 0)
        moved = jnp.where(iota(moved.shape, 0) == length - 1, 0.0, moved)
        running_ref[:, lanes] = moved - keys * far_keys
        sums_ref[0, :, lanes] = put_rows([jnp.sum(receive * keys * meet, axis=0, keepdims=True)])


def back_outer_kernel(
    place_ref, kv_ref, log_ref, key_ref, value_ref, running_ref, state_ref, packed_ref, terms_ref, *outs
):
    grad_key_ref, grad_value_ref, grad_log_ref, start_ref, sums_ref = outs
    blocks = packed_ref.shape[0]
    place = place_ref[0]
    for pair in range(WIDE // PAIR):
        lanes = slice(pair * PAIR, (pair + 1) * PAIR)
        keys, values = kv_ref[1, :, lanes], kv_ref[2, :, lanes]
        rates, total = running_decay(log_ref[:, lanes])
        length = keys.shape[0]
        final = total[length - 1 : length]
        decays = block_decays(packed_ref[:, 0, pair, PAIR // 2 :, :])
        later = jnp.zeros((PAIR // 2, PAIR), jnp.float32)
        whole = jnp.zeros((PAIR // 2, PAIR), jnp.float32)
        for k in range(blocks - 1, -1, -1):
            term = terms_ref[k, 0, pair].astype(jnp.float32)
            later = jnp.where(k > place, decays[k] * later + term, later)
            whole = decays[k] * whole + term
        start_ref[0, 2 * pair] = whole[:, : PAIR // 2]
        start_ref[0, 2 * pair + 1] = whole[:, PAIR // 2 :]
        spread_later = spread(later).astype(jnp.bfloat16)
        fade = jnp.exp(final - total)
        far_keys = fade * halves_dot(values, spread_later, ((1,), (1,)))
        grad_key_ref[:, lanes] = (key_ref[:, lanes] + far_keys).astype(jnp.bfloat16)
        grad_value_ref[:, lanes] = (
            value_ref[:, lanes] + halves_dot(keys * fade, spread_later, ((1,), (0,)))
        ).astype(jnp.bfloat16)
        moved = keys * far_keys
        met = spread(state_ref[0, pair] * later)
        high, low = two_parts(met)
        ones = jnp.ones((8, PAIR), jnp.bfloat16)
        met_row = (halves_dot(ones, high, ((1,), (1,))) + halves_dot(ones, low, ((1,), (1,))))[:1]
        last = jnp.sum(moved, axis=0, keepdims=True) + jnp.exp(final) * met_row
        running = running_ref[:, lanes] - moved
        running = running + jnp.where(iota(running.shape, 0) == length - 1, last, 0.0)
        onward = iota((length, length), 0) <= iota((length, length), 1)
        grad_log = exact_dot(onward.astype(jnp.float32), running) * rates
        grad_log_ref[:, lanes] = grad_log
        sums_ref[0, :, lanes] = put_rows([jnp.sum(grad_log, axis=0, keepdims=True)])


class Recurrence:
    def __init__(self, sequences, length, columns):
        self.sequences, self.length, self.columns = sequences, length, columns
        self.grid = (sequences, columns // WIDE)
        self.pairs = columns // PAIR
        self.tokens = pl.BlockSpec((length, WIDE), lambda s, p: (s, p))
        self.row = pl.BlockSpec((1, WIDE), lambda s, p: (0, p))
        self.stack = pl.BlockSpec((3, length, WIDE), lambda s, p: (0, s, p))
        self.gate = pl.BlockSpec((1, length, WIDE), lambda s, p: (3, s, p))
        self.state = pl.BlockSpec((1, WIDE // PAIR, PAIR // 2, PAIR), lambda s, p: (s, p, 0, 0))
        self.heads = pl.BlockSpec(
            (1, 2 * WIDE // PAIR, PAIR // 2, PAIR // 2), lambda s, p: (s, p, 0, 0)
        )
        self.sums = pl.BlockSpec((1, 8, WIDE), lambda s, p: (s, 0, p))
        self.place = pl.BlockSpec(memory_space=pltpu.SMEM)

    def packed(self, blocks=None):
        rows = PAIR // 2 + EXTRA
        if blocks is None:
            return pl.BlockSpec((1, WIDE // PAIR, rows, PAIR), lambda s, p: (s, p, 0, 0))
        return pl.BlockSpec((blocks, 1, WIDE // PAIR, rows, PAIR), lambda s, p: (0, s, p, 0, 0))

    def terms(self, blocks):
        return pl.BlockSpec(
            (blocks, 1, WIDE // PAIR, PAIR // 2, PAIR), lambda s, p: (0, s, p, 0, 0)
        )

    def token_shape(self, kind):
        return jax.ShapeDtypeStruct((self.sequences * self.length, self.columns), kind)

    def state_shape(self, kind, rows=PAIR // 2):
        return jax.ShapeDtypeStruct((self.sequences, self.pairs, rows, PAIR), kind)

    def sums_shape(self):
        return jax.ShapeDtypeStruct((self.sequences, 8, self.columns), jnp.float32)

    def call(self, kernel, ins, outs, args, flops):
        size = sum(arg.size * arg.dtype.itemsize for arg in args)
        return pl.pallas_call(
            kernel,
            grid=self.grid,
            in_specs=ins,
            out_specs=[spec for spec, _ in outs],
            out_shape=[shape for _, shape in outs],
            compiler_params=pltpu.CompilerParams(vmem_limit_bytes=40 * 2**20),
            cost_estimate=pl.CostEstimate(
                flops=flops, bytes_accessed=size, transcendentals=6 * args[0].size
            ),
        )(*args)

    def totals(self, projected, log_rows):
        outs = [(self.packed(), self.state_shape(jnp.bfloat16, PAIR // 2 + EXTRA))]
        return self.call(
            totals_kernel, [self.stack, self.tokens], outs, (projected, log_rows), 10**9
        )[0]

    def inner(self, projected, log_rows, bonus):
        outs = [
            (self.tokens, self.token_shape(jnp.float32)),
            (self.tokens, self.token_shape(jnp.bfloat16)),
        ]
        ins = [self.stack, self.tokens, self.row]
        return self.call(inner_kernel, ins, outs, (projected, log_rows, bonus), 2 * 10**9)

    def join(self, place, inner, decayed, projected, packed, start, gain, bias):
        ins = [
            self.place,
            self.tokens,
            self.tokens,
            self.gate,
            self.packed(packed.shape[0]),
            self.heads,
            self.row,
            self.row,
        ]
        outs = [
            (self.tokens, self.token_shape(jnp.float32)),
            (self.tokens, self.token_shape(jnp.bfloat16)),
            (self.state, self.state_shape(jnp.float32)),
            (self.sums, self.sums_shape()),
        ]
        args = (place, inner, decayed, projected, packed, start, gain, bias)
        return self.call(join_kernel, ins, outs, args, 10**9)

    def back_join(self, grad, wkv, projected, decayed, gain, bias):
        ins = [self.tokens, self.tokens, self.gate, self.tokens, self.row, self.row]
        outs = [
            (self.tokens, self.token_shape(jnp.float32)),
            (self.tokens, self.token_shape(jnp.bfloat16)),
            (self.state, self.state_shape(jnp.bfloat16)),
            (self.sums, self.sums_shape()),
        ]
        args = (grad, wkv, projected, decayed, gain, bias)
        return self.call(back_join_kernel, ins, outs, args, 10**9)

    def back_inner(self, projected, log_rows, bonus, grad, state):
        ins = [self.stack, self.tokens, self.row, self.tokens, self.state]
        outs = [
            (self.tokens, self.token_shape(jnp.bfloat16)),
            (self.tokens, self.token_shape(jnp.float32)),
            (self.tokens, self.token_shape(jnp.float32)),
            (self.tokens, self.token_shape(jnp.float32)),
            (self.sums, self.sums_shape()),
        ]
        args = (projected, log_rows, bonus, grad, state)
        return self.call(back_inner_kernel, ins, outs, args, 4 * 10**9)

    def back_outer(self, place, projected, log_rows, keys, values, running, state, packed, terms):
        blocks = packed.shape[0]
        ins = [
            self.place,
            self.stack,
            self.tokens,
            self.tokens,
            self.tokens,
            self.tokens,
            self.state,
            self.packed(blocks),
            self.terms(blocks),
        ]
        outs = [
            (self.tokens, self.token_shape(jnp.bfloat16)),
            (self.tokens, self.token_shape(jnp.bfloat16)),
            (self.tokens, self.token_shape(jnp.float32)),
            (
                self.heads,
                jax.ShapeDtypeStruct(
                    (self.sequences, 2 * self.pairs, PAIR // 2, PAIR // 2), jnp.float32
                ),
            ),
            (self.sums, self.sums_shape()),
        ]
        args = (place, projected, log_rows, keys, values, running, state, packed, terms)
        return self.call(back_outer_kernel, ins, outs, args, 3 * 10**9)


BRANCHES = (3, 1, 2, 4)
STRIP = 512


def mix_back_kernel(
    x_ref,
    before_ref,
    grad_ref,
    log_ref,
    hidden_ref,
    decay_ref,
    proj_ref,
    coeff_ref,
    norm_ref,
    down_ref,
    up_ref,
    decay_down_ref,
    decay_up_ref,
    block_ref,
    edge_ref,
    all_ref,
    grad_decay_up_ref,
    hat_ref,
    grad_diff_ref,
    grad_all_ref,
):
    together, length, columns = x_ref.shape
    tokens = together * length
    ranks = up_ref.shape[0] // 5
    up_rows, decay_rows = up_ref.shape[0], decay_down_ref.shape[0]
    sums_ref = all_ref.at[0:8]
    grad_up_ref = all_ref.at[16 : 16 + up_rows]
    grad_down_ref = all_ref.at[16 + up_rows : 16 + 2 * up_rows]
    grad_decay_down_ref = all_ref.at[16 + 2 * up_rows : 16 + 2 * up_rows + decay_rows]
    strips = columns // STRIP
    low = jnp.bfloat16

    @pl.when(pl.program_id(0) == 0)
    def _():
        for ref in (all_ref, grad_decay_up_ref):
            ref[...] = jnp.zeros_like(ref)

    x = x_ref[...].reshape(tokens, columns).astype(jnp.float32)
    mean = jnp.mean(x, axis=-1, keepdims=True)
    variance = jnp.mean((x - mean) * (x - mean), axis=-1, keepdims=True)
    scale = lax.rsqrt(variance + NORM_EPS)
    hidden, hidden_decay = hidden_ref[...], decay_ref[...]
    low_hidden, low_decay = hidden.astype(low), hidden_decay.astype(low)
    grad_log = log_ref[...].astype(low)
    grad_decay = halves_dot(grad_log, decay_up_ref[...], ((1,), (1,)))
    grad_decay = grad_decay * (1.0 - hidden_decay * hidden_decay)
    low_grad_decay = grad_decay.astype(low)
    grad_decay_up_ref[...] += halves_dot(low_decay, grad_log, ((0,), (0,)))

    def strip_of(strip):
        return pl.ds(pl.multiple_of(strip * STRIP, STRIP), STRIP)

    def normed_and_diff(at, hat):
        normed = hat * norm_ref[0:1, at] + norm_ref[1:2, at]
        earlier = pltpu.roll(normed, 1, 0)
        for k in range(together):
            earlier = jnp.where(
                iota(normed.shape, 0) == k * length, before_ref[k, :, at], earlier
            )
        return normed, earlier - normed

    def first(strip, grad_pre):
        at = strip_of(strip)
        hat = (x_ref[:, :, at].reshape(tokens, STRIP).astype(jnp.float32) - mean) * scale
        hat_ref[:, at] = hat
        normed, diff = normed_and_diff(at, hat)
        grad_diff = jnp.zeros_like(diff)
        grad_all = jnp.zeros_like(diff)
        parts = []
        for branch in range(5):
            rows = slice(branch * ranks, (branch + 1) * ranks)
            up = up_ref[rows, at]
            weight = coeff_ref[1 + branch : 2 + branch, at] + halves_dot(
                low_hidden[:, rows], up, ((1,), (0,))
            )
            if branch == 0:
                mixed = normed + diff * weight
                grad_decay_down_ref[:, at] += halves_dot(low_grad_decay, mixed, ((0,), (0,)))
                grad = halves_dot(low_grad_decay, decay_down_ref[:, at], ((1,), (0,)))
            else:
                n = BRANCHES.index(branch)
                grad = halves_dot(grad_ref[n], proj_ref[n, at, :], ((1,), (1,)))
            grad_all += grad
            grad_diff += grad * weight
            moved = grad * diff
            sums_ref[1 + branch : 2 + branch, at] += jnp.sum(moved, axis=0, keepdims=True)
            moved = moved.astype(low)
            grad_up_ref[rows, at] += halves_dot(low_hidden[:, rows], moved, ((0,), (0,)))
            parts.append(halves_dot(moved, up, ((1,), (1,))))
        grad_diff_ref[:, at] = grad_diff
        grad_all_ref[:, at] = grad_all
        return grad_pre + jnp.concatenate(parts, axis=1)

    grad_pre = lax.fori_loop(0, strips, first, jnp.zeros(hidden.shape, jnp.float32))
    grad_pre = (grad_pre * (1.0 - hidden * hidden)).astype(low)

    def second(strip, carry):
        total, against = carry
        at = strip_of(strip)
        hat = hat_ref[:, at]
        normed, diff = normed_and_diff(at, hat)
        coeff = coeff_ref[0:1, at]
        grad_base = halves_dot(grad_pre, down_ref[:, at], ((1,), (0,)))
        grad_down_ref[:, at] += halves_dot(grad_pre, normed + diff * coeff, ((0,), (0,)))
        sums_ref[0:1, at] += jnp.sum(grad_base * diff, axis=0, keepdims=True)
        grad_diff = grad_diff_ref[:, at] + grad_base * coeff
        onward = pltpu.roll(grad_diff, tokens - 1, 0)
        for k in range(together):
            edge_ref[k, :, at] = grad_diff[k * length : k * length + 1]
            onward = jnp.where(iota(onward.shape, 0) == (k + 1) * length - 1, 0.0, onward)
        grad = grad_base + grad_all_ref[:, at] - grad_diff + onward
        sums_ref[6:7, at] += jnp.sum(grad * hat, axis=0, keepdims=True)
        sums_ref[7:8, at] += jnp.sum(grad, axis=0, keepdims=True)
        q = grad * norm_ref[0:1, at]
        grad_all_ref[:, at] = q
        total += jnp.sum(q, axis=-1, keepdims=True)
        against += jnp.sum(q * hat, axis=-1, keepdims=True)
        return total, against

    zero = jnp.zeros((tokens, 1), jnp.float32)
    total, against = lax.fori_loop(0, strips, second, (zero, zero))
    total, against = total * (1.0 / columns), against * (1.0 / columns)

    def third(strip, carry):
        at = strip_of(strip)
        block = scale * (grad_all_ref[:, at] - total - hat_ref[:, at] * against)
        block_ref[:, :, at] = block.reshape(together, length, STRIP)
        return carry

    lax.fori_loop(0, strips, third, 0)


def mix_back(
    block_input,
    before,
    grad_proj,
    grad_log,
    hidden,
    hidden_decay,
    projections,
    coeffs,
    norm,
    down,
    up,
    decay_down,
    decay_up,
    sum_rows,
):
    sequences, length, columns = block_input.shape
    heads = grad_proj.shape[-1]
    ranks, decay_ranks = up.shape[0], decay_up.shape[0]

    def whole(array):
        return pl.BlockSpec(array.shape, lambda s: (0,) * array.ndim)

    def kept(shape):
        return pl.BlockSpec(shape, lambda s: (0, 0)), jax.ShapeDtypeStruct(shape, jnp.float32)

    together = 2 - sequences % 2
    tokens = together * length
    block = pl.BlockSpec((together, length, columns), lambda s: (s, 0, 0))
    edge = pl.BlockSpec((together, 1, columns), lambda s: (s, 0, 0))
    outs = [
        (block, jax.ShapeDtypeStruct(block_input.shape, jnp.float32)),
        (edge, jax.ShapeDtypeStruct((sequences, 1, columns), jnp.float32)),
        kept((sum_rows, columns)),
        kept((decay_ranks, heads)),
    ]
    args = (
        block_input,
        before,
        grad_proj,
        grad_log,
        hidden,
        hidden_decay,
        projections,
        coeffs,
        norm,
        down,
        up,
        decay_down,
        decay_up,
    )
    return pl.pallas_call(
        mix_back_kernel,
        grid=(sequences // together,),
        in_specs=[
            block,
            edge,
            pl.BlockSpec((4, tokens, heads), lambda s: (0, s, 0)),
            pl.BlockSpec((tokens, heads), lambda s: (s, 0)),
            pl.BlockSpec((tokens, hidden.shape[1]), lambda s: (s, 0)),
            pl.BlockSpec((tokens, decay_ranks), lambda s: (s, 0)),
            pl.BlockSpec(projections.shape, lambda s: (0, 0, 0), pipeline_mode=pl.Buffered(1)),
        ]
        + [whole(array) for array in args[7:]],
        out_specs=[spec for spec, _ in outs],
        out_shape=[shape for _, shape in outs],
        scratch_shapes=[pltpu.VMEM((tokens, columns), jnp.float32)] * 3,
        compiler_params=pltpu.CompilerParams(vmem_limit_bytes=58 * 2**20),
        cost_estimate=pl.CostEstimate(
            flops=10**10, bytes_accessed=40 * 2**20, transcendentals=0
        ),
    )(*args)


def other_half(block):
    return lax.ppermute(block, "tp", [(0, 1), (1, 0)])


CORES = 2


def ring_places(dp_size, seq_size):
    per_row = seq_size // CORES
    count = dp_size * per_row

    def chip(position):
        position = lax.rem(position + 2 * count, count)
        row = lax.div(position, per_row)
        column = lax.rem(position, per_row)
        column = jnp.where(lax.rem(row, 2) == 0, column, per_row - 1 - column)
        return row, column

    def own():
        row, column = lax.axis_index("dp"), lax.div(lax.axis_index("seq"), CORES)
        return row * per_row + jnp.where(lax.rem(row, 2) == 0, column, per_row - 1 - column)

    return count, chip, own


def cut_rings(widths, rings):
    each = sum(widths) // rings
    runs, product, column = [], 0, 0
    for _ in range(rings):
        run, left = [], each
        while left:
            take = min(left, widths[product] - column)
            run.append((product, column, take))
            left, column = left - take, column + take
            if column == widths[product]:
                product, column = product + 1, 0
        runs.append(run)
    return runs


def ring_kernel(dp_size, seq_size, rows, widths, runs, places, operands, *refs):
    products = len(widths)
    lefts = [(refs[left], lead) for left, _, lead in places]
    rights = [(None if right is None else refs[right], lead) for _, right, lead in places]
    sent_ref, received_ref = refs[operands - 1], refs[operands + products]
    totals, refs = refs[operands : operands + products], refs[operands + products + 1 :]
    rings = len(runs)
    mine, pair_out, pair_in, ring_out, ring_in = [
        refs[k * rings : (k + 1) * rings] for k in range(5)
    ]
    pair_send, pair_recv, pair_free, ring_send, ring_recv, ring_free, half_send, half_recv = refs[
        5 * rings :
    ]
    count, chip, own = ring_places(dp_size, seq_size)
    position, core = own(), lax.rem(lax.axis_index("seq"), CORES)

    def device(place, which):
        row, column = chip(place)
        return {"dp": row, "seq": column * CORES + which}

    sibling = device(position, 1 - core)
    after, before = device(position + 1, core), device(position - 1, core)
    barrier = pltpu.get_barrier_semaphore()
    partner = {"tp": 1 - lax.axis_index("tp")}
    for other in (sibling, after, before, partner):
        pl.semaphore_signal(barrier, inc=1, device_id=other, device_id_type=pl.DeviceIdType.MESH)
    pl.semaphore_wait(barrier, 4)
    halves = pltpu.make_async_remote_copy(
        src_ref=sent_ref,
        dst_ref=received_ref,
        send_sem=half_send,
        recv_sem=half_recv,
        device_id=partner,
        device_id_type=pl.DeviceIdType.MESH,
    )
    halves.start()

    def pair_copy(ring):
        return pltpu.make_async_remote_copy(
            src_ref=pair_out[ring],
            dst_ref=pair_in[ring],
            send_sem=pair_send.at[ring],
            recv_sem=pair_recv.at[ring],
            device_id=sibling,
            device_id_type=pl.DeviceIdType.MESH,
        )

    def ring_copy(ring, slot):
        return pltpu.make_async_remote_copy(
            src_ref=ring_out[ring].at[slot],
            dst_ref=ring_in[ring].at[slot],
            send_sem=ring_send.at[ring, slot],
            recv_sem=ring_recv.at[ring, slot],
            device_id=after if ring % 2 == 0 else before,
            device_id_type=pl.DeviceIdType.MESH,
        )

    def part(ring, place, which, put):
        row, column = chip(place)
        start = (row * seq_size + column * CORES + which) * rows
        start = pl.multiple_of(start, rows)
        at = 0
        for product, first, wide in runs[ring]:
            ref, lead = lefts[product]
            if rights[product][0] is None:
                if rows % 128 == 0:
                    put(at, wide, ref[pl.ds(first, wide), pl.ds(start, rows)].T)
                else:
                    put(at, wide, ref[pl.ds(start, rows), pl.ds(first, wide)])
                at += wide
                continue
            if rows % 128 == 0:
                left = ref[(*lead, slice(None), pl.ds(start, rows))]
            else:
                left = ref[(*lead, pl.ds(start, rows), slice(None))]
            ref, lead = rights[product]
            right = ref[(*lead, slice(None), pl.ds(first, wide))]
            put(
                at,
                wide,
                lax.dot_general(
                    left,
                    right,
                    (((0 if rows % 128 == 0 else 1,), (0,)), ((), ())),
                    preferred_element_type=jnp.float32,
                ),
            )
            at += wide

    def turn(step, carry):
        slot = lax.rem(step, 2)
        last = 1 - slot
        for ring in range(rings):
            place = position - 1 - step if ring % 2 == 0 else position + 1 + step

            @pl.when(step >= 1)
            def _():
                pair_copy(ring).wait_send()

            def put_out(at, wide, value):
                pair_out[ring][:, at : at + wide] = value.astype(jnp.bfloat16)

            part(ring, place, 1 - core, put_out)

            @pl.when(step >= 1)
            def _():
                pl.semaphore_wait(pair_free.at[ring], 1)

            pair_copy(ring).start()

            def put_mine(at, wide, value):
                mine[ring][:, at : at + wide] = value

            part(ring, place, core, put_mine)
        for ring in range(rings):
            source = before if ring % 2 == 0 else after
            pair_copy(ring).wait_recv()

            @pl.when(step == 0)
            def _():
                ring_out[ring][slot] = (
                    mine[ring][...] + pair_in[ring][...].astype(jnp.float32)
                ).astype(jnp.bfloat16)

            @pl.when(step >= 1)
            def _():
                ring_copy(ring, last).wait_recv()

            @pl.when(jnp.logical_and(step >= 1, step < count - 1))
            def _():
                @pl.when(step >= 2)
                def _():
                    ring_copy(ring, slot).wait_send()

                ring_out[ring][slot] = (
                    mine[ring][...]
                    + pair_in[ring][...].astype(jnp.float32)
                    + ring_in[ring][last].astype(jnp.float32)
                ).astype(jnp.bfloat16)

            @pl.when(step == count - 1)
            def _():
                at = 0
                for product, first, wide in runs[ring]:
                    totals[product][:, first : first + wide] = (
                        mine[ring][:, at : at + wide]
                        + pair_in[ring][:, at : at + wide].astype(jnp.float32)
                        + ring_in[ring][last, :, at : at + wide].astype(jnp.float32)
                    )
                    at += wide

            @pl.when(step < count - 1)
            def _():
                @pl.when(step >= 2)
                def _():
                    pl.semaphore_wait(ring_free.at[ring], 1)

                ring_copy(ring, slot).start()
                pl.semaphore_signal(
                    pair_free.at[ring],
                    inc=1,
                    device_id=sibling,
                    device_id_type=pl.DeviceIdType.MESH,
                )

            @pl.when(jnp.logical_and(step >= 1, step < count - 2))
            def _():
                pl.semaphore_signal(
                    ring_free.at[ring],
                    inc=1,
                    device_id=source,
                    device_id_type=pl.DeviceIdType.MESH,
                )

        return carry

    lax.fori_loop(0, count, turn, 0)
    for ring in range(rings):
        pair_copy(ring).wait_send()
        for step in (count - 3, count - 2):
            ring_copy(ring, step % 2).wait_send()
    halves.wait()


def ring_sums(pairs, given, sent, sizes, collective_id):
    dp_size, seq_size = sizes
    rows = pairs[0][0].shape[-1] // (dp_size * seq_size)
    tokens = pairs[0][1].shape[-2]
    operands, known, places = [], {}, []

    def place_of(array, turned):
        if id(array) not in known:
            known[id(array)] = len(operands)
            operands.append(jnp.swapaxes(array, -1, -2) if turned else array)
        return known[id(array)]

    for left, right, lead in pairs:
        places.append((place_of(left, rows % 128 != 0), place_of(right, False), lead))
    places.append((place_of(given, rows % 128 != 0), None, ()))
    operands.append(sent)
    widths = [right.shape[-1] for _, right, _ in pairs] + [given.shape[0]]
    rings = 4
    runs = cut_rings(widths, rings)
    each = sum(widths) // rings
    low = jnp.bfloat16
    return pl.pallas_call(
        functools.partial(
            ring_kernel, dp_size, seq_size, rows, widths, runs, places, len(operands)
        ),
        out_shape=[jax.ShapeDtypeStruct((rows, wide), jnp.float32) for wide in widths]
        + [jax.ShapeDtypeStruct(sent.shape, sent.dtype)],
        in_specs=[pl.BlockSpec(memory_space=pltpu.VMEM)] * len(operands),
        out_specs=[pl.BlockSpec(memory_space=pltpu.VMEM)] * (len(widths) + 1),
        scratch_shapes=[pltpu.VMEM((rows, each), jnp.float32)] * rings
        + [pltpu.VMEM((rows, each), low)] * (2 * rings)
        + [pltpu.VMEM((2, rows, each), low)] * (2 * rings)
        + [
            pltpu.SemaphoreType.DMA((rings,)),
            pltpu.SemaphoreType.DMA((rings,)),
            pltpu.SemaphoreType.REGULAR((rings,)),
            pltpu.SemaphoreType.DMA((rings, 2)),
            pltpu.SemaphoreType.DMA((rings, 2)),
            pltpu.SemaphoreType.REGULAR((rings,)),
            pltpu.SemaphoreType.DMA(()),
            pltpu.SemaphoreType.DMA(()),
        ],
        compiler_params=pltpu.CompilerParams(
            collective_id=collective_id, has_side_effects=True, vmem_limit_bytes=60 * 2**20
        ),
        cost_estimate=pl.CostEstimate(
            flops=2 * tokens * rows * dp_size * seq_size * sum(widths),
            bytes_accessed=2 * tokens * (2048 * len(pairs) + sum(widths)),
            transcendentals=0,
        ),
    )(*operands)


def gather_kernel(
    dp_size,
    seq_size,
    small_ref,
    proj_ref,
    out_ref,
    small_all,
    proj_all,
    out_all,
    keep,
    send,
    recv,
    pair_send,
    pair_recv,
):
    width = small_ref.shape[1]
    count, chip, own = ring_places(dp_size, seq_size)
    position, core = own(), lax.rem(lax.axis_index("seq"), CORES)
    far = count // 2
    hops = [(far, far - 1), (far, far - 1), (far - 1, far), (far - 1, far)]
    halfway = proj_ref.shape[0] // 2

    def device(place, which):
        row, column = chip(place)
        return {"dp": row, "seq": column * CORES + which}

    def regions(place, which):
        row, column = chip(place)
        start = (row * seq_size + column * CORES + which) * width
        at = pl.ds(pl.multiple_of(start, width), width)
        return [
            small_all.at[:, at],
            proj_all.at[:halfway, at, :],
            proj_all.at[halfway:, at, :],
            out_all.at[:, at],
        ]

    sources = [small_ref, proj_ref.at[:halfway], proj_ref.at[halfway:], out_ref]
    sibling = device(position, 1 - core)
    ways = [device(position + 1, core), device(position - 1, core)]
    barrier = pltpu.get_barrier_semaphore()
    for other in [sibling] + ways:
        pl.semaphore_signal(barrier, inc=1, device_id=other, device_id_type=pl.DeviceIdType.MESH)
    pl.semaphore_wait(barrier, 3)

    def place_of(way, hop):
        return position - hop if way == 0 else position + hop

    def onward(part, way, hop):
        at = regions(place_of(way, hop - 1), core)[part]
        return pltpu.make_async_remote_copy(
            src_ref=sources[part] if hop == 1 else at,
            dst_ref=at,
            send_sem=send.at[part, way, hop - 1],
            recv_sem=recv.at[part, way, hop - 1],
            device_id=ways[way],
            device_id_type=pl.DeviceIdType.MESH,
        )

    def across(part, way, hop):
        at = regions(place_of(way, hop), core)[part]
        return pltpu.make_async_remote_copy(
            src_ref=sources[part] if hop == 0 else at,
            dst_ref=at,
            send_sem=pair_send.at[part, way, hop],
            recv_sem=pair_recv.at[part, way, hop],
            device_id=sibling,
            device_id_type=pl.DeviceIdType.MESH,
        )

    parts = range(len(sources))
    kept = []
    for part in parts:
        for way in range(2):
            onward(part, way, 1).start()
        across(part, 0, 0).start()
        copy = pltpu.make_async_copy(
            sources[part], regions(position, core)[part], keep.at[part]
        )
        copy.start()
        kept.append(copy)
    for hop in range(1, far + 1):
        for part in parts:
            for way in range(2):
                if hop <= hops[part][way]:
                    onward(part, way, hop).wait_recv()
                    if hop < hops[part][way]:
                        onward(part, way, hop + 1).start()
                    across(part, way, hop).start()
    for part in parts:
        kept[part].wait()
        across(part, 0, 0).wait()
        for way in range(2):
            for hop in range(1, hops[part][way] + 1):
                onward(part, way, hop).wait_send()
                across(part, way, hop).wait()


def gather_weights(small, proj, out, sizes, collective_id):
    if small.shape[1] % 128:
        return (
            lax.all_gather(small, ("dp", "seq"), axis=1, tiled=True),
            lax.all_gather(proj, ("dp", "seq"), axis=1, tiled=True),
            lax.all_gather(out, ("dp", "seq"), axis=1, tiled=True),
        )
    dp_size, seq_size = sizes
    every = dp_size * seq_size
    far = every // CORES // 2
    rows, width = small.shape
    shapes = [
        (rows, width * every),
        (proj.shape[0], width * every, proj.shape[2]),
        (out.shape[0], width * every),
    ]
    return pl.pallas_call(
        functools.partial(gather_kernel, dp_size, seq_size),
        out_shape=[jax.ShapeDtypeStruct(shape, small.dtype) for shape in shapes],
        in_specs=[pl.BlockSpec(memory_space=pl.ANY)] * 3,
        out_specs=[pl.BlockSpec(memory_space=pl.ANY)] * 3,
        scratch_shapes=[pltpu.SemaphoreType.DMA((4,))]
        + [pltpu.SemaphoreType.DMA((4, 2, far))] * 2
        + [pltpu.SemaphoreType.DMA((4, 2, far + 1))] * 2,
        compiler_params=pltpu.CompilerParams(collective_id=collective_id, has_side_effects=True),
    )(small, proj, out)


def mix_kernel(
    x_ref,
    before_ref,
    coeff_ref,
    norm_ref,
    down_ref,
    up_ref,
    decay_down_ref,
    decay_up_ref,
    base_ref,
    mixed_ref,
    hidden_ref,
    decay_ref,
    log_ref,
):
    length, columns = x_ref.shape[1:]
    ranks = up_ref.shape[0] // 5
    strips = columns // STRIP
    x = x_ref[0].astype(jnp.float32)
    mean = jnp.mean(x, axis=-1, keepdims=True)
    variance = jnp.mean((x - mean) * (x - mean), axis=-1, keepdims=True)
    scale = lax.rsqrt(variance + NORM_EPS)

    def normed_and_diff(strip):
        at = pl.ds(pl.multiple_of(strip * STRIP, STRIP), STRIP)
        hat = (x_ref[0, :, at].astype(jnp.float32) - mean) * scale
        normed = hat * norm_ref[0:1, at] + norm_ref[1:2, at]
        earlier = pltpu.roll(normed, 1, 0)
        earlier = jnp.where(iota(normed.shape, 0) == 0, before_ref[0, :, at], earlier)
        return at, normed, earlier - normed

    def first(strip, hidden):
        at, normed, diff = normed_and_diff(strip)
        return hidden + halves_dot(normed + diff * coeff_ref[0:1, at], down_ref[:, at], ((1,), (1,)))

    hidden = lax.fori_loop(0, strips, first, jnp.zeros(hidden_ref.shape, jnp.float32))
    hidden = jnp.tanh(hidden)
    hidden_ref[...] = hidden
    hidden = hidden.astype(jnp.bfloat16)

    def second(strip, decay):
        at, normed, diff = normed_and_diff(strip)
        for branch in range(5):
            rows = slice(branch * ranks, (branch + 1) * ranks)
            weight = coeff_ref[1 + branch : 2 + branch, at] + halves_dot(
                hidden[:, rows], up_ref[rows, at], ((1,), (0,))
            )
            mixed = (normed + diff * weight).astype(jnp.bfloat16)
            if branch == 0:
                decay += halves_dot(mixed, decay_down_ref[:, at], ((1,), (1,)))
            else:
                mixed_ref[BRANCHES.index(branch), :, at] = mixed
        return decay

    decay = lax.fori_loop(0, strips, second, jnp.zeros(decay_ref.shape, jnp.float32))
    decay = jnp.tanh(decay)
    decay_ref[...] = decay
    log_ref[...] = base_ref[...] + halves_dot(decay, decay_up_ref[...], ((1,), (0,)))


def mix_forward(block_input, before, coeffs, norm, down, up, decay_down, decay_up, base):
    sequences, length, columns = block_input.shape
    heads, tokens = decay_up.shape[1], sequences * length
    args = (block_input, before, coeffs, norm, down, up, decay_down, decay_up, base)

    def rows(wide):
        return pl.BlockSpec((length, wide), lambda s: (s, 0))

    outs = [(down.shape[0], jnp.float32), (decay_up.shape[0], jnp.float32), (heads, jnp.float32)]
    return pl.pallas_call(
        mix_kernel,
        grid=(sequences,),
        in_specs=[
            pl.BlockSpec((1, length, columns), lambda s: (s, 0, 0)),
            pl.BlockSpec((1, 1, columns), lambda s: (s, 0, 0)),
        ]
        + [pl.BlockSpec(array.shape, lambda s: (0, 0)) for array in args[2:]],
        out_specs=[pl.BlockSpec((4, length, columns), lambda s: (0, s, 0))]
        + [rows(wide) for wide, _ in outs],
        out_shape=[jax.ShapeDtypeStruct((4, tokens, columns), jnp.bfloat16)]
        + [jax.ShapeDtypeStruct((tokens, wide), kind) for wide, kind in outs],
        compiler_params=pltpu.CompilerParams(vmem_limit_bytes=40 * 2**20),
        cost_estimate=pl.CostEstimate(
            flops=2 * 10**9, bytes_accessed=16 * 2**20, transcendentals=10**5
        ),
    )(*args)


def per_device(
    block_input,
    initial_state,
    norm_gains,
    norm_biases,
    mixing_coefficients,
    mix_down,
    mixing_up_weight,
    decay_down,
    decay_up,
    proj_weights,
    out_weight,
    time_decay,
    time_first,
    group_gain,
    group_bias,
    channel_key,
    channel_value,
    channel_recept,
    out_grad,
):
    blocks, place = lax.axis_size("seq"), lax.axis_index("seq")
    half = lax.axis_index("tp")
    sizes = (lax.axis_size("dp"), blocks)
    width = norm_gains.shape[1]
    heads_here, each = time_decay.shape
    head_size = initial_state.shape[-1]
    head_cols = heads_here * head_size
    ranks, decay_ranks = mix_down.shape[1], decay_down.shape[1]

    def narrow_rows(part):
        part = part.reshape(-1, heads_here * each)
        return jnp.pad(part, ((0, 0), (0, width - part.shape[1])))

    up_at = 16
    down_at = up_at + ranks
    decay_at = down_at + ranks
    narrow_at = decay_at + decay_ranks
    top_rows = jnp.concatenate(
        [norm_gains, norm_biases, mixing_coefficients, jnp.zeros((4, width), jnp.bfloat16)]
    )
    low_rows = jnp.concatenate(
        [
            narrow_rows(time_decay),
            narrow_rows(time_first),
            narrow_rows(group_gain),
            narrow_rows(group_bias),
            jnp.zeros((12, width), jnp.bfloat16),
        ]
    )
    top_rows, low_rows = lax.optimization_barrier((top_rows, low_rows))
    own_rows = jnp.concatenate(
        [
            top_rows,
            mixing_up_weight,
            mix_down.T,
            decay_down.T,
            narrow_rows(decay_up),
            low_rows,
        ]
    )
    spread_rows, projections, out_proj = gather_weights(
        own_rows, proj_weights, out_weight, sizes, 1
    )
    channel = jnp.arange(head_cols)
    lane = (channel % head_size) // each * width + channel // head_size * each + channel % each
    choose = (jnp.arange(spread_rows.shape[1])[:, None] == lane[None, :]).astype(jnp.bfloat16)
    narrow_all = jnp.dot(
        spread_rows[narrow_at:], choose, preferred_element_type=jnp.float32
    )
    gains_all, biases_all = (spread_rows[k : k + 2].astype(jnp.float32) for k in (0, 2))
    shift_coefficient = spread_rows[4:12].astype(jnp.float32)
    lowrank_up = spread_rows[up_at:down_at]
    lowrank_down = spread_rows[down_at:decay_at]
    decay_projection = spread_rows[decay_at:narrow_at]
    lift_rows = narrow_all[:decay_ranks].astype(jnp.bfloat16)
    base_row, bonus, group_scale, group_shift = (
        narrow_all[decay_ranks + k : decay_ranks + k + 1] for k in range(4)
    )
    seq_count, length, feature_columns = block_input.shape
    tokens = seq_count * length
    own_cols = channel_recept.shape[1]

    def both_halves(own):
        other = other_half(own)
        low = jnp.where(half == 0, own, other)
        high = jnp.where(half == 0, other, own)
        return jnp.concatenate([low, high], axis=-1)

    def own_half(rows):
        return lax.dynamic_slice_in_dim(rows, half * own_cols, own_cols, rows.ndim - 1)

    def add_last(rows, last):
        at_last = jnp.arange(length)[None, :, None] == length - 1
        return rows + jnp.where(at_last, last[:, None, :], 0.0)

    full_out = both_halves(out_grad)
    last_input = block_input[:, -1].astype(jnp.float32)
    last_one = layer_norm(last_input, gains_all[0], biases_all[0])
    preceding_first = from_behind(last_one.astype(jnp.bfloat16), "seq", 1)
    preceding_first = preceding_first.astype(jnp.float32)[:, None, :]
    norm_one = jnp.stack([gains_all[0], biases_all[0]])
    stacked, hidden_mixture, hidden_decay, log_flat = mix_forward(
        block_input,
        preceding_first,
        shift_coefficient,
        norm_one,
        lowrank_down,
        lowrank_up,
        decay_projection,
        lift_rows,
        base_row,
    )
    projected = jnp.einsum("ntd,nde->nte", stacked, projections, preferred_element_type=jnp.float32)
    recurrence = Recurrence(seq_count, length, head_cols)
    where_here = place.astype(jnp.int32).reshape(1)
    all_packed = lax.all_gather(recurrence.totals(projected, log_flat), "seq")
    inner, decayed = recurrence.inner(projected, log_flat, bonus)
    wkv, mixer_rows, state, decay_range = recurrence.join(
        where_here,
        inner,
        decayed,
        projected,
        all_packed,
        initial_state,
        group_scale,
        group_shift,
    )
    mixer_in = mixer_rows.reshape(seq_count, length, head_cols)
    decay_range = decay_range[:, :2].reshape(seq_count, 2, heads_here, head_size)
    total_least = jnp.min(decay_range[:, 0], axis=-1)
    total_most = jnp.max(decay_range[:, 1], axis=-1)
    mixer_part = jnp.einsum("std,de->ste", mixer_in, out_proj, preferred_element_type=jnp.float32)
    late_input, mixer_part = lax.optimization_barrier((block_input, mixer_part))
    residual = (
        late_input.astype(jnp.float32) + mixer_part + other_half(mixer_part.astype(jnp.bfloat16)).astype(jnp.float32)
    )
    normed_two, norm_two_back = jax.vjp(layer_norm, residual, gains_all[1], biases_all[1])
    prev_two = from_behind(normed_two[:, -1, :].astype(jnp.bfloat16), "seq", 1).astype(jnp.float32)
    (chan_key, chan_recept), chan_back = jax.vjp(
        channel_mix, normed_two, prev_two, shift_coefficient
    )
    chan_key_b = chan_key.astype(jnp.bfloat16)
    chan_recept_b = chan_recept.astype(jnp.bfloat16)
    key_pre = jnp.einsum("std,df->stf", chan_key_b, channel_key, preferred_element_type=jnp.float32)
    hidden = jnp.square(jnp.maximum(key_pre, 0.0)).astype(jnp.bfloat16)
    own_value, sent_value = (
        lax.dynamic_slice_in_dim(channel_value, which * own_cols, own_cols, 1)
        for which in (half, 1 - half)
    )
    sent_part = jnp.einsum("stf,fd->std", hidden, sent_value, preferred_element_type=jnp.float32)
    other_part = other_half(sent_part.astype(jnp.bfloat16)).astype(jnp.float32)
    own_part = jnp.einsum("stf,fd->std", hidden, own_value, preferred_element_type=jnp.float32)
    recept_pre = jnp.einsum(
        "std,de->ste", chan_recept_b, channel_recept, preferred_element_type=jnp.float32
    )
    own_part, recept_pre = lax.optimization_barrier((own_part, recept_pre))
    kv_rows = own_part + other_part
    gate_chan = jax.nn.sigmoid(recept_pre)
    output = (own_half(residual) + gate_chan * kv_rows).astype(jnp.bfloat16)
    grad_out = out_grad.astype(jnp.float32)
    grad_value = (grad_out * gate_chan).astype(jnp.bfloat16)
    grad_recept = (grad_out * kv_rows * gate_chan * (1.0 - gate_chan)).astype(jnp.bfloat16)
    full_value = both_halves(grad_value)

    def weight_terms(left, right):
        return jnp.einsum(
            "td,tf->df",
            left.reshape(tokens, -1),
            right.reshape(tokens, -1),
            preferred_element_type=jnp.float32,
        ).astype(jnp.bfloat16)

    def scattered(whole):
        return lax.psum_scatter(whole, ("dp", "seq"), scatter_dimension=0, tiled=True).astype(
            jnp.float32
        )

    full_value, value_whole = lax.optimization_barrier(
        (full_value, weight_terms(full_value, hidden))
    )
    value_sum = scattered(value_whole)
    grad_hidden = jnp.einsum(
        "std,fd->stf", full_value, channel_value, preferred_element_type=jnp.float32
    )
    grad_key = (grad_hidden * 2.0 * jnp.maximum(key_pre, 0.0)).astype(jnp.bfloat16)
    part_key = jnp.einsum("stf,df->std", grad_key, channel_key, preferred_element_type=jnp.float32)
    part_recept = jnp.einsum(
        "ste,de->std", grad_recept, channel_recept, preferred_element_type=jnp.float32
    )
    part_normed_two, part_prev_two, grad_coeffs_chan = chan_back((part_key, part_recept))
    from_next_two = from_behind(for_sending(part_prev_two), "seq", -1).astype(jnp.float32)
    part_normed_two = add_last(part_normed_two, from_next_two)
    sizes = (lax.axis_size("dp"), blocks)
    grad_key_rows = grad_key.reshape(tokens, -1)
    key_cut = grad_key_rows.shape[1] * 5 // 7
    key_whole = weight_terms(chan_key_b, grad_key_rows[:, :key_cut])
    grad_normed_two = part_normed_two + other_half(part_normed_two.astype(jnp.bfloat16)).astype(
        jnp.float32
    )
    grad_residual, grad_gain_two, grad_bias_two = norm_two_back(grad_normed_two)
    grad_residual = grad_residual + full_out.astype(jnp.float32)
    grad_residual, key_whole = lax.optimization_barrier((grad_residual, key_whole))
    grad_branch = grad_residual.astype(jnp.bfloat16)
    grad_mixer = jnp.einsum(
        "ste,de->std", grad_branch, out_proj, preferred_element_type=jnp.float32
    )
    grad_wkv, grad_gate, block_term, group_sums = recurrence.back_join(
        grad_mixer.reshape(tokens, head_cols), wkv, projected, decayed, group_scale, group_shift
    )
    all_terms = lax.all_gather(block_term, "seq")
    grad_wkv, value_sum, key_whole = lax.optimization_barrier((grad_wkv, value_sum, key_whole))
    key_sum = scattered(key_whole)
    grad_receive, near_key, near_value, running, bonus_sums = recurrence.back_inner(
        projected, log_flat, bonus, grad_wkv, state
    )
    grad_keys, grad_values, grad_log, state_grad, rate_sums = recurrence.back_outer(
        where_here,
        projected,
        log_flat,
        near_key,
        near_value,
        running,
        state,
        all_packed,
        all_terms,
    )

    grad_proj = jnp.stack([grad_receive, grad_keys, grad_values, grad_gate])
    part_block, edge, small_rows, lift_grad = mix_back(
        block_input,
        preceding_first,
        grad_proj,
        grad_log,
        hidden_mixture,
        hidden_decay,
        projections,
        shift_coefficient,
        norm_one,
        lowrank_down,
        lowrank_up,
        decay_projection,
        lift_rows,
        narrow_at + 112,
    )
    from_next_one = from_behind(edge[:, 0].astype(jnp.bfloat16), "seq", -1).astype(jnp.float32)
    _, last_back = jax.vjp(layer_norm, last_input, gains_all[0], biases_all[0])
    part_last, gain_last, bias_last = last_back(from_next_one)
    part_block = add_last(part_block, part_last)
    head_rows = jnp.concatenate(
        [
            lift_grad,
            jnp.sum(rate_sums[:, :1], axis=0),
            jnp.sum(bonus_sums[:, :1], axis=0),
            jnp.sum(group_sums[:, :2], axis=0),
            jnp.zeros((12, head_cols), jnp.float32),
        ]
    )
    thirds = []
    for _ in range(3):
        thirds.append(head_rows.astype(jnp.bfloat16))
        head_rows = head_rows - lax.optimization_barrier(thirds[-1]).astype(jnp.float32)
    head_rows = jnp.sum(
        lax.dot_general(
            jnp.stack(thirds),
            choose,
            (((2,), (1,)), ((), ())),
            preferred_element_type=jnp.float32,
        ),
        axis=0,
    )
    other_rows = jnp.concatenate(
        [
            grad_coeffs_chan[6:],
            jnp.stack([0.5 * grad_gain_two, 0.5 * grad_bias_two, gain_last, bias_last]),
            jnp.zeros((2, feature_columns), jnp.float32),
        ]
    )
    small_rows = lax.dynamic_update_slice(small_rows, other_rows, (8, 0))
    small_rows = lax.dynamic_update_slice(small_rows, head_rows, (narrow_at, 0))
    sent_block = lax.dynamic_slice_in_dim(part_block, (1 - half) * own_cols, own_cols, 2)
    *proj_sums, out_sum, recept_sum, key_rest, small_sums, other_block = ring_sums(
        [(stacked, grad_proj, (branch,)) for branch in range(4)]
        + [
            (grad_branch.reshape(tokens, -1), mixer_in.reshape(tokens, -1), ()),
            (chan_recept_b.reshape(tokens, -1), grad_recept.reshape(tokens, -1), ()),
            (chan_key_b.reshape(tokens, -1), grad_key_rows[:, key_cut:], ()),
        ],
        small_rows,
        sent_block.astype(jnp.bfloat16),
        sizes,
        0,
    )
    small_sums = small_sums.T
    input_grad = own_half(grad_residual) + own_half(part_block) + other_block.astype(jnp.float32)
    shared = small_sums[:narrow_at] + other_half(small_sums[:narrow_at])
    narrow = small_sums[narrow_at:, : heads_here * each]
    head_sums = [
        narrow[decay_ranks + k].reshape(heads_here, each) for k in range(4)
    ]
    return (
        output,
        input_grad,
        state_grad,
        jnp.stack([shared[6] + shared[12], shared[10]]),
        jnp.stack([shared[7] + shared[13], shared[11]]),
        jnp.concatenate([shared[:1], shared[2:6], shared[8:10]], axis=0),
        shared[1:2],
        shared[down_at:decay_at].T,
        shared[up_at:down_at],
        shared[decay_at:].T,
        narrow[:decay_ranks].reshape(decay_ranks, heads_here, each),
        jnp.stack(proj_sums),
        out_sum.T,
        *head_sums,
        jnp.concatenate([key_sum, key_rest], axis=1),
        value_sum.T,
        recept_sum,
        total_least,
        total_most,
    )


def solution(mesh):
    return jax.shard_map(
        per_device,
        mesh=mesh,
        in_specs=(
            P("dp", "seq", None),
            P("dp", "tp", None, None),
            P(None, ("dp", "seq")),
            P(None, ("dp", "seq")),
            P(None, ("dp", "seq")),
            P(("dp", "seq"), None),
            P(None, ("dp", "seq")),
            P(("dp", "seq"), None),
            P(None, "tp", ("dp", "seq")),
            P(None, ("dp", "seq"), "tp"),
            P("tp", ("dp", "seq")),
            P("tp", ("dp", "seq")),
            P("tp", ("dp", "seq")),
            P("tp", ("dp", "seq")),
            P("tp", ("dp", "seq")),
            P(None, "tp"),
            P("tp", None),
            P(None, "tp"),
            P("dp", "seq", "tp"),
        ),
        out_specs=(
            P("dp", "seq", "tp"),
            P("dp", "seq", "tp"),
            P("dp", "tp", None, None),
            P(None, ("dp", "seq")),
            P(None, ("dp", "seq")),
            P(None, ("dp", "seq")),
            P(None, ("dp", "seq")),
            P(("dp", "seq"), None),
            P(None, ("dp", "seq")),
            P(("dp", "seq"), None),
            P(None, "tp", ("dp", "seq")),
            P(None, ("dp", "seq"), "tp"),
            P("tp", ("dp", "seq")),
            P("tp", ("dp", "seq")),
            P("tp", ("dp", "seq")),
            P("tp", ("dp", "seq")),
            P("tp", ("dp", "seq")),
            P(("dp", "seq"), "tp"),
            P("tp", ("dp", "seq")),
            P(("dp", "seq"), "tp"),
            P("dp", "tp"),
            P("dp", "tp"),
        ),
        check_vma=False,
    )
```

```python
import functools

import jax
import jax.numpy as jnp
from jax import lax
from jax.experimental import pallas as pl
from jax.experimental.pallas import tpu as pltpu
from jax.sharding import PartitionSpec as P

NORM_EPS = 1e-05
GROUP_EPS = 0.00064


def from_behind(block, axis, distance):
    devices = range(lax.axis_size(axis))
    route = [(i - distance, i) for i in devices if i - distance in devices]
    return lax.ppermute(block, axis, route)


def for_sending(array):

    def short(part):
        return part.astype(jnp.bfloat16) if part.dtype == jnp.float32 else part

    return jax.tree.map(short, array)


def layer_norm(values, scale_row, shift_row):
    mean_val = jnp.mean(values, axis=-1, keepdims=True)
    centered = values - mean_val
    variance = jnp.mean(centered * centered, axis=-1, keepdims=True)
    return centered * lax.rsqrt(variance + NORM_EPS) * scale_row + shift_row


def channel_mix(normalized_rows, preceding_row, shift_coefficient):
    earlier = jnp.concatenate([preceding_row[:, None, :], normalized_rows[:, :-1, :]], axis=1)
    shift_difference = earlier - normalized_rows
    return (
        normalized_rows + shift_difference * shift_coefficient[6],
        normalized_rows + shift_difference * shift_coefficient[7],
    )


WIDE = 256
PAIR = 128
EXTRA = 16


def halves_dot(left, right, dims):
    return lax.dot_general(
        left.astype(jnp.bfloat16),
        right.astype(jnp.bfloat16),
        (dims, ((), ())),
        preferred_element_type=jnp.float32,
    )


def exact_dot(ones, values):
    high = values.astype(jnp.bfloat16)
    rest = values - high.astype(jnp.float32)
    middle = rest.astype(jnp.bfloat16)
    low = (rest - middle.astype(jnp.float32)).astype(jnp.bfloat16)
    ones = ones.astype(jnp.bfloat16)
    dims = ((1,), (0,))
    return (
        halves_dot(ones, high, dims) + halves_dot(ones, middle, dims) + halves_dot(ones, low, dims)
    )


def iota(shape, dim):
    return lax.broadcasted_iota(jnp.int32, shape, dim)


def first_head(shape):
    return iota(shape, len(shape) - 1) < PAIR // 2


def compact(full):
    top, low = full[: PAIR // 2], full[PAIR // 2 :]
    return jnp.where(first_head(top.shape), top, low)


def spread(state):
    first = first_head(state.shape)
    return jnp.concatenate([jnp.where(first, state, 0.0), jnp.where(first, 0.0, state)], axis=0)


def head_sum(values):
    first = first_head(values.shape)
    a = jnp.sum(jnp.where(first, values, 0.0), axis=-1, keepdims=True)
    b = jnp.sum(jnp.where(first, 0.0, values), axis=-1, keepdims=True)
    return jnp.where(first, a, b)


def running_decay(log_rates):
    length = log_rates.shape[0]
    rates = -jnp.exp(log_rates)
    up_to = iota((length, length), 0) >= iota((length, length), 1)
    return rates, exact_dot(up_to.astype(jnp.float32), rates)


def two_parts(row):
    high = row.astype(jnp.bfloat16).astype(jnp.float32)
    return high, row - high


def totals_kernel(kv_ref, log_ref, packed_ref):
    for pair in range(WIDE // PAIR):
        lanes = slice(pair * PAIR, (pair + 1) * PAIR)
        keys, values = kv_ref[1, :, lanes], kv_ref[2, :, lanes]
        rates, total = running_decay(log_ref[:, lanes])
        length = rates.shape[0]
        final = total[length - 1 : length]
        state = compact(halves_dot(keys * jnp.exp(final - total), values, ((0,), (0,))))
        decay = jnp.exp(rates)
        rows = [
            *two_parts(jnp.exp(final)),
            *two_parts(jnp.min(decay, axis=0, keepdims=True)),
            *two_parts(jnp.max(decay, axis=0, keepdims=True)),
        ]
        row_at = iota((EXTRA, PAIR), 0)
        extra = jnp.zeros((EXTRA, PAIR), jnp.float32)
        for at, row in enumerate(rows):
            extra = jnp.where(row_at == at, row, extra)
        packed_ref[0, pair] = jnp.concatenate([state, extra], axis=0).astype(jnp.bfloat16)


def inner_scores(receive, keys, rates, total):
    length = receive.shape[0]
    before = total - rates
    middle = before[length // 2 : length // 2 + 1]
    up, down = jnp.exp(before - middle), jnp.exp(middle - total)
    rows, columns = receive * up, keys * down
    first = first_head(rows.shape)
    later = iota((length, length), 0) > iota((length, length), 1)
    columns = columns.astype(jnp.bfloat16)
    scores = [
        jnp.where(
            later, halves_dot(jnp.where(own, rows, 0.0), columns, ((1,), (1,))), 0.0
        ).astype(jnp.bfloat16)
        for own in (first, jnp.logical_not(first))
    ]
    return rows.astype(jnp.bfloat16), columns, scores, up, down, before


def heads_apply(left, right, side):
    first = first_head(right.shape)
    a = halves_dot(left[0], right, ((side,), (0,)))
    b = halves_dot(left[1], right, ((side,), (0,)))
    return jnp.where(first, a, b)


def inner_kernel(rkv_ref, log_ref, bonus_ref, inner_ref, decayed_ref):
    for pair in range(WIDE // PAIR):
        lanes = slice(pair * PAIR, (pair + 1) * PAIR)
        receive, keys, values = (rkv_ref[n, :, lanes] for n in range(3))
        rates, total = running_decay(log_ref[:, lanes])
        _, _, scores, _, _, before = inner_scores(receive, keys, rates, total)
        now = head_sum(receive * bonus_ref[:, lanes] * keys)
        inner_ref[:, lanes] = heads_apply(scores, values, 1) + now * values
        decayed_ref[:, lanes] = (receive * jnp.exp(before)).astype(jnp.bfloat16)


def block_decays(extra):
    blocks = extra.shape[0]
    flat = extra.astype(jnp.float32)
    columns = []
    for start in range(0, blocks, PAIR // EXTRA):
        some = flat[start : start + PAIR // EXTRA]
        some = some.reshape(some.shape[0] * EXTRA, PAIR)
        if some.shape[0] < PAIR:
            some = jnp.concatenate(
                [some, jnp.zeros((PAIR - some.shape[0], PAIR), jnp.float32)], axis=0
            )
        turned = some.T
        for k in range(min(PAIR // EXTRA, blocks - start)):
            both = turned[:, k * EXTRA : k * EXTRA + 1] + turned[:, k * EXTRA + 1 : k * EXTRA + 2]
            columns.append(compact(jnp.broadcast_to(both, (PAIR, PAIR))))
    return columns


def norm_heads(wkv, count):
    mean = head_sum(wkv) * (1.0 / count)
    centered = wkv - mean
    scale = lax.rsqrt(head_sum(centered * centered) * (1.0 / count) + GROUP_EPS)
    return centered * scale, scale


def join_kernel(
    place_ref, inner_ref, decayed_ref, gate_ref, packed_ref, start_ref, gain_ref, bias_ref, *outs
):
    wkv_ref, mixer_ref, state_ref, range_ref = outs
    blocks = packed_ref.shape[0]
    place = place_ref[0]
    for pair in range(WIDE // PAIR):
        lanes = slice(pair * PAIR, (pair + 1) * PAIR)
        state = jnp.concatenate([start_ref[0, 2 * pair], start_ref[0, 2 * pair + 1]], axis=1)
        extra = packed_ref[:, 0, pair, PAIR // 2 :, :]
        decays = block_decays(extra)
        extra = extra.astype(jnp.float32)
        range_ref[0, :, lanes] = put_rows(
            [
                jnp.min(extra[:, 2] + extra[:, 3], axis=0, keepdims=True),
                jnp.max(extra[:, 4] + extra[:, 5], axis=0, keepdims=True),
            ]
        )
        for k in range(blocks - 1):
            term = packed_ref[k, 0, pair, : PAIR // 2, :].astype(jnp.float32)
            state = jnp.where(k < place, decays[k] * state + term, state)
        state_ref[0, pair] = state
        wkv = inner_ref[:, lanes] + halves_dot(decayed_ref[:, lanes], spread(state), ((1,), (0,)))
        wkv_ref[:, lanes] = wkv
        normed, _ = norm_heads(wkv, PAIR // 2)
        normed = normed * gain_ref[:, lanes] + bias_ref[:, lanes]
        gate = gate_ref[0, :, lanes]
        mixer_ref[:, lanes] = (normed * gate * jax.nn.sigmoid(gate)).astype(jnp.bfloat16)


def put_rows(rows):
    row_at = iota((8, PAIR), 0)
    out = jnp.zeros((8, PAIR), jnp.float32)
    for at, row in enumerate(rows):
        out = jnp.where(row_at == at, row, out)
    return out


def back_join_kernel(grad_ref, wkv_ref, gate_ref, decayed_ref, gain_ref, bias_ref, *outs):
    grad_wkv_ref, grad_gate_ref, term_ref, sums_ref = outs
    for pair in range(WIDE // PAIR):
        lanes = slice(pair * PAIR, (pair + 1) * PAIR)
        grad, gate = grad_ref[:, lanes], gate_ref[0, :, lanes]
        gain = gain_ref[:, lanes]
        hat, scale = norm_heads(wkv_ref[:, lanes], PAIR // 2)
        sigmoid = jax.nn.sigmoid(gate)
        normed = hat * gain + bias_ref[:, lanes]
        grad_gate = grad * normed * sigmoid * (1.0 + gate * (1.0 - sigmoid))
        grad_gate_ref[:, lanes] = grad_gate.astype(jnp.bfloat16)
        grad_normed = grad * gate * sigmoid
        sums_ref[0, :, lanes] = put_rows(
            [
                jnp.sum(grad_normed * hat, axis=0, keepdims=True),
                jnp.sum(grad_normed, axis=0, keepdims=True),
            ]
        )
        q = grad_normed * gain
        each = 2.0 / PAIR
        grad_wkv = scale * (q - head_sum(q) * each - hat * (head_sum(q * hat) * each))
        grad_wkv_ref[:, lanes] = grad_wkv
        term_ref[0, pair] = compact(
            halves_dot(decayed_ref[:, lanes], grad_wkv, ((0,), (0,)))
        ).astype(jnp.bfloat16)


def back_inner_kernel(rkv_ref, log_ref, bonus_ref, grad_ref, state_ref, *outs):
    receive_ref, key_ref, value_ref, running_ref, sums_ref = outs
    for pair in range(WIDE // PAIR):
        lanes = slice(pair * PAIR, (pair + 1) * PAIR)
        receive, keys, values = (rkv_ref[n, :, lanes] for n in range(3))
        bonus, grad = bonus_ref[:, lanes], grad_ref[:, lanes]
        rates, total = running_decay(log_ref[:, lanes])
        rows, columns, scores, up, down, before = inner_scores(receive, keys, rates, total)
        length = receive.shape[0]
        first = first_head(values.shape)
        later = iota((length, length), 0) > iota((length, length), 1)
        low_values = values.astype(jnp.bfloat16)
        low_grad = grad.astype(jnp.bfloat16)
        grad_scores = [
            jnp.where(
                later, halves_dot(jnp.where(own, grad, 0.0), low_values, ((1,), (1,))), 0.0
            ).astype(jnp.bfloat16)
            for own in (first, jnp.logical_not(first))
        ]
        from_state = halves_dot(low_grad, spread(state_ref[0, pair]), ((1,), (1,)))
        far_receive = heads_apply(grad_scores, columns, 1) * up + jnp.exp(before) * from_state
        far_keys = heads_apply(grad_scores, rows, 0) * down
        meet = head_sum(grad * values)
        receive_ref[:, lanes] = (far_receive + bonus * keys * meet).astype(jnp.bfloat16)
        key_ref[:, lanes] = far_keys + bonus * receive * meet
        now = head_sum(receive * bonus * keys)
        value_ref[:, lanes] = heads_apply(scores, low_grad, 0) + now * grad
        moved = receive * far_receive
        moved = pltpu.roll(moved, length - 1, 0)
        moved = jnp.where(iota(moved.shape, 0) == length - 1, 0.0, moved)
        running_ref[:, lanes] = moved - keys * far_keys
        sums_ref[0, :, lanes] = put_rows([jnp.sum(receive * keys * meet, axis=0, keepdims=True)])


def back_outer_kernel(
    place_ref, kv_ref, log_ref, key_ref, value_ref, running_ref, state_ref, packed_ref, terms_ref, *outs
):
    grad_key_ref, grad_value_ref, grad_log_ref, start_ref, sums_ref = outs
    blocks = packed_ref.shape[0]
    place = place_ref[0]
    for pair in range(WIDE // PAIR):
        lanes = slice(pair * PAIR, (pair + 1) * PAIR)
        keys, values = kv_ref[1, :, lanes], kv_ref[2, :, lanes]
        rates, total = running_decay(log_ref[:, lanes])
        length = keys.shape[0]
        final = total[length - 1 : length]
        decays = block_decays(packed_ref[:, 0, pair, PAIR // 2 :, :])
        later = jnp.zeros((PAIR // 2, PAIR), jnp.float32)
        whole = jnp.zeros((PAIR // 2, PAIR), jnp.float32)
        for k in range(blocks - 1, -1, -1):
            term = terms_ref[k, 0, pair].astype(jnp.float32)
            later = jnp.where(k > place, decays[k] * later + term, later)
            whole = decays[k] * whole + term
        start_ref[0, 2 * pair] = whole[:, : PAIR // 2]
        start_ref[0, 2 * pair + 1] = whole[:, PAIR // 2 :]
        spread_later = spread(later).astype(jnp.bfloat16)
        fade = jnp.exp(final - total)
        far_keys = fade * halves_dot(values, spread_later, ((1,), (1,)))
        grad_key_ref[:, lanes] = (key_ref[:, lanes] + far_keys).astype(jnp.bfloat16)
        grad_value_ref[:, lanes] = (
            value_ref[:, lanes] + halves_dot(keys * fade, spread_later, ((1,), (0,)))
        ).astype(jnp.bfloat16)
        moved = keys * far_keys
        met = spread(state_ref[0, pair] * later)
        high, low = two_parts(met)
        ones = jnp.ones((8, PAIR), jnp.bfloat16)
        met_row = (halves_dot(ones, high, ((1,), (1,))) + halves_dot(ones, low, ((1,), (1,))))[:1]
        last = jnp.sum(moved, axis=0, keepdims=True) + jnp.exp(final) * met_row
        running = running_ref[:, lanes] - moved
        running = running + jnp.where(iota(running.shape, 0) == length - 1, last, 0.0)
        onward = iota((length, length), 0) <= iota((length, length), 1)
        grad_log = exact_dot(onward.astype(jnp.float32), running) * rates
        grad_log_ref[:, lanes] = grad_log
        sums_ref[0, :, lanes] = put_rows([jnp.sum(grad_log, axis=0, keepdims=True)])


class Recurrence:
    def __init__(self, sequences, length, columns):
        self.sequences, self.length, self.columns = sequences, length, columns
        self.grid = (sequences, columns // WIDE)
        self.pairs = columns // PAIR
        self.tokens = pl.BlockSpec((length, WIDE), lambda s, p: (s, p))
        self.row = pl.BlockSpec((1, WIDE), lambda s, p: (0, p))
        self.stack = pl.BlockSpec((3, length, WIDE), lambda s, p: (0, s, p))
        self.gate = pl.BlockSpec((1, length, WIDE), lambda s, p: (3, s, p))
        self.state = pl.BlockSpec((1, WIDE // PAIR, PAIR // 2, PAIR), lambda s, p: (s, p, 0, 0))
        self.heads = pl.BlockSpec(
            (1, 2 * WIDE // PAIR, PAIR // 2, PAIR // 2), lambda s, p: (s, p, 0, 0)
        )
        self.sums = pl.BlockSpec((1, 8, WIDE), lambda s, p: (s, 0, p))
        self.place = pl.BlockSpec(memory_space=pltpu.SMEM)

    def packed(self, blocks=None):
        rows = PAIR // 2 + EXTRA
        if blocks is None:
            return pl.BlockSpec((1, WIDE // PAIR, rows, PAIR), lambda s, p: (s, p, 0, 0))
        return pl.BlockSpec((blocks, 1, WIDE // PAIR, rows, PAIR), lambda s, p: (0, s, p, 0, 0))

    def terms(self, blocks):
        return pl.BlockSpec(
            (blocks, 1, WIDE // PAIR, PAIR // 2, PAIR), lambda s, p: (0, s, p, 0, 0)
        )

    def token_shape(self, kind):
        return jax.ShapeDtypeStruct((self.sequences * self.length, self.columns), kind)

    def state_shape(self, kind, rows=PAIR // 2):
        return jax.ShapeDtypeStruct((self.sequences, self.pairs, rows, PAIR), kind)

    def sums_shape(self):
        return jax.ShapeDtypeStruct((self.sequences, 8, self.columns), jnp.float32)

    def call(self, kernel, ins, outs, args, flops):
        size = sum(arg.size * arg.dtype.itemsize for arg in args)
        return pl.pallas_call(
            kernel,
            grid=self.grid,
            in_specs=ins,
            out_specs=[spec for spec, _ in outs],
            out_shape=[shape for _, shape in outs],
            compiler_params=pltpu.CompilerParams(vmem_limit_bytes=40 * 2**20),
            cost_estimate=pl.CostEstimate(
                flops=flops, bytes_accessed=size, transcendentals=6 * args[0].size
            ),
        )(*args)

    def totals(self, projected, log_rows):
        outs = [(self.packed(), self.state_shape(jnp.bfloat16, PAIR // 2 + EXTRA))]
        return self.call(
            totals_kernel, [self.stack, self.tokens], outs, (projected, log_rows), 10**9
        )[0]

    def inner(self, projected, log_rows, bonus):
        outs = [
            (self.tokens, self.token_shape(jnp.float32)),
            (self.tokens, self.token_shape(jnp.bfloat16)),
        ]
        ins = [self.stack, self.tokens, self.row]
        return self.call(inner_kernel, ins, outs, (projected, log_rows, bonus), 2 * 10**9)

    def join(self, place, inner, decayed, projected, packed, start, gain, bias):
        ins = [
            self.place,
            self.tokens,
            self.tokens,
            self.gate,
            self.packed(packed.shape[0]),
            self.heads,
            self.row,
            self.row,
        ]
        outs = [
            (self.tokens, self.token_shape(jnp.float32)),
            (self.tokens, self.token_shape(jnp.bfloat16)),
            (self.state, self.state_shape(jnp.float32)),
            (self.sums, self.sums_shape()),
        ]
        args = (place, inner, decayed, projected, packed, start, gain, bias)
        return self.call(join_kernel, ins, outs, args, 10**9)

    def back_join(self, grad, wkv, projected, decayed, gain, bias):
        ins = [self.tokens, self.tokens, self.gate, self.tokens, self.row, self.row]
        outs = [
            (self.tokens, self.token_shape(jnp.float32)),
            (self.tokens, self.token_shape(jnp.bfloat16)),
            (self.state, self.state_shape(jnp.bfloat16)),
            (self.sums, self.sums_shape()),
        ]
        args = (grad, wkv, projected, decayed, gain, bias)
        return self.call(back_join_kernel, ins, outs, args, 10**9)

    def back_inner(self, projected, log_rows, bonus, grad, state):
        ins = [self.stack, self.tokens, self.row, self.tokens, self.state]
        outs = [
            (self.tokens, self.token_shape(jnp.bfloat16)),
            (self.tokens, self.token_shape(jnp.float32)),
            (self.tokens, self.token_shape(jnp.float32)),
            (self.tokens, self.token_shape(jnp.float32)),
            (self.sums, self.sums_shape()),
        ]
        args = (projected, log_rows, bonus, grad, state)
        return self.call(back_inner_kernel, ins, outs, args, 4 * 10**9)

    def back_outer(self, place, projected, log_rows, keys, values, running, state, packed, terms):
        blocks = packed.shape[0]
        ins = [
            self.place,
            self.stack,
            self.tokens,
            self.tokens,
            self.tokens,
            self.tokens,
            self.state,
            self.packed(blocks),
            self.terms(blocks),
        ]
        outs = [
            (self.tokens, self.token_shape(jnp.bfloat16)),
            (self.tokens, self.token_shape(jnp.bfloat16)),
            (self.tokens, self.token_shape(jnp.float32)),
            (
                self.heads,
                jax.ShapeDtypeStruct(
                    (self.sequences, 2 * self.pairs, PAIR // 2, PAIR // 2), jnp.float32
                ),
            ),
            (self.sums, self.sums_shape()),
        ]
        args = (place, projected, log_rows, keys, values, running, state, packed, terms)
        return self.call(back_outer_kernel, ins, outs, args, 3 * 10**9)


BRANCHES = (3, 1, 2, 4)
STRIP = 512


def mix_back_kernel(
    x_ref,
    before_ref,
    grad_ref,
    log_ref,
    hidden_ref,
    decay_ref,
    proj_ref,
    coeff_ref,
    norm_ref,
    down_ref,
    up_ref,
    decay_down_ref,
    decay_up_ref,
    block_ref,
    edge_ref,
    all_ref,
    grad_decay_up_ref,
    hat_ref,
    grad_diff_ref,
    grad_all_ref,
):
    together, length, columns = x_ref.shape
    tokens = together * length
    ranks = up_ref.shape[0] // 5
    up_rows, decay_rows = up_ref.shape[0], decay_down_ref.shape[0]
    sums_ref = all_ref.at[0:8]
    grad_up_ref = all_ref.at[16 : 16 + up_rows]
    grad_down_ref = all_ref.at[16 + up_rows : 16 + 2 * up_rows]
    grad_decay_down_ref = all_ref.at[16 + 2 * up_rows : 16 + 2 * up_rows + decay_rows]
    strips = columns // STRIP
    low = jnp.bfloat16

    @pl.when(pl.program_id(0) == 0)
    def _():
        for ref in (all_ref, grad_decay_up_ref):
            ref[...] = jnp.zeros_like(ref)

    x = x_ref[...].reshape(tokens, columns).astype(jnp.float32)
    mean = jnp.mean(x, axis=-1, keepdims=True)
    variance = jnp.mean((x - mean) * (x - mean), axis=-1, keepdims=True)
    scale = lax.rsqrt(variance + NORM_EPS)
    hidden, hidden_decay = hidden_ref[...], decay_ref[...]
    low_hidden, low_decay = hidden.astype(low), hidden_decay.astype(low)
    grad_log = log_ref[...].astype(low)
    grad_decay = halves_dot(grad_log, decay_up_ref[...], ((1,), (1,)))
    grad_decay = grad_decay * (1.0 - hidden_decay * hidden_decay)
    low_grad_decay = grad_decay.astype(low)
    grad_decay_up_ref[...] += halves_dot(low_decay, grad_log, ((0,), (0,)))

    def strip_of(strip):
        return pl.ds(pl.multiple_of(strip * STRIP, STRIP), STRIP)

    def normed_and_diff(at, hat):
        normed = hat * norm_ref[0:1, at] + norm_ref[1:2, at]
        earlier = pltpu.roll(normed, 1, 0)
        for k in range(together):
            earlier = jnp.where(
                iota(normed.shape, 0) == k * length, before_ref[k, :, at], earlier
            )
        return normed, earlier - normed

    def first(strip, grad_pre):
        at = strip_of(strip)
        hat = (x_ref[:, :, at].reshape(tokens, STRIP).astype(jnp.float32) - mean) * scale
        hat_ref[:, at] = hat
        normed, diff = normed_and_diff(at, hat)
        grad_diff = jnp.zeros_like(diff)
        grad_all = jnp.zeros_like(diff)
        parts = []
        for branch in range(5):
            rows = slice(branch * ranks, (branch + 1) * ranks)
            up = up_ref[rows, at]
            weight = coeff_ref[1 + branch : 2 + branch, at] + halves_dot(
                low_hidden[:, rows], up, ((1,), (0,))
            )
            if branch == 0:
                mixed = normed + diff * weight
                grad_decay_down_ref[:, at] += halves_dot(low_grad_decay, mixed, ((0,), (0,)))
                grad = halves_dot(low_grad_decay, decay_down_ref[:, at], ((1,), (0,)))
            else:
                n = BRANCHES.index(branch)
                grad = halves_dot(grad_ref[n], proj_ref[n, at, :], ((1,), (1,)))
            grad_all += grad
            grad_diff += grad * weight
            moved = grad * diff
            sums_ref[1 + branch : 2 + branch, at] += jnp.sum(moved, axis=0, keepdims=True)
            moved = moved.astype(low)
            grad_up_ref[rows, at] += halves_dot(low_hidden[:, rows], moved, ((0,), (0,)))
            parts.append(halves_dot(moved, up, ((1,), (1,))))
        grad_diff_ref[:, at] = grad_diff
        grad_all_ref[:, at] = grad_all
        return grad_pre + jnp.concatenate(parts, axis=1)

    grad_pre = lax.fori_loop(0, strips, first, jnp.zeros(hidden.shape, jnp.float32))
    grad_pre = (grad_pre * (1.0 - hidden * hidden)).astype(low)

    def second(strip, carry):
        total, against = carry
        at = strip_of(strip)
        hat = hat_ref[:, at]
        normed, diff = normed_and_diff(at, hat)
        coeff = coeff_ref[0:1, at]
        grad_base = halves_dot(grad_pre, down_ref[:, at], ((1,), (0,)))
        grad_down_ref[:, at] += halves_dot(grad_pre, normed + diff * coeff, ((0,), (0,)))
        sums_ref[0:1, at] += jnp.sum(grad_base * diff, axis=0, keepdims=True)
        grad_diff = grad_diff_ref[:, at] + grad_base * coeff
        onward = pltpu.roll(grad_diff, tokens - 1, 0)
        for k in range(together):
            edge_ref[k, :, at] = grad_diff[k * length : k * length + 1]
            onward = jnp.where(iota(onward.shape, 0) == (k + 1) * length - 1, 0.0, onward)
        grad = grad_base + grad_all_ref[:, at] - grad_diff + onward
        sums_ref[6:7, at] += jnp.sum(grad * hat, axis=0, keepdims=True)
        sums_ref[7:8, at] += jnp.sum(grad, axis=0, keepdims=True)
        q = grad * norm_ref[0:1, at]
        grad_all_ref[:, at] = q
        total += jnp.sum(q, axis=-1, keepdims=True)
        against += jnp.sum(q * hat, axis=-1, keepdims=True)
        return total, against

    zero = jnp.zeros((tokens, 1), jnp.float32)
    total, against = lax.fori_loop(0, strips, second, (zero, zero))
    total, against = total * (1.0 / columns), against * (1.0 / columns)

    def third(strip, carry):
        at = strip_of(strip)
        block = scale * (grad_all_ref[:, at] - total - hat_ref[:, at] * against)
        block_ref[:, :, at] = block.reshape(together, length, STRIP)
        return carry

    lax.fori_loop(0, strips, third, 0)


def mix_back(
    block_input,
    before,
    grad_proj,
    grad_log,
    hidden,
    hidden_decay,
    projections,
    coeffs,
    norm,
    down,
    up,
    decay_down,
    decay_up,
    sum_rows,
):
    sequences, length, columns = block_input.shape
    heads = grad_proj.shape[-1]
    ranks, decay_ranks = up.shape[0], decay_up.shape[0]

    def whole(array):
        return pl.BlockSpec(array.shape, lambda s: (0,) * array.ndim)

    def kept(shape):
        return pl.BlockSpec(shape, lambda s: (0, 0)), jax.ShapeDtypeStruct(shape, jnp.float32)

    together = 2 - sequences % 2
    tokens = together * length
    block = pl.BlockSpec((together, length, columns), lambda s: (s, 0, 0))
    edge = pl.BlockSpec((together, 1, columns), lambda s: (s, 0, 0))
    outs = [
        (block, jax.ShapeDtypeStruct(block_input.shape, jnp.float32)),
        (edge, jax.ShapeDtypeStruct((sequences, 1, columns), jnp.float32)),
        kept((sum_rows, columns)),
        kept((decay_ranks, heads)),
    ]
    args = (
        block_input,
        before,
        grad_proj,
        grad_log,
        hidden,
        hidden_decay,
        projections,
        coeffs,
        norm,
        down,
        up,
        decay_down,
        decay_up,
    )
    return pl.pallas_call(
        mix_back_kernel,
        grid=(sequences // together,),
        in_specs=[
            block,
            edge,
            pl.BlockSpec((4, tokens, heads), lambda s: (0, s, 0)),
            pl.BlockSpec((tokens, heads), lambda s: (s, 0)),
            pl.BlockSpec((tokens, hidden.shape[1]), lambda s: (s, 0)),
            pl.BlockSpec((tokens, decay_ranks), lambda s: (s, 0)),
            pl.BlockSpec(projections.shape, lambda s: (0, 0, 0), pipeline_mode=pl.Buffered(1)),
        ]
        + [whole(array) for array in args[7:]],
        out_specs=[spec for spec, _ in outs],
        out_shape=[shape for _, shape in outs],
        scratch_shapes=[pltpu.VMEM((tokens, columns), jnp.float32)] * 3,
        compiler_params=pltpu.CompilerParams(vmem_limit_bytes=58 * 2**20),
        cost_estimate=pl.CostEstimate(
            flops=10**10, bytes_accessed=40 * 2**20, transcendentals=0
        ),
    )(*args)


def other_half(block):
    return lax.ppermute(block, "tp", [(0, 1), (1, 0)])


CORES = 2


def ring_places(dp_size, seq_size):
    per_row = seq_size // CORES
    count = dp_size * per_row

    def chip(position):
        position = lax.rem(position + 2 * count, count)
        row = lax.div(position, per_row)
        column = lax.rem(position, per_row)
        column = jnp.where(lax.rem(row, 2) == 0, column, per_row - 1 - column)
        return row, column

    def own():
        row, column = lax.axis_index("dp"), lax.div(lax.axis_index("seq"), CORES)
        return row * per_row + jnp.where(lax.rem(row, 2) == 0, column, per_row - 1 - column)

    return count, chip, own


def cut_rings(widths, rings):
    each = sum(widths) // rings
    runs, product, column = [], 0, 0
    for _ in range(rings):
        run, left = [], each
        while left:
            take = min(left, widths[product] - column)
            run.append((product, column, take))
            left, column = left - take, column + take
            if column == widths[product]:
                product, column = product + 1, 0
        runs.append(run)
    return runs


def ring_kernel(dp_size, seq_size, rows, widths, runs, places, operands, *refs):
    products = len(widths)
    lefts = [(refs[left], lead) for left, _, lead in places]
    rights = [(None if right is None else refs[right], lead) for _, right, lead in places]
    sent_ref, received_ref = refs[operands - 1], refs[operands + products]
    totals, refs = refs[operands : operands + products], refs[operands + products + 1 :]
    rings = len(runs)
    mine, pair_out, pair_in, ring_out, ring_in = [
        refs[k * rings : (k + 1) * rings] for k in range(5)
    ]
    pair_send, pair_recv, pair_free, ring_send, ring_recv, ring_free, half_send, half_recv = refs[
        5 * rings :
    ]
    count, chip, own = ring_places(dp_size, seq_size)
    position, core = own(), lax.rem(lax.axis_index("seq"), CORES)

    def device(place, which):
        row, column = chip(place)
        return {"dp": row, "seq": column * CORES + which}

    sibling = device(position, 1 - core)
    after, before = device(position + 1, core), device(position - 1, core)
    barrier = pltpu.get_barrier_semaphore()
    partner = {"tp": 1 - lax.axis_index("tp")}
    for other in (sibling, after, before, partner):
        pl.semaphore_signal(barrier, inc=1, device_id=other, device_id_type=pl.DeviceIdType.MESH)
    pl.semaphore_wait(barrier, 4)
    halves = pltpu.make_async_remote_copy(
        src_ref=sent_ref,
        dst_ref=received_ref,
        send_sem=half_send,
        recv_sem=half_recv,
        device_id=partner,
        device_id_type=pl.DeviceIdType.MESH,
    )
    halves.start()

    def pair_copy(ring):
        return pltpu.make_async_remote_copy(
            src_ref=pair_out[ring],
            dst_ref=pair_in[ring],
            send_sem=pair_send.at[ring],
            recv_sem=pair_recv.at[ring],
            device_id=sibling,
            device_id_type=pl.DeviceIdType.MESH,
        )

    def ring_copy(ring, slot):
        return pltpu.make_async_remote_copy(
            src_ref=ring_out[ring].at[slot],
            dst_ref=ring_in[ring].at[slot],
            send_sem=ring_send.at[ring, slot],
            recv_sem=ring_recv.at[ring, slot],
            device_id=after if ring % 2 == 0 else before,
            device_id_type=pl.DeviceIdType.MESH,
        )

    def part(ring, place, which, put):
        row, column = chip(place)
        start = (row * seq_size + column * CORES + which) * rows
        start = pl.multiple_of(start, rows)
        at = 0
        for product, first, wide in runs[ring]:
            ref, lead = lefts[product]
            if rights[product][0] is None:
                if rows % 128 == 0:
                    put(at, wide, ref[pl.ds(first, wide), pl.ds(start, rows)].T)
                else:
                    put(at, wide, ref[pl.ds(start, rows), pl.ds(first, wide)])
                at += wide
                continue
            if rows % 128 == 0:
                left = ref[(*lead, slice(None), pl.ds(start, rows))]
            else:
                left = ref[(*lead, pl.ds(start, rows), slice(None))]
            ref, lead = rights[product]
            right = ref[(*lead, slice(None), pl.ds(first, wide))]
            put(
                at,
                wide,
                lax.dot_general(
                    left,
                    right,
                    (((0 if rows % 128 == 0 else 1,), (0,)), ((), ())),
                    preferred_element_type=jnp.float32,
                ),
            )
            at += wide

    def turn(step, carry):
        slot = lax.rem(step, 2)
        last = 1 - slot
        for ring in range(rings):
            place = position - 1 - step if ring % 2 == 0 else position + 1 + step

            @pl.when(step >= 1)
            def _():
                pair_copy(ring).wait_send()

            def put_out(at, wide, value):
                pair_out[ring][:, at : at + wide] = value.astype(jnp.bfloat16)

            part(ring, place, 1 - core, put_out)

            @pl.when(step >= 1)
            def _():
                pl.semaphore_wait(pair_free.at[ring], 1)

            pair_copy(ring).start()

            def put_mine(at, wide, value):
                mine[ring][:, at : at + wide] = value

            part(ring, place, core, put_mine)
        for ring in range(rings):
            source = before if ring % 2 == 0 else after
            pair_copy(ring).wait_recv()

            @pl.when(step == 0)
            def _():
                ring_out[ring][slot] = (
                    mine[ring][...] + pair_in[ring][...].astype(jnp.float32)
                ).astype(jnp.bfloat16)

            @pl.when(step >= 1)
            def _():
                ring_copy(ring, last).wait_recv()

            @pl.when(jnp.logical_and(step >= 1, step < count - 1))
            def _():
                @pl.when(step >= 2)
                def _():
                    ring_copy(ring, slot).wait_send()

                ring_out[ring][slot] = (
                    mine[ring][...]
                    + pair_in[ring][...].astype(jnp.float32)
                    + ring_in[ring][last].astype(jnp.float32)
                ).astype(jnp.bfloat16)

            @pl.when(step == count - 1)
            def _():
                at = 0
                for product, first, wide in runs[ring]:
                    totals[product][:, first : first + wide] = (
                        mine[ring][:, at : at + wide]
                        + pair_in[ring][:, at : at + wide].astype(jnp.float32)
                        + ring_in[ring][last, :, at : at + wide].astype(jnp.float32)
                    )
                    at += wide

            @pl.when(step < count - 1)
            def _():
                @pl.when(step >= 2)
                def _():
                    pl.semaphore_wait(ring_free.at[ring], 1)

                ring_copy(ring, slot).start()
                pl.semaphore_signal(
                    pair_free.at[ring],
                    inc=1,
                    device_id=sibling,
                    device_id_type=pl.DeviceIdType.MESH,
                )

            @pl.when(jnp.logical_and(step >= 1, step < count - 2))
            def _():
                pl.semaphore_signal(
                    ring_free.at[ring],
                    inc=1,
                    device_id=source,
                    device_id_type=pl.DeviceIdType.MESH,
                )

        return carry

    lax.fori_loop(0, count, turn, 0)
    for ring in range(rings):
        pair_copy(ring).wait_send()
        for step in (count - 3, count - 2):
            ring_copy(ring, step % 2).wait_send()
    halves.wait()


def ring_sums(pairs, given, sent, sizes, collective_id):
    dp_size, seq_size = sizes
    rows = pairs[0][0].shape[-1] // (dp_size * seq_size)
    tokens = pairs[0][1].shape[-2]
    operands, known, places = [], {}, []

    def place_of(array, turned):
        if id(array) not in known:
            known[id(array)] = len(operands)
            operands.append(jnp.swapaxes(array, -1, -2) if turned else array)
        return known[id(array)]

    for left, right, lead in pairs:
        places.append((place_of(left, rows % 128 != 0), place_of(right, False), lead))
    places.append((place_of(given, rows % 128 != 0), None, ()))
    operands.append(sent)
    widths = [right.shape[-1] for _, right, _ in pairs] + [given.shape[0]]
    rings = 4
    runs = cut_rings(widths, rings)
    each = sum(widths) // rings
    low = jnp.bfloat16
    return pl.pallas_call(
        functools.partial(
            ring_kernel, dp_size, seq_size, rows, widths, runs, places, len(operands)
        ),
        out_shape=[jax.ShapeDtypeStruct((rows, wide), jnp.float32) for wide in widths]
        + [jax.ShapeDtypeStruct(sent.shape, sent.dtype)],
        in_specs=[pl.BlockSpec(memory_space=pltpu.VMEM)] * len(operands),
        out_specs=[pl.BlockSpec(memory_space=pltpu.VMEM)] * (len(widths) + 1),
        scratch_shapes=[pltpu.VMEM((rows, each), jnp.float32)] * rings
        + [pltpu.VMEM((rows, each), low)] * (2 * rings)
        + [pltpu.VMEM((2, rows, each), low)] * (2 * rings)
        + [
            pltpu.SemaphoreType.DMA((rings,)),
            pltpu.SemaphoreType.DMA((rings,)),
            pltpu.SemaphoreType.REGULAR((rings,)),
            pltpu.SemaphoreType.DMA((rings, 2)),
            pltpu.SemaphoreType.DMA((rings, 2)),
            pltpu.SemaphoreType.REGULAR((rings,)),
            pltpu.SemaphoreType.DMA(()),
            pltpu.SemaphoreType.DMA(()),
        ],
        compiler_params=pltpu.CompilerParams(
            collective_id=collective_id, has_side_effects=True, vmem_limit_bytes=60 * 2**20
        ),
        cost_estimate=pl.CostEstimate(
            flops=2 * tokens * rows * dp_size * seq_size * sum(widths),
            bytes_accessed=2 * tokens * (2048 * len(pairs) + sum(widths)),
            transcendentals=0,
        ),
    )(*operands)


def gather_kernel(
    dp_size,
    seq_size,
    small_ref,
    proj_ref,
    out_ref,
    small_all,
    proj_all,
    out_all,
    keep,
    send,
    recv,
    pair_send,
    pair_recv,
):
    width = small_ref.shape[1]
    count, chip, own = ring_places(dp_size, seq_size)
    position, core = own(), lax.rem(lax.axis_index("seq"), CORES)
    far = count // 2
    hops = [(far, far - 1), (far, far - 1), (far - 1, far), (far - 1, far)]
    halfway = proj_ref.shape[0] // 2

    def device(place, which):
        row, column = chip(place)
        return {"dp": row, "seq": column * CORES + which}

    def regions(place, which):
        row, column = chip(place)
        start = (row * seq_size + column * CORES + which) * width
        at = pl.ds(pl.multiple_of(start, width), width)
        return [
            small_all.at[:, at],
            proj_all.at[:halfway, at, :],
            proj_all.at[halfway:, at, :],
            out_all.at[:, at],
        ]

    sources = [small_ref, proj_ref.at[:halfway], proj_ref.at[halfway:], out_ref]
    sibling = device(position, 1 - core)
    ways = [device(position + 1, core), device(position - 1, core)]
    barrier = pltpu.get_barrier_semaphore()
    for other in [sibling] + ways:
        pl.semaphore_signal(barrier, inc=1, device_id=other, device_id_type=pl.DeviceIdType.MESH)
    pl.semaphore_wait(barrier, 3)

    def place_of(way, hop):
        return position - hop if way == 0 else position + hop

    def onward(part, way, hop):
        at = regions(place_of(way, hop - 1), core)[part]
        return pltpu.make_async_remote_copy(
            src_ref=sources[part] if hop == 1 else at,
            dst_ref=at,
            send_sem=send.at[part, way, hop - 1],
            recv_sem=recv.at[part, way, hop - 1],
            device_id=ways[way],
            device_id_type=pl.DeviceIdType.MESH,
        )

    def across(part, way, hop):
        at = regions(place_of(way, hop), core)[part]
        return pltpu.make_async_remote_copy(
            src_ref=sources[part] if hop == 0 else at,
            dst_ref=at,
            send_sem=pair_send.at[part, way, hop],
            recv_sem=pair_recv.at[part, way, hop],
            device_id=sibling,
            device_id_type=pl.DeviceIdType.MESH,
        )

    parts = range(len(sources))
    kept = []
    for part in parts:
        for way in range(2):
            onward(part, way, 1).start()
        across(part, 0, 0).start()
        copy = pltpu.make_async_copy(
            sources[part], regions(position, core)[part], keep.at[part]
        )
        copy.start()
        kept.append(copy)
    for hop in range(1, far + 1):
        for part in parts:
            for way in range(2):
                if hop <= hops[part][way]:
                    onward(part, way, hop).wait_recv()
                    if hop < hops[part][way]:
                        onward(part, way, hop + 1).start()
                    across(part, way, hop).start()
    for part in parts:
        kept[part].wait()
        across(part, 0, 0).wait()
        for way in range(2):
            for hop in range(1, hops[part][way] + 1):
                onward(part, way, hop).wait_send()
                across(part, way, hop).wait()


def gather_weights(small, proj, out, sizes, collective_id):
    if small.shape[1] % 128:
        return (
            lax.all_gather(small, ("dp", "seq"), axis=1, tiled=True),
            lax.all_gather(proj, ("dp", "seq"), axis=1, tiled=True),
            lax.all_gather(out, ("dp", "seq"), axis=1, tiled=True),
        )
    dp_size, seq_size = sizes
    every = dp_size * seq_size
    far = every // CORES // 2
    rows, width = small.shape
    shapes = [
        (rows, width * every),
        (proj.shape[0], width * every, proj.shape[2]),
        (out.shape[0], width * every),
    ]
    return pl.pallas_call(
        functools.partial(gather_kernel, dp_size, seq_size),
        out_shape=[jax.ShapeDtypeStruct(shape, small.dtype) for shape in shapes],
        in_specs=[pl.BlockSpec(memory_space=pl.ANY)] * 3,
        out_specs=[pl.BlockSpec(memory_space=pl.ANY)] * 3,
        scratch_shapes=[pltpu.SemaphoreType.DMA((4,))]
        + [pltpu.SemaphoreType.DMA((4, 2, far))] * 2
        + [pltpu.SemaphoreType.DMA((4, 2, far + 1))] * 2,
        compiler_params=pltpu.CompilerParams(collective_id=collective_id, has_side_effects=True),
    )(small, proj, out)


def mix_kernel(
    x_ref,
    before_ref,
    coeff_ref,
    norm_ref,
    down_ref,
    up_ref,
    decay_down_ref,
    decay_up_ref,
    base_ref,
    mixed_ref,
    hidden_ref,
    decay_ref,
    log_ref,
):
    length, columns = x_ref.shape[1:]
    ranks = up_ref.shape[0] // 5
    strips = columns // STRIP
    x = x_ref[0].astype(jnp.float32)
    mean = jnp.mean(x, axis=-1, keepdims=True)
    variance = jnp.mean((x - mean) * (x - mean), axis=-1, keepdims=True)
    scale = lax.rsqrt(variance + NORM_EPS)

    def normed_and_diff(strip):
        at = pl.ds(pl.multiple_of(strip * STRIP, STRIP), STRIP)
        hat = (x_ref[0, :, at].astype(jnp.float32) - mean) * scale
        normed = hat * norm_ref[0:1, at] + norm_ref[1:2, at]
        earlier = pltpu.roll(normed, 1, 0)
        earlier = jnp.where(iota(normed.shape, 0) == 0, before_ref[0, :, at], earlier)
        return at, normed, earlier - normed

    def first(strip, hidden):
        at, normed, diff = normed_and_diff(strip)
        return hidden + halves_dot(normed + diff * coeff_ref[0:1, at], down_ref[:, at], ((1,), (1,)))

    hidden = lax.fori_loop(0, strips, first, jnp.zeros(hidden_ref.shape, jnp.float32))
    hidden = jnp.tanh(hidden)
    hidden_ref[...] = hidden
    hidden = hidden.astype(jnp.bfloat16)

    def second(strip, decay):
        at, normed, diff = normed_and_diff(strip)
        for branch in range(5):
            rows = slice(branch * ranks, (branch + 1) * ranks)
            weight = coeff_ref[1 + branch : 2 + branch, at] + halves_dot(
                hidden[:, rows], up_ref[rows, at], ((1,), (0,))
            )
            mixed = (normed + diff * weight).astype(jnp.bfloat16)
            if branch == 0:
                decay += halves_dot(mixed, decay_down_ref[:, at], ((1,), (1,)))
            else:
                mixed_ref[BRANCHES.index(branch), :, at] = mixed
        return decay

    decay = lax.fori_loop(0, strips, second, jnp.zeros(decay_ref.shape, jnp.float32))
    decay = jnp.tanh(decay)
    decay_ref[...] = decay
    log_ref[...] = base_ref[...] + halves_dot(decay, decay_up_ref[...], ((1,), (0,)))


def mix_forward(block_input, before, coeffs, norm, down, up, decay_down, decay_up, base):
    sequences, length, columns = block_input.shape
    heads, tokens = decay_up.shape[1], sequences * length
    args = (block_input, before, coeffs, norm, down, up, decay_down, decay_up, base)

    def rows(wide):
        return pl.BlockSpec((length, wide), lambda s: (s, 0))

    outs = [(down.shape[0], jnp.float32), (decay_up.shape[0], jnp.float32), (heads, jnp.float32)]
    return pl.pallas_call(
        mix_kernel,
        grid=(sequences,),
        in_specs=[
            pl.BlockSpec((1, length, columns), lambda s: (s, 0, 0)),
            pl.BlockSpec((1, 1, columns), lambda s: (s, 0, 0)),
        ]
        + [pl.BlockSpec(array.shape, lambda s: (0, 0)) for array in args[2:]],
        out_specs=[pl.BlockSpec((4, length, columns), lambda s: (0, s, 0))]
        + [rows(wide) for wide, _ in outs],
        out_shape=[jax.ShapeDtypeStruct((4, tokens, columns), jnp.bfloat16)]
        + [jax.ShapeDtypeStruct((tokens, wide), kind) for wide, kind in outs],
        compiler_params=pltpu.CompilerParams(vmem_limit_bytes=40 * 2**20),
        cost_estimate=pl.CostEstimate(
            flops=2 * 10**9, bytes_accessed=16 * 2**20, transcendentals=10**5
        ),
    )(*args)


def per_device(
    block_input,
    initial_state,
    norm_gains,
    norm_biases,
    mixing_coefficients,
    mix_down,
    mixing_up_weight,
    decay_down,
    decay_up,
    proj_weights,
    out_weight,
    time_decay,
    time_first,
    group_gain,
    group_bias,
    channel_key,
    channel_value,
    channel_recept,
    out_grad,
):
    blocks, place = lax.axis_size("seq"), lax.axis_index("seq")
    half = lax.axis_index("tp")
    sizes = (lax.axis_size("dp"), blocks)
    width = norm_gains.shape[1]
    heads_here, each = time_decay.shape
    head_size = initial_state.shape[-1]
    head_cols = heads_here * head_size
    ranks, decay_ranks = mix_down.shape[1], decay_down.shape[1]

    def narrow_rows(part):
        part = part.reshape(-1, heads_here * each)
        return jnp.pad(part, ((0, 0), (0, width - part.shape[1])))

    up_at = 16
    down_at = up_at + ranks
    decay_at = down_at + ranks
    narrow_at = decay_at + decay_ranks
    top_rows = jnp.concatenate(
        [norm_gains, norm_biases, mixing_coefficients, jnp.zeros((4, width), jnp.bfloat16)]
    )
    low_rows = jnp.concatenate(
        [
            narrow_rows(time_decay),
            narrow_rows(time_first),
            narrow_rows(group_gain),
            narrow_rows(group_bias),
            jnp.zeros((12, width), jnp.bfloat16),
        ]
    )
    top_rows, low_rows = lax.optimization_barrier((top_rows, low_rows))
    own_rows = jnp.concatenate(
        [
            top_rows,
            mixing_up_weight,
            mix_down.T,
            decay_down.T,
            narrow_rows(decay_up),
            low_rows,
        ]
    )
    spread_rows, projections, out_proj = gather_weights(
        own_rows, proj_weights, out_weight, sizes, 1
    )
    channel = jnp.arange(head_cols)
    lane = (channel % head_size) // each * width + channel // head_size * each + channel % each
    choose = (jnp.arange(spread_rows.shape[1])[:, None] == lane[None, :]).astype(jnp.bfloat16)
    narrow_all = jnp.dot(
        spread_rows[narrow_at:], choose, preferred_element_type=jnp.float32
    )
    gains_all, biases_all = (spread_rows[k : k + 2].astype(jnp.float32) for k in (0, 2))
    shift_coefficient = spread_rows[4:12].astype(jnp.float32)
    lowrank_up = spread_rows[up_at:down_at]
    lowrank_down = spread_rows[down_at:decay_at]
    decay_projection = spread_rows[decay_at:narrow_at]
    lift_rows = narrow_all[:decay_ranks].astype(jnp.bfloat16)
    base_row, bonus, group_scale, group_shift = (
        narrow_all[decay_ranks + k : decay_ranks + k + 1] for k in range(4)
    )
    seq_count, length, feature_columns = block_input.shape
    tokens = seq_count * length
    own_cols = channel_recept.shape[1]

    def both_halves(own):
        other = other_half(own)
        low = jnp.where(half == 0, own, other)
        high = jnp.where(half == 0, other, own)
        return jnp.concatenate([low, high], axis=-1)

    def own_half(rows):
        return lax.dynamic_slice_in_dim(rows, half * own_cols, own_cols, rows.ndim - 1)

    def add_last(rows, last):
        at_last = jnp.arange(length)[None, :, None] == length - 1
        return rows + jnp.where(at_last, last[:, None, :], 0.0)

    full_out = both_halves(out_grad)
    last_input = block_input[:, -1].astype(jnp.float32)
    last_one = layer_norm(last_input, gains_all[0], biases_all[0])
    preceding_first = from_behind(last_one.astype(jnp.bfloat16), "seq", 1)
    preceding_first = preceding_first.astype(jnp.float32)[:, None, :]
    norm_one = jnp.stack([gains_all[0], biases_all[0]])
    stacked, hidden_mixture, hidden_decay, log_flat = mix_forward(
        block_input,
        preceding_first,
        shift_coefficient,
        norm_one,
        lowrank_down,
        lowrank_up,
        decay_projection,
        lift_rows,
        base_row,
    )
    projected = jnp.einsum("ntd,nde->nte", stacked, projections, preferred_element_type=jnp.float32)
    recurrence = Recurrence(seq_count, length, head_cols)
    where_here = place.astype(jnp.int32).reshape(1)
    all_packed = lax.all_gather(recurrence.totals(projected, log_flat), "seq")
    inner, decayed = recurrence.inner(projected, log_flat, bonus)
    wkv, mixer_rows, state, decay_range = recurrence.join(
        where_here,
        inner,
        decayed,
        projected,
        all_packed,
        initial_state,
        group_scale,
        group_shift,
    )
    mixer_in = mixer_rows.reshape(seq_count, length, head_cols)
    decay_range = decay_range[:, :2].reshape(seq_count, 2, heads_here, head_size)
    total_least = jnp.min(decay_range[:, 0], axis=-1)
    total_most = jnp.max(decay_range[:, 1], axis=-1)
    runs = 2 - seq_count % 2
    each_run = seq_count // runs
    parts = range(runs)

    def run_of(rows):
        return [rows[k * each_run : (k + 1) * each_run] for k in parts]

    def flat(rows):
        return jnp.concatenate([part.reshape(-1, part.shape[-1]) for part in rows])

    def product(pattern, left, right):
        return jnp.einsum(pattern, left, right, preferred_element_type=jnp.float32)

    def summed(part):
        return part + other_half(part.astype(jnp.bfloat16)).astype(jnp.float32)

    mixer_part = [product("std,de->ste", rows, out_proj) for rows in run_of(mixer_in)]
    late_input, *mixer_part = lax.optimization_barrier((block_input, *mixer_part))
    residual = [
        rows.astype(jnp.float32) + summed(part)
        for rows, part in zip(run_of(late_input), mixer_part)
    ]
    normed_two, norm_two_back = zip(
        *[jax.vjp(layer_norm, rows, gains_all[1], biases_all[1]) for rows in residual]
    )
    prev_two = [
        from_behind(rows[:, -1, :].astype(jnp.bfloat16), "seq", 1).astype(jnp.float32)
        for rows in normed_two
    ]
    chan_inputs, chan_back = zip(
        *[
            jax.vjp(channel_mix, rows, prev, shift_coefficient)
            for rows, prev in zip(normed_two, prev_two)
        ]
    )
    chan_key_b = [rows.astype(jnp.bfloat16) for rows, _ in chan_inputs]
    chan_recept_b = [rows.astype(jnp.bfloat16) for _, rows in chan_inputs]
    own_value, sent_value = (
        lax.dynamic_slice_in_dim(channel_value, which * own_cols, own_cols, 1)
        for which in (half, 1 - half)
    )
    out_grads = run_of(out_grad.astype(jnp.float32))
    key_pre, hidden, own_part, other_part, recept_pre = [], [], [], [], []
    for k in parts:
        key_pre.append(product("std,df->stf", chan_key_b[k], channel_key))
        hidden.append(jnp.square(jnp.maximum(key_pre[k], 0.0)).astype(jnp.bfloat16))
        sent_part = product("stf,fd->std", hidden[k], sent_value).astype(jnp.bfloat16)
        other_part.append(other_half(sent_part).astype(jnp.float32))
        own, recept = lax.optimization_barrier(
            (
                product("stf,fd->std", hidden[k], own_value),
                product("std,de->ste", chan_recept_b[k], channel_recept),
            )
        )
        own_part.append(own)
        recept_pre.append(recept)
    output, grad_recept, full_value = [], [], []
    for k in parts:
        kv_rows = own_part[k] + other_part[k]
        gate_chan = jax.nn.sigmoid(recept_pre[k])
        output.append((own_half(residual[k]) + gate_chan * kv_rows).astype(jnp.bfloat16))
        grad_recept.append(
            (out_grads[k] * kv_rows * gate_chan * (1.0 - gate_chan)).astype(jnp.bfloat16)
        )
        full_value.append(both_halves((out_grads[k] * gate_chan).astype(jnp.bfloat16)))
    output = jnp.concatenate(output)

    def weight_terms(left, right):
        return product("td,tf->df", left, right).astype(jnp.bfloat16)

    def scattered(whole):
        return lax.psum_scatter(whole, ("dp", "seq"), scatter_dimension=0, tiled=True).astype(
            jnp.float32
        )

    flat_value, flat_hidden = flat(full_value), flat(hidden)
    value_cut = flat_hidden.shape[1] * 5 // 7
    value_whole = weight_terms(flat_value, flat_hidden[:, :value_cut])
    full_value[-1], value_whole = lax.optimization_barrier((full_value[-1], value_whole))
    value_sum = scattered(value_whole)
    grad_key, part_normed_two, grad_coeffs_chan = [], [], 0.0
    for k in parts:
        grad_hidden = product("std,fd->stf", full_value[k], channel_value)
        grad_key.append((grad_hidden * 2.0 * jnp.maximum(key_pre[k], 0.0)).astype(jnp.bfloat16))
        part_key = product("stf,df->std", grad_key[k], channel_key)
        part_recept = product("ste,de->std", grad_recept[k], channel_recept)
        part_two, part_prev_two, coeffs = chan_back[k]((part_key, part_recept))
        from_next_two = from_behind(for_sending(part_prev_two), "seq", -1).astype(jnp.float32)
        part_normed_two.append(add_last(part_two, from_next_two))
        grad_coeffs_chan += coeffs
    flat_chan_key, flat_grad_key = flat(chan_key_b), flat(grad_key)
    key_cut = flat_grad_key.shape[1] * 5 // 7
    key_whole = weight_terms(flat_chan_key, flat_grad_key[:, :key_cut])
    two_back = [back(summed(part)) for back, part in zip(norm_two_back, part_normed_two)]
    grad_gain_two, grad_bias_two = (sum(back[k] for back in two_back) for k in (1, 2))
    grad_residual = jnp.concatenate([back[0] for back in two_back])
    grad_residual = grad_residual + full_out.astype(jnp.float32)
    grad_residual, key_whole = lax.optimization_barrier((grad_residual, key_whole))
    grad_branch = grad_residual.astype(jnp.bfloat16)
    grad_mixer = jnp.einsum(
        "ste,de->std", grad_branch, out_proj, preferred_element_type=jnp.float32
    )
    grad_wkv, grad_gate, block_term, group_sums = recurrence.back_join(
        grad_mixer.reshape(tokens, head_cols), wkv, projected, decayed, group_scale, group_shift
    )
    all_terms = lax.all_gather(block_term, "seq")
    grad_wkv, value_sum, key_whole = lax.optimization_barrier((grad_wkv, value_sum, key_whole))
    key_sum = scattered(key_whole)
    grad_receive, near_key, near_value, running, bonus_sums = recurrence.back_inner(
        projected, log_flat, bonus, grad_wkv, state
    )
    grad_keys, grad_values, grad_log, state_grad, rate_sums = recurrence.back_outer(
        where_here,
        projected,
        log_flat,
        near_key,
        near_value,
        running,
        state,
        all_packed,
        all_terms,
    )

    grad_proj = jnp.stack([grad_receive, grad_keys, grad_values, grad_gate])
    part_block, edge, small_rows, lift_grad = mix_back(
        block_input,
        preceding_first,
        grad_proj,
        grad_log,
        hidden_mixture,
        hidden_decay,
        projections,
        shift_coefficient,
        norm_one,
        lowrank_down,
        lowrank_up,
        decay_projection,
        lift_rows,
        narrow_at + 112,
    )
    from_next_one = from_behind(edge[:, 0].astype(jnp.bfloat16), "seq", -1).astype(jnp.float32)
    _, last_back = jax.vjp(layer_norm, last_input, gains_all[0], biases_all[0])
    part_last, gain_last, bias_last = last_back(from_next_one)
    part_block = add_last(part_block, part_last)
    head_rows = jnp.concatenate(
        [
            lift_grad,
            jnp.sum(rate_sums[:, :1], axis=0),
            jnp.sum(bonus_sums[:, :1], axis=0),
            jnp.sum(group_sums[:, :2], axis=0),
            jnp.zeros((12, head_cols), jnp.float32),
        ]
    )
    thirds = []
    for _ in range(3):
        thirds.append(head_rows.astype(jnp.bfloat16))
        head_rows = head_rows - lax.optimization_barrier(thirds[-1]).astype(jnp.float32)
    head_rows = jnp.sum(
        lax.dot_general(
            jnp.stack(thirds),
            choose,
            (((2,), (1,)), ((), ())),
            preferred_element_type=jnp.float32,
        ),
        axis=0,
    )
    other_rows = jnp.concatenate(
        [
            grad_coeffs_chan[6:],
            jnp.stack([0.5 * grad_gain_two, 0.5 * grad_bias_two, gain_last, bias_last]),
            jnp.zeros((2, feature_columns), jnp.float32),
        ]
    )
    small_rows = lax.dynamic_update_slice(small_rows, other_rows, (8, 0))
    small_rows = lax.dynamic_update_slice(small_rows, head_rows, (narrow_at, 0))
    sent_block = lax.dynamic_slice_in_dim(part_block, (1 - half) * own_cols, own_cols, 2)
    *proj_sums, out_sum, recept_sum, key_rest, value_rest, small_sums, other_block = ring_sums(
        [(stacked, grad_proj, (branch,)) for branch in range(4)]
        + [
            (grad_branch.reshape(tokens, -1), mixer_in.reshape(tokens, -1), ()),
            (flat(chan_recept_b), flat(grad_recept), ()),
            (flat_chan_key, flat_grad_key[:, key_cut:], ()),
            (flat_value, flat_hidden[:, value_cut:], ()),
        ],
        small_rows,
        sent_block.astype(jnp.bfloat16),
        sizes,
        0,
    )
    small_sums = small_sums.T
    input_grad = own_half(grad_residual) + own_half(part_block) + other_block.astype(jnp.float32)
    shared = small_sums[:narrow_at] + other_half(small_sums[:narrow_at])
    narrow = small_sums[narrow_at:, : heads_here * each]
    head_sums = [
        narrow[decay_ranks + k].reshape(heads_here, each) for k in range(4)
    ]
    return (
        output,
        input_grad,
        state_grad,
        jnp.stack([shared[6] + shared[12], shared[10]]),
        jnp.stack([shared[7] + shared[13], shared[11]]),
        jnp.concatenate([shared[:1], shared[2:6], shared[8:10]], axis=0),
        shared[1:2],
        shared[down_at:decay_at].T,
        shared[up_at:down_at],
        shared[decay_at:].T,
        narrow[:decay_ranks].reshape(decay_ranks, heads_here, each),
        jnp.stack(proj_sums),
        out_sum.T,
        *head_sums,
        jnp.concatenate([key_sum, key_rest], axis=1),
        jnp.concatenate([value_sum, value_rest], axis=1).T,
        recept_sum,
        total_least,
        total_most,
    )


def solution(mesh):
    return jax.shard_map(
        per_device,
        mesh=mesh,
        in_specs=(
            P("dp", "seq", None),
            P("dp", "tp", None, None),
            P(None, ("dp", "seq")),
            P(None, ("dp", "seq")),
            P(None, ("dp", "seq")),
            P(("dp", "seq"), None),
            P(None, ("dp", "seq")),
            P(("dp", "seq"), None),
            P(None, "tp", ("dp", "seq")),
            P(None, ("dp", "seq"), "tp"),
            P("tp", ("dp", "seq")),
            P("tp", ("dp", "seq")),
            P("tp", ("dp", "seq")),
            P("tp", ("dp", "seq")),
            P("tp", ("dp", "seq")),
            P(None, "tp"),
            P("tp", None),
            P(None, "tp"),
            P("dp", "seq", "tp"),
        ),
        out_specs=(
            P("dp", "seq", "tp"),
            P("dp", "seq", "tp"),
            P("dp", "tp", None, None),
            P(None, ("dp", "seq")),
            P(None, ("dp", "seq")),
            P(None, ("dp", "seq")),
            P(None, ("dp", "seq")),
            P(("dp", "seq"), None),
            P(None, ("dp", "seq")),
            P(("dp", "seq"), None),
            P(None, "tp", ("dp", "seq")),
            P(None, ("dp", "seq"), "tp"),
            P("tp", ("dp", "seq")),
            P("tp", ("dp", "seq")),
            P("tp", ("dp", "seq")),
            P("tp", ("dp", "seq")),
            P("tp", ("dp", "seq")),
            P(("dp", "seq"), "tp"),
            P("tp", ("dp", "seq")),
            P(("dp", "seq"), "tp"),
            P("dp", "tp"),
            P("dp", "tp"),
        ),
        check_vma=False,
    )
```

```python
import functools

import jax
import jax.numpy as jnp
from jax import lax
from jax.experimental import pallas as pl
from jax.experimental.pallas import tpu as pltpu
from jax.sharding import PartitionSpec as P

NORM_EPS = 1e-05
GROUP_EPS = 0.00064


def from_behind(block, axis, distance):
    devices = range(lax.axis_size(axis))
    route = [(i - distance, i) for i in devices if i - distance in devices]
    return lax.ppermute(block, axis, route)


def for_sending(array):

    def short(part):
        return part.astype(jnp.bfloat16) if part.dtype == jnp.float32 else part

    return jax.tree.map(short, array)


def layer_norm(values, scale_row, shift_row):
    mean_val = jnp.mean(values, axis=-1, keepdims=True)
    centered = values - mean_val
    variance = jnp.mean(centered * centered, axis=-1, keepdims=True)
    return centered * lax.rsqrt(variance + NORM_EPS) * scale_row + shift_row


def channel_mix(normalized_rows, preceding_row, shift_coefficient):
    earlier = jnp.concatenate([preceding_row[:, None, :], normalized_rows[:, :-1, :]], axis=1)
    shift_difference = earlier - normalized_rows
    return (
        normalized_rows + shift_difference * shift_coefficient[6],
        normalized_rows + shift_difference * shift_coefficient[7],
    )


WIDE = 256
PAIR = 128
EXTRA = 16


def halves_dot(left, right, dims):
    return lax.dot_general(
        left.astype(jnp.bfloat16),
        right.astype(jnp.bfloat16),
        (dims, ((), ())),
        preferred_element_type=jnp.float32,
    )


def exact_dot(ones, values):
    high = values.astype(jnp.bfloat16)
    rest = values - high.astype(jnp.float32)
    middle = rest.astype(jnp.bfloat16)
    low = (rest - middle.astype(jnp.float32)).astype(jnp.bfloat16)
    ones = ones.astype(jnp.bfloat16)
    dims = ((1,), (0,))
    return (
        halves_dot(ones, high, dims) + halves_dot(ones, middle, dims) + halves_dot(ones, low, dims)
    )


def iota(shape, dim):
    return lax.broadcasted_iota(jnp.int32, shape, dim)


def first_head(shape):
    return iota(shape, len(shape) - 1) < PAIR // 2


def compact(full):
    top, low = full[: PAIR // 2], full[PAIR // 2 :]
    return jnp.where(first_head(top.shape), top, low)


def spread(state):
    first = first_head(state.shape)
    return jnp.concatenate([jnp.where(first, state, 0.0), jnp.where(first, 0.0, state)], axis=0)


def head_sum(values):
    first = first_head(values.shape)
    a = jnp.sum(jnp.where(first, values, 0.0), axis=-1, keepdims=True)
    b = jnp.sum(jnp.where(first, 0.0, values), axis=-1, keepdims=True)
    return jnp.where(first, a, b)


def running_decay(log_rates):
    length = log_rates.shape[0]
    rates = -jnp.exp(log_rates)
    up_to = iota((length, length), 0) >= iota((length, length), 1)
    return rates, exact_dot(up_to.astype(jnp.float32), rates)


def two_parts(row):
    high = row.astype(jnp.bfloat16).astype(jnp.float32)
    return high, row - high


def totals_kernel(kv_ref, log_ref, packed_ref):
    for pair in range(WIDE // PAIR):
        lanes = slice(pair * PAIR, (pair + 1) * PAIR)
        keys, values = kv_ref[1, :, lanes], kv_ref[2, :, lanes]
        rates, total = running_decay(log_ref[:, lanes])
        length = rates.shape[0]
        final = total[length - 1 : length]
        state = compact(halves_dot(keys * jnp.exp(final - total), values, ((0,), (0,))))
        decay = jnp.exp(rates)
        rows = [
            *two_parts(jnp.exp(final)),
            *two_parts(jnp.min(decay, axis=0, keepdims=True)),
            *two_parts(jnp.max(decay, axis=0, keepdims=True)),
        ]
        row_at = iota((EXTRA, PAIR), 0)
        extra = jnp.zeros((EXTRA, PAIR), jnp.float32)
        for at, row in enumerate(rows):
            extra = jnp.where(row_at == at, row, extra)
        packed_ref[0, pair] = jnp.concatenate([state, extra], axis=0).astype(jnp.bfloat16)


def inner_scores(receive, keys, rates, total):
    length = receive.shape[0]
    before = total - rates
    middle = before[length // 2 : length // 2 + 1]
    up, down = jnp.exp(before - middle), jnp.exp(middle - total)
    rows, columns = receive * up, keys * down
    first = first_head(rows.shape)
    later = iota((length, length), 0) > iota((length, length), 1)
    columns = columns.astype(jnp.bfloat16)
    scores = [
        jnp.where(
            later, halves_dot(jnp.where(own, rows, 0.0), columns, ((1,), (1,))), 0.0
        ).astype(jnp.bfloat16)
        for own in (first, jnp.logical_not(first))
    ]
    return rows.astype(jnp.bfloat16), columns, scores, up, down, before


def heads_apply(left, right, side):
    first = first_head(right.shape)
    a = halves_dot(left[0], right, ((side,), (0,)))
    b = halves_dot(left[1], right, ((side,), (0,)))
    return jnp.where(first, a, b)


def inner_kernel(rkv_ref, log_ref, bonus_ref, inner_ref, decayed_ref):
    for pair in range(WIDE // PAIR):
        lanes = slice(pair * PAIR, (pair + 1) * PAIR)
        receive, keys, values = (rkv_ref[n, :, lanes] for n in range(3))
        rates, total = running_decay(log_ref[:, lanes])
        _, _, scores, _, _, before = inner_scores(receive, keys, rates, total)
        now = head_sum(receive * bonus_ref[:, lanes] * keys)
        inner_ref[:, lanes] = heads_apply(scores, values, 1) + now * values
        decayed_ref[:, lanes] = (receive * jnp.exp(before)).astype(jnp.bfloat16)


def block_decays(extra):
    blocks = extra.shape[0]
    flat = extra.astype(jnp.float32)
    columns = []
    for start in range(0, blocks, PAIR // EXTRA):
        some = flat[start : start + PAIR // EXTRA]
        some = some.reshape(some.shape[0] * EXTRA, PAIR)
        if some.shape[0] < PAIR:
            some = jnp.concatenate(
                [some, jnp.zeros((PAIR - some.shape[0], PAIR), jnp.float32)], axis=0
            )
        turned = some.T
        for k in range(min(PAIR // EXTRA, blocks - start)):
            both = turned[:, k * EXTRA : k * EXTRA + 1] + turned[:, k * EXTRA + 1 : k * EXTRA + 2]
            columns.append(compact(jnp.broadcast_to(both, (PAIR, PAIR))))
    return columns


def norm_heads(wkv, count):
    mean = head_sum(wkv) * (1.0 / count)
    centered = wkv - mean
    scale = lax.rsqrt(head_sum(centered * centered) * (1.0 / count) + GROUP_EPS)
    return centered * scale, scale


def join_kernel(
    place_ref, inner_ref, decayed_ref, gate_ref, packed_ref, start_ref, gain_ref, bias_ref, *outs
):
    wkv_ref, mixer_ref, state_ref, range_ref = outs
    blocks = packed_ref.shape[0]
    place = place_ref[0]
    for pair in range(WIDE // PAIR):
        lanes = slice(pair * PAIR, (pair + 1) * PAIR)
        state = jnp.concatenate([start_ref[0, 2 * pair], start_ref[0, 2 * pair + 1]], axis=1)
        extra = packed_ref[:, 0, pair, PAIR // 2 :, :]
        decays = block_decays(extra)
        extra = extra.astype(jnp.float32)
        range_ref[0, :, lanes] = put_rows(
            [
                jnp.min(extra[:, 2] + extra[:, 3], axis=0, keepdims=True),
                jnp.max(extra[:, 4] + extra[:, 5], axis=0, keepdims=True),
            ]
        )
        for k in range(blocks - 1):
            term = packed_ref[k, 0, pair, : PAIR // 2, :].astype(jnp.float32)
            state = jnp.where(k < place, decays[k] * state + term, state)
        state_ref[0, pair] = state
        wkv = inner_ref[:, lanes] + halves_dot(decayed_ref[:, lanes], spread(state), ((1,), (0,)))
        wkv_ref[:, lanes] = wkv
        normed, _ = norm_heads(wkv, PAIR // 2)
        normed = normed * gain_ref[:, lanes] + bias_ref[:, lanes]
        gate = gate_ref[0, :, lanes]
        mixer_ref[:, lanes] = (normed * gate * jax.nn.sigmoid(gate)).astype(jnp.bfloat16)


def put_rows(rows):
    row_at = iota((8, PAIR), 0)
    out = jnp.zeros((8, PAIR), jnp.float32)
    for at, row in enumerate(rows):
        out = jnp.where(row_at == at, row, out)
    return out


def back_join_kernel(grad_ref, wkv_ref, gate_ref, decayed_ref, gain_ref, bias_ref, *outs):
    grad_wkv_ref, grad_gate_ref, term_ref, sums_ref = outs
    for pair in range(WIDE // PAIR):
        lanes = slice(pair * PAIR, (pair + 1) * PAIR)
        grad, gate = grad_ref[:, lanes], gate_ref[0, :, lanes]
        gain = gain_ref[:, lanes]
        hat, scale = norm_heads(wkv_ref[:, lanes], PAIR // 2)
        sigmoid = jax.nn.sigmoid(gate)
        normed = hat * gain + bias_ref[:, lanes]
        grad_gate = grad * normed * sigmoid * (1.0 + gate * (1.0 - sigmoid))
        grad_gate_ref[:, lanes] = grad_gate.astype(jnp.bfloat16)
        grad_normed = grad * gate * sigmoid
        sums_ref[0, :, lanes] = put_rows(
            [
                jnp.sum(grad_normed * hat, axis=0, keepdims=True),
                jnp.sum(grad_normed, axis=0, keepdims=True),
            ]
        )
        q = grad_normed * gain
        each = 2.0 / PAIR
        grad_wkv = scale * (q - head_sum(q) * each - hat * (head_sum(q * hat) * each))
        grad_wkv_ref[:, lanes] = grad_wkv
        term_ref[0, pair] = compact(
            halves_dot(decayed_ref[:, lanes], grad_wkv, ((0,), (0,)))
        ).astype(jnp.bfloat16)


def back_inner_kernel(rkv_ref, log_ref, bonus_ref, grad_ref, state_ref, *outs):
    receive_ref, key_ref, value_ref, running_ref, sums_ref = outs
    for pair in range(WIDE // PAIR):
        lanes = slice(pair * PAIR, (pair + 1) * PAIR)
        receive, keys, values = (rkv_ref[n, :, lanes] for n in range(3))
        bonus, grad = bonus_ref[:, lanes], grad_ref[:, lanes]
        rates, total = running_decay(log_ref[:, lanes])
        rows, columns, scores, up, down, before = inner_scores(receive, keys, rates, total)
        length = receive.shape[0]
        first = first_head(values.shape)
        later = iota((length, length), 0) > iota((length, length), 1)
        low_values = values.astype(jnp.bfloat16)
        low_grad = grad.astype(jnp.bfloat16)
        grad_scores = [
            jnp.where(
                later, halves_dot(jnp.where(own, grad, 0.0), low_values, ((1,), (1,))), 0.0
            ).astype(jnp.bfloat16)
            for own in (first, jnp.logical_not(first))
        ]
        from_state = halves_dot(low_grad, spread(state_ref[0, pair]), ((1,), (1,)))
        far_receive = heads_apply(grad_scores, columns, 1) * up + jnp.exp(before) * from_state
        far_keys = heads_apply(grad_scores, rows, 0) * down
        meet = head_sum(grad * values)
        receive_ref[:, lanes] = (far_receive + bonus * keys * meet).astype(jnp.bfloat16)
        key_ref[:, lanes] = far_keys + bonus * receive * meet
        now = head_sum(receive * bonus * keys)
        value_ref[:, lanes] = heads_apply(scores, low_grad, 0) + now * grad
        moved = receive * far_receive
        moved = pltpu.roll(moved, length - 1, 0)
        moved = jnp.where(iota(moved.shape, 0) == length - 1, 0.0, moved)
        running_ref[:, lanes] = moved - keys * far_keys
        sums_ref[0, :, lanes] = put_rows([jnp.sum(receive * keys * meet, axis=0, keepdims=True)])


def back_outer_kernel(
    place_ref, kv_ref, log_ref, key_ref, value_ref, running_ref, state_ref, packed_ref, terms_ref, *outs
):
    grad_key_ref, grad_value_ref, grad_log_ref, start_ref, sums_ref = outs
    blocks = packed_ref.shape[0]
    place = place_ref[0]
    for pair in range(WIDE // PAIR):
        lanes = slice(pair * PAIR, (pair + 1) * PAIR)
        keys, values = kv_ref[1, :, lanes], kv_ref[2, :, lanes]
        rates, total = running_decay(log_ref[:, lanes])
        length = keys.shape[0]
        final = total[length - 1 : length]
        decays = block_decays(packed_ref[:, 0, pair, PAIR // 2 :, :])
        later = jnp.zeros((PAIR // 2, PAIR), jnp.float32)
        whole = jnp.zeros((PAIR // 2, PAIR), jnp.float32)
        for k in range(blocks - 1, -1, -1):
            term = terms_ref[k, 0, pair].astype(jnp.float32)
            later = jnp.where(k > place, decays[k] * later + term, later)
            whole = decays[k] * whole + term
        start_ref[0, 2 * pair] = whole[:, : PAIR // 2]
        start_ref[0, 2 * pair + 1] = whole[:, PAIR // 2 :]
        spread_later = spread(later).astype(jnp.bfloat16)
        fade = jnp.exp(final - total)
        far_keys = fade * halves_dot(values, spread_later, ((1,), (1,)))
        grad_key_ref[:, lanes] = (key_ref[:, lanes] + far_keys).astype(jnp.bfloat16)
        grad_value_ref[:, lanes] = (
            value_ref[:, lanes] + halves_dot(keys * fade, spread_later, ((1,), (0,)))
        ).astype(jnp.bfloat16)
        moved = keys * far_keys
        met = spread(state_ref[0, pair] * later)
        high, low = two_parts(met)
        ones = jnp.ones((8, PAIR), jnp.bfloat16)
        met_row = (halves_dot(ones, high, ((1,), (1,))) + halves_dot(ones, low, ((1,), (1,))))[:1]
        last = jnp.sum(moved, axis=0, keepdims=True) + jnp.exp(final) * met_row
        running = running_ref[:, lanes] - moved
        running = running + jnp.where(iota(running.shape, 0) == length - 1, last, 0.0)
        onward = iota((length, length), 0) <= iota((length, length), 1)
        grad_log = exact_dot(onward.astype(jnp.float32), running) * rates
        grad_log_ref[:, lanes] = grad_log
        sums_ref[0, :, lanes] = put_rows([jnp.sum(grad_log, axis=0, keepdims=True)])


class Recurrence:
    def __init__(self, sequences, length, columns):
        self.sequences, self.length, self.columns = sequences, length, columns
        self.grid = (sequences, columns // WIDE)
        self.pairs = columns // PAIR
        self.tokens = pl.BlockSpec((length, WIDE), lambda s, p: (s, p))
        self.row = pl.BlockSpec((1, WIDE), lambda s, p: (0, p))
        self.stack = pl.BlockSpec((3, length, WIDE), lambda s, p: (0, s, p))
        self.gate = pl.BlockSpec((1, length, WIDE), lambda s, p: (3, s, p))
        self.state = pl.BlockSpec((1, WIDE // PAIR, PAIR // 2, PAIR), lambda s, p: (s, p, 0, 0))
        self.heads = pl.BlockSpec(
            (1, 2 * WIDE // PAIR, PAIR // 2, PAIR // 2), lambda s, p: (s, p, 0, 0)
        )
        self.sums = pl.BlockSpec((1, 8, WIDE), lambda s, p: (s, 0, p))
        self.place = pl.BlockSpec(memory_space=pltpu.SMEM)

    def packed(self, blocks=None):
        rows = PAIR // 2 + EXTRA
        if blocks is None:
            return pl.BlockSpec((1, WIDE // PAIR, rows, PAIR), lambda s, p: (s, p, 0, 0))
        return pl.BlockSpec((blocks, 1, WIDE // PAIR, rows, PAIR), lambda s, p: (0, s, p, 0, 0))

    def terms(self, blocks):
        return pl.BlockSpec(
            (blocks, 1, WIDE // PAIR, PAIR // 2, PAIR), lambda s, p: (0, s, p, 0, 0)
        )

    def token_shape(self, kind):
        return jax.ShapeDtypeStruct((self.sequences * self.length, self.columns), kind)

    def state_shape(self, kind, rows=PAIR // 2):
        return jax.ShapeDtypeStruct((self.sequences, self.pairs, rows, PAIR), kind)

    def sums_shape(self):
        return jax.ShapeDtypeStruct((self.sequences, 8, self.columns), jnp.float32)

    def call(self, kernel, ins, outs, args, flops):
        size = sum(arg.size * arg.dtype.itemsize for arg in args)
        return pl.pallas_call(
            kernel,
            grid=self.grid,
            in_specs=ins,
            out_specs=[spec for spec, _ in outs],
            out_shape=[shape for _, shape in outs],
            compiler_params=pltpu.CompilerParams(vmem_limit_bytes=40 * 2**20),
            cost_estimate=pl.CostEstimate(
                flops=flops, bytes_accessed=size, transcendentals=6 * args[0].size
            ),
        )(*args)

    def totals(self, projected, log_rows):
        outs = [(self.packed(), self.state_shape(jnp.bfloat16, PAIR // 2 + EXTRA))]
        return self.call(
            totals_kernel, [self.stack, self.tokens], outs, (projected, log_rows), 10**9
        )[0]

    def inner(self, projected, log_rows, bonus):
        outs = [
            (self.tokens, self.token_shape(jnp.float32)),
            (self.tokens, self.token_shape(jnp.bfloat16)),
        ]
        ins = [self.stack, self.tokens, self.row]
        return self.call(inner_kernel, ins, outs, (projected, log_rows, bonus), 2 * 10**9)

    def join(self, place, inner, decayed, projected, packed, start, gain, bias):
        ins = [
            self.place,
            self.tokens,
            self.tokens,
            self.gate,
            self.packed(packed.shape[0]),
            self.heads,
            self.row,
            self.row,
        ]
        outs = [
            (self.tokens, self.token_shape(jnp.float32)),
            (self.tokens, self.token_shape(jnp.bfloat16)),
            (self.state, self.state_shape(jnp.float32)),
            (self.sums, self.sums_shape()),
        ]
        args = (place, inner, decayed, projected, packed, start, gain, bias)
        return self.call(join_kernel, ins, outs, args, 10**9)

    def back_join(self, grad, wkv, projected, decayed, gain, bias):
        ins = [self.tokens, self.tokens, self.gate, self.tokens, self.row, self.row]
        outs = [
            (self.tokens, self.token_shape(jnp.float32)),
            (self.tokens, self.token_shape(jnp.bfloat16)),
            (self.state, self.state_shape(jnp.bfloat16)),
            (self.sums, self.sums_shape()),
        ]
        args = (grad, wkv, projected, decayed, gain, bias)
        return self.call(back_join_kernel, ins, outs, args, 10**9)

    def back_inner(self, projected, log_rows, bonus, grad, state):
        ins = [self.stack, self.tokens, self.row, self.tokens, self.state]
        outs = [
            (self.tokens, self.token_shape(jnp.bfloat16)),
            (self.tokens, self.token_shape(jnp.float32)),
            (self.tokens, self.token_shape(jnp.float32)),
            (self.tokens, self.token_shape(jnp.float32)),
            (self.sums, self.sums_shape()),
        ]
        args = (projected, log_rows, bonus, grad, state)
        return self.call(back_inner_kernel, ins, outs, args, 4 * 10**9)

    def back_outer(self, place, projected, log_rows, keys, values, running, state, packed, terms):
        blocks = packed.shape[0]
        ins = [
            self.place,
            self.stack,
            self.tokens,
            self.tokens,
            self.tokens,
            self.tokens,
            self.state,
            self.packed(blocks),
            self.terms(blocks),
        ]
        outs = [
            (self.tokens, self.token_shape(jnp.bfloat16)),
            (self.tokens, self.token_shape(jnp.bfloat16)),
            (self.tokens, self.token_shape(jnp.float32)),
            (
                self.heads,
                jax.ShapeDtypeStruct(
                    (self.sequences, 2 * self.pairs, PAIR // 2, PAIR // 2), jnp.float32
                ),
            ),
            (self.sums, self.sums_shape()),
        ]
        args = (place, projected, log_rows, keys, values, running, state, packed, terms)
        return self.call(back_outer_kernel, ins, outs, args, 3 * 10**9)


BRANCHES = (3, 1, 2, 4)
STRIP = 512


def mix_back_kernel(
    x_ref,
    before_ref,
    grad_ref,
    log_ref,
    hidden_ref,
    decay_ref,
    proj_ref,
    coeff_ref,
    norm_ref,
    down_ref,
    up_ref,
    decay_down_ref,
    decay_up_ref,
    block_ref,
    edge_ref,
    all_ref,
    grad_decay_up_ref,
    hat_ref,
    grad_diff_ref,
    grad_all_ref,
):
    together, length, columns = x_ref.shape
    tokens = together * length
    ranks = up_ref.shape[0] // 5
    up_rows, decay_rows = up_ref.shape[0], decay_down_ref.shape[0]
    sums_ref = all_ref.at[0:8]
    grad_up_ref = all_ref.at[16 : 16 + up_rows]
    grad_down_ref = all_ref.at[16 + up_rows : 16 + 2 * up_rows]
    grad_decay_down_ref = all_ref.at[16 + 2 * up_rows : 16 + 2 * up_rows + decay_rows]
    strips = columns // STRIP
    low = jnp.bfloat16

    @pl.when(pl.program_id(0) == 0)
    def _():
        for ref in (all_ref, grad_decay_up_ref):
            ref[...] = jnp.zeros_like(ref)

    x = x_ref[...].reshape(tokens, columns).astype(jnp.float32)
    mean = jnp.mean(x, axis=-1, keepdims=True)
    variance = jnp.mean((x - mean) * (x - mean), axis=-1, keepdims=True)
    scale = lax.rsqrt(variance + NORM_EPS)
    hidden, hidden_decay = hidden_ref[...], decay_ref[...]
    low_hidden, low_decay = hidden.astype(low), hidden_decay.astype(low)
    grad_log = log_ref[...].astype(low)
    grad_decay = halves_dot(grad_log, decay_up_ref[...], ((1,), (1,)))
    grad_decay = grad_decay * (1.0 - hidden_decay * hidden_decay)
    low_grad_decay = grad_decay.astype(low)
    grad_decay_up_ref[...] += halves_dot(low_decay, grad_log, ((0,), (0,)))

    def strip_of(strip):
        return pl.ds(pl.multiple_of(strip * STRIP, STRIP), STRIP)

    def normed_and_diff(at, hat):
        normed = hat * norm_ref[0:1, at] + norm_ref[1:2, at]
        earlier = pltpu.roll(normed, 1, 0)
        for k in range(together):
            earlier = jnp.where(
                iota(normed.shape, 0) == k * length, before_ref[k, :, at], earlier
            )
        return normed, earlier - normed

    def first(strip, grad_pre):
        at = strip_of(strip)
        hat = (x_ref[:, :, at].reshape(tokens, STRIP).astype(jnp.float32) - mean) * scale
        hat_ref[:, at] = hat
        normed, diff = normed_and_diff(at, hat)
        grad_diff = jnp.zeros_like(diff)
        grad_all = jnp.zeros_like(diff)
        parts = []
        for branch in range(5):
            rows = slice(branch * ranks, (branch + 1) * ranks)
            up = up_ref[rows, at]
            weight = coeff_ref[1 + branch : 2 + branch, at] + halves_dot(
                low_hidden[:, rows], up, ((1,), (0,))
            )
            if branch == 0:
                mixed = normed + diff * weight
                grad_decay_down_ref[:, at] += halves_dot(low_grad_decay, mixed, ((0,), (0,)))
                grad = halves_dot(low_grad_decay, decay_down_ref[:, at], ((1,), (0,)))
            else:
                n = BRANCHES.index(branch)
                grad = halves_dot(grad_ref[n], proj_ref[n, at, :], ((1,), (1,)))
            grad_all += grad
            grad_diff += grad * weight
            moved = grad * diff
            sums_ref[1 + branch : 2 + branch, at] += jnp.sum(moved, axis=0, keepdims=True)
            moved = moved.astype(low)
            grad_up_ref[rows, at] += halves_dot(low_hidden[:, rows], moved, ((0,), (0,)))
            parts.append(halves_dot(moved, up, ((1,), (1,))))
        grad_diff_ref[:, at] = grad_diff
        grad_all_ref[:, at] = grad_all
        return grad_pre + jnp.concatenate(parts, axis=1)

    grad_pre = lax.fori_loop(0, strips, first, jnp.zeros(hidden.shape, jnp.float32))
    grad_pre = (grad_pre * (1.0 - hidden * hidden)).astype(low)

    def second(strip, carry):
        total, against = carry
        at = strip_of(strip)
        hat = hat_ref[:, at]
        normed, diff = normed_and_diff(at, hat)
        coeff = coeff_ref[0:1, at]
        grad_base = halves_dot(grad_pre, down_ref[:, at], ((1,), (0,)))
        grad_down_ref[:, at] += halves_dot(grad_pre, normed + diff * coeff, ((0,), (0,)))
        sums_ref[0:1, at] += jnp.sum(grad_base * diff, axis=0, keepdims=True)
        grad_diff = grad_diff_ref[:, at] + grad_base * coeff
        onward = pltpu.roll(grad_diff, tokens - 1, 0)
        for k in range(together):
            edge_ref[k, :, at] = grad_diff[k * length : k * length + 1]
            onward = jnp.where(iota(onward.shape, 0) == (k + 1) * length - 1, 0.0, onward)
        grad = grad_base + grad_all_ref[:, at] - grad_diff + onward
        sums_ref[6:7, at] += jnp.sum(grad * hat, axis=0, keepdims=True)
        sums_ref[7:8, at] += jnp.sum(grad, axis=0, keepdims=True)
        q = grad * norm_ref[0:1, at]
        grad_all_ref[:, at] = q
        total += jnp.sum(q, axis=-1, keepdims=True)
        against += jnp.sum(q * hat, axis=-1, keepdims=True)
        return total, against

    zero = jnp.zeros((tokens, 1), jnp.float32)
    total, against = lax.fori_loop(0, strips, second, (zero, zero))
    total, against = total * (1.0 / columns), against * (1.0 / columns)

    def third(strip, carry):
        at = strip_of(strip)
        block = scale * (grad_all_ref[:, at] - total - hat_ref[:, at] * against)
        block_ref[:, :, at] = block.reshape(together, length, STRIP)
        return carry

    lax.fori_loop(0, strips, third, 0)


def mix_back(
    block_input,
    before,
    grad_proj,
    grad_log,
    hidden,
    hidden_decay,
    projections,
    coeffs,
    norm,
    down,
    up,
    decay_down,
    decay_up,
    sum_rows,
):
    sequences, length, columns = block_input.shape
    heads = grad_proj.shape[-1]
    ranks, decay_ranks = up.shape[0], decay_up.shape[0]

    def whole(array):
        return pl.BlockSpec(array.shape, lambda s: (0,) * array.ndim)

    def kept(shape):
        return pl.BlockSpec(shape, lambda s: (0, 0)), jax.ShapeDtypeStruct(shape, jnp.float32)

    together = 2 - sequences % 2
    tokens = together * length
    block = pl.BlockSpec((together, length, columns), lambda s: (s, 0, 0))
    edge = pl.BlockSpec((together, 1, columns), lambda s: (s, 0, 0))
    outs = [
        (block, jax.ShapeDtypeStruct(block_input.shape, jnp.float32)),
        (edge, jax.ShapeDtypeStruct((sequences, 1, columns), jnp.float32)),
        kept((sum_rows, columns)),
        kept((decay_ranks, heads)),
    ]
    args = (
        block_input,
        before,
        grad_proj,
        grad_log,
        hidden,
        hidden_decay,
        projections,
        coeffs,
        norm,
        down,
        up,
        decay_down,
        decay_up,
    )
    return pl.pallas_call(
        mix_back_kernel,
        grid=(sequences // together,),
        in_specs=[
            block,
            edge,
            pl.BlockSpec((4, tokens, heads), lambda s: (0, s, 0)),
            pl.BlockSpec((tokens, heads), lambda s: (s, 0)),
            pl.BlockSpec((tokens, hidden.shape[1]), lambda s: (s, 0)),
            pl.BlockSpec((tokens, decay_ranks), lambda s: (s, 0)),
            pl.BlockSpec(projections.shape, lambda s: (0, 0, 0), pipeline_mode=pl.Buffered(1)),
        ]
        + [whole(array) for array in args[7:]],
        out_specs=[spec for spec, _ in outs],
        out_shape=[shape for _, shape in outs],
        scratch_shapes=[pltpu.VMEM((tokens, columns), jnp.float32)] * 3,
        compiler_params=pltpu.CompilerParams(vmem_limit_bytes=58 * 2**20),
        cost_estimate=pl.CostEstimate(
            flops=10**10, bytes_accessed=40 * 2**20, transcendentals=0
        ),
    )(*args)


def other_half(block):
    return lax.ppermute(block, "tp", [(0, 1), (1, 0)])


CORES = 2


def ring_places(dp_size, seq_size):
    per_row = seq_size // CORES
    count = dp_size * per_row

    def chip(position):
        position = lax.rem(position + 2 * count, count)
        row = lax.div(position, per_row)
        column = lax.rem(position, per_row)
        column = jnp.where(lax.rem(row, 2) == 0, column, per_row - 1 - column)
        return row, column

    def own():
        row, column = lax.axis_index("dp"), lax.div(lax.axis_index("seq"), CORES)
        return row * per_row + jnp.where(lax.rem(row, 2) == 0, column, per_row - 1 - column)

    return count, chip, own


def cut_rings(widths, rings):
    each = sum(widths) // rings
    runs, product, column = [], 0, 0
    for _ in range(rings):
        run, left = [], each
        while left:
            take = min(left, widths[product] - column)
            run.append((product, column, take))
            left, column = left - take, column + take
            if column == widths[product]:
                product, column = product + 1, 0
        runs.append(run)
    return runs


def ring_kernel(dp_size, seq_size, rows, widths, runs, places, operands, *refs):
    products = len(widths)
    lefts = [(refs[left], lead) for left, _, lead in places]
    rights = [(None if right is None else refs[right], lead) for _, right, lead in places]
    sent_ref, received_ref = refs[operands - 1], refs[operands + products]
    totals, refs = refs[operands : operands + products], refs[operands + products + 1 :]
    rings = len(runs)
    mine, pair_out, pair_in, ring_out, ring_in = [
        refs[k * rings : (k + 1) * rings] for k in range(5)
    ]
    pair_send, pair_recv, pair_free, ring_send, ring_recv, ring_free, half_send, half_recv = refs[
        5 * rings :
    ]
    count, chip, own = ring_places(dp_size, seq_size)
    position, core = own(), lax.rem(lax.axis_index("seq"), CORES)

    def device(place, which):
        row, column = chip(place)
        return {"dp": row, "seq": column * CORES + which}

    sibling = device(position, 1 - core)
    after, before = device(position + 1, core), device(position - 1, core)
    barrier = pltpu.get_barrier_semaphore()
    partner = {"tp": 1 - lax.axis_index("tp")}
    for other in (sibling, after, before, partner):
        pl.semaphore_signal(barrier, inc=1, device_id=other, device_id_type=pl.DeviceIdType.MESH)
    pl.semaphore_wait(barrier, 4)
    halves = pltpu.make_async_remote_copy(
        src_ref=sent_ref,
        dst_ref=received_ref,
        send_sem=half_send,
        recv_sem=half_recv,
        device_id=partner,
        device_id_type=pl.DeviceIdType.MESH,
    )
    halves.start()

    def pair_copy(ring):
        return pltpu.make_async_remote_copy(
            src_ref=pair_out[ring],
            dst_ref=pair_in[ring],
            send_sem=pair_send.at[ring],
            recv_sem=pair_recv.at[ring],
            device_id=sibling,
            device_id_type=pl.DeviceIdType.MESH,
        )

    def ring_copy(ring, slot):
        return pltpu.make_async_remote_copy(
            src_ref=ring_out[ring].at[slot],
            dst_ref=ring_in[ring].at[slot],
            send_sem=ring_send.at[ring, slot],
            recv_sem=ring_recv.at[ring, slot],
            device_id=after if ring % 2 == 0 else before,
            device_id_type=pl.DeviceIdType.MESH,
        )

    def part(ring, place, which, put):
        row, column = chip(place)
        start = (row * seq_size + column * CORES + which) * rows
        start = pl.multiple_of(start, rows)
        at = 0
        for product, first, wide in runs[ring]:
            ref, lead = lefts[product]
            if rights[product][0] is None:
                if rows % 128 == 0:
                    put(at, wide, ref[pl.ds(first, wide), pl.ds(start, rows)].T)
                else:
                    put(at, wide, ref[pl.ds(start, rows), pl.ds(first, wide)])
                at += wide
                continue
            if rows % 128 == 0:
                left = ref[(*lead, slice(None), pl.ds(start, rows))]
            else:
                left = ref[(*lead, pl.ds(start, rows), slice(None))]
            ref, lead = rights[product]
            right = ref[(*lead, slice(None), pl.ds(first, wide))]
            put(
                at,
                wide,
                lax.dot_general(
                    left,
                    right,
                    (((0 if rows % 128 == 0 else 1,), (0,)), ((), ())),
                    preferred_element_type=jnp.float32,
                ),
            )
            at += wide

    def turn(step, carry):
        slot = lax.rem(step, 2)
        last = 1 - slot
        for ring in range(rings):
            place = position - 1 - step if ring % 2 == 0 else position + 1 + step

            @pl.when(step >= 1)
            def _():
                pair_copy(ring).wait_send()

            def put_out(at, wide, value):
                pair_out[ring][:, at : at + wide] = value.astype(jnp.bfloat16)

            part(ring, place, 1 - core, put_out)

            @pl.when(step >= 1)
            def _():
                pl.semaphore_wait(pair_free.at[ring], 1)

            pair_copy(ring).start()

            def put_mine(at, wide, value):
                mine[ring][:, at : at + wide] = value

            part(ring, place, core, put_mine)
        for ring in range(rings):
            source = before if ring % 2 == 0 else after
            pair_copy(ring).wait_recv()

            @pl.when(step == 0)
            def _():
                ring_out[ring][slot] = (
                    mine[ring][...] + pair_in[ring][...].astype(jnp.float32)
                ).astype(jnp.bfloat16)

            @pl.when(step >= 1)
            def _():
                ring_copy(ring, last).wait_recv()

            @pl.when(jnp.logical_and(step >= 1, step < count - 1))
            def _():
                @pl.when(step >= 2)
                def _():
                    ring_copy(ring, slot).wait_send()

                ring_out[ring][slot] = (
                    mine[ring][...]
                    + pair_in[ring][...].astype(jnp.float32)
                    + ring_in[ring][last].astype(jnp.float32)
                ).astype(jnp.bfloat16)

            @pl.when(step == count - 1)
            def _():
                at = 0
                for product, first, wide in runs[ring]:
                    totals[product][:, first : first + wide] = (
                        mine[ring][:, at : at + wide]
                        + pair_in[ring][:, at : at + wide].astype(jnp.float32)
                        + ring_in[ring][last, :, at : at + wide].astype(jnp.float32)
                    )
                    at += wide

            @pl.when(step < count - 1)
            def _():
                @pl.when(step >= 2)
                def _():
                    pl.semaphore_wait(ring_free.at[ring], 1)

                ring_copy(ring, slot).start()
                pl.semaphore_signal(
                    pair_free.at[ring],
                    inc=1,
                    device_id=sibling,
                    device_id_type=pl.DeviceIdType.MESH,
                )

            @pl.when(jnp.logical_and(step >= 1, step < count - 2))
            def _():
                pl.semaphore_signal(
                    ring_free.at[ring],
                    inc=1,
                    device_id=source,
                    device_id_type=pl.DeviceIdType.MESH,
                )

        return carry

    lax.fori_loop(0, count, turn, 0)
    for ring in range(rings):
        pair_copy(ring).wait_send()
        for step in (count - 3, count - 2):
            ring_copy(ring, step % 2).wait_send()
    halves.wait()


def ring_sums(pairs, given, sent, sizes, collective_id):
    dp_size, seq_size = sizes
    rows = pairs[0][0].shape[-1] // (dp_size * seq_size)
    tokens = pairs[0][1].shape[-2]
    operands, known, places = [], {}, []

    def place_of(array, turned):
        if id(array) not in known:
            known[id(array)] = len(operands)
            operands.append(jnp.swapaxes(array, -1, -2) if turned else array)
        return known[id(array)]

    for left, right, lead in pairs:
        places.append((place_of(left, rows % 128 != 0), place_of(right, False), lead))
    places.append((place_of(given, rows % 128 != 0), None, ()))
    operands.append(sent)
    widths = [right.shape[-1] for _, right, _ in pairs] + [given.shape[0]]
    rings = 4
    runs = cut_rings(widths, rings)
    each = sum(widths) // rings
    low = jnp.bfloat16
    return pl.pallas_call(
        functools.partial(
            ring_kernel, dp_size, seq_size, rows, widths, runs, places, len(operands)
        ),
        out_shape=[jax.ShapeDtypeStruct((rows, wide), jnp.float32) for wide in widths]
        + [jax.ShapeDtypeStruct(sent.shape, sent.dtype)],
        in_specs=[pl.BlockSpec(memory_space=pltpu.VMEM)] * len(operands),
        out_specs=[pl.BlockSpec(memory_space=pltpu.VMEM)] * (len(widths) + 1),
        scratch_shapes=[pltpu.VMEM((rows, each), jnp.float32)] * rings
        + [pltpu.VMEM((rows, each), low)] * (2 * rings)
        + [pltpu.VMEM((2, rows, each), low)] * (2 * rings)
        + [
            pltpu.SemaphoreType.DMA((rings,)),
            pltpu.SemaphoreType.DMA((rings,)),
            pltpu.SemaphoreType.REGULAR((rings,)),
            pltpu.SemaphoreType.DMA((rings, 2)),
            pltpu.SemaphoreType.DMA((rings, 2)),
            pltpu.SemaphoreType.REGULAR((rings,)),
            pltpu.SemaphoreType.DMA(()),
            pltpu.SemaphoreType.DMA(()),
        ],
        compiler_params=pltpu.CompilerParams(
            collective_id=collective_id, has_side_effects=True, vmem_limit_bytes=60 * 2**20
        ),
        cost_estimate=pl.CostEstimate(
            flops=2 * tokens * rows * dp_size * seq_size * sum(widths),
            bytes_accessed=2 * tokens * (2048 * len(pairs) + sum(widths)),
            transcendentals=0,
        ),
    )(*operands)


def gather_kernel(
    dp_size,
    seq_size,
    small_ref,
    proj_ref,
    out_ref,
    small_all,
    proj_all,
    out_all,
    keep,
    send,
    recv,
    pair_send,
    pair_recv,
):
    width = small_ref.shape[1]
    count, chip, own = ring_places(dp_size, seq_size)
    position, core = own(), lax.rem(lax.axis_index("seq"), CORES)
    far = count // 2
    hops = [(far, far - 1), (far, far - 1), (far - 1, far), (far - 1, far)]
    halfway = proj_ref.shape[0] // 2

    def device(place, which):
        row, column = chip(place)
        return {"dp": row, "seq": column * CORES + which}

    def regions(place, which):
        row, column = chip(place)
        start = (row * seq_size + column * CORES + which) * width
        at = pl.ds(pl.multiple_of(start, width), width)
        return [
            small_all.at[:, at],
            proj_all.at[:halfway, at, :],
            proj_all.at[halfway:, at, :],
            out_all.at[:, at],
        ]

    sources = [small_ref, proj_ref.at[:halfway], proj_ref.at[halfway:], out_ref]
    sibling = device(position, 1 - core)
    ways = [device(position + 1, core), device(position - 1, core)]
    barrier = pltpu.get_barrier_semaphore()
    for other in [sibling] + ways:
        pl.semaphore_signal(barrier, inc=1, device_id=other, device_id_type=pl.DeviceIdType.MESH)
    pl.semaphore_wait(barrier, 3)

    def place_of(way, hop):
        return position - hop if way == 0 else position + hop

    def onward(part, way, hop):
        at = regions(place_of(way, hop - 1), core)[part]
        return pltpu.make_async_remote_copy(
            src_ref=sources[part] if hop == 1 else at,
            dst_ref=at,
            send_sem=send.at[part, way, hop - 1],
            recv_sem=recv.at[part, way, hop - 1],
            device_id=ways[way],
            device_id_type=pl.DeviceIdType.MESH,
        )

    def across(part, way, hop):
        at = regions(place_of(way, hop), core)[part]
        return pltpu.make_async_remote_copy(
            src_ref=sources[part] if hop == 0 else at,
            dst_ref=at,
            send_sem=pair_send.at[part, way, hop],
            recv_sem=pair_recv.at[part, way, hop],
            device_id=sibling,
            device_id_type=pl.DeviceIdType.MESH,
        )

    parts = range(len(sources))
    kept = []
    for part in parts:
        for way in range(2):
            onward(part, way, 1).start()
        across(part, 0, 0).start()
        copy = pltpu.make_async_copy(
            sources[part], regions(position, core)[part], keep.at[part]
        )
        copy.start()
        kept.append(copy)
    for hop in range(1, far + 1):
        for part in parts:
            for way in range(2):
                if hop <= hops[part][way]:
                    onward(part, way, hop).wait_recv()
                    if hop < hops[part][way]:
                        onward(part, way, hop + 1).start()
                    across(part, way, hop).start()
    for part in parts:
        kept[part].wait()
        across(part, 0, 0).wait()
        for way in range(2):
            for hop in range(1, hops[part][way] + 1):
                onward(part, way, hop).wait_send()
                across(part, way, hop).wait()


def gather_weights(small, proj, out, sizes, collective_id):
    if small.shape[1] % 128:
        return (
            lax.all_gather(small, ("dp", "seq"), axis=1, tiled=True),
            lax.all_gather(proj, ("dp", "seq"), axis=1, tiled=True),
            lax.all_gather(out, ("dp", "seq"), axis=1, tiled=True),
        )
    dp_size, seq_size = sizes
    every = dp_size * seq_size
    far = every // CORES // 2
    rows, width = small.shape
    shapes = [
        (rows, width * every),
        (proj.shape[0], width * every, proj.shape[2]),
        (out.shape[0], width * every),
    ]
    return pl.pallas_call(
        functools.partial(gather_kernel, dp_size, seq_size),
        out_shape=[jax.ShapeDtypeStruct(shape, small.dtype) for shape in shapes],
        in_specs=[pl.BlockSpec(memory_space=pl.ANY)] * 3,
        out_specs=[pl.BlockSpec(memory_space=pl.ANY)] * 3,
        scratch_shapes=[pltpu.SemaphoreType.DMA((4,))]
        + [pltpu.SemaphoreType.DMA((4, 2, far))] * 2
        + [pltpu.SemaphoreType.DMA((4, 2, far + 1))] * 2,
        compiler_params=pltpu.CompilerParams(collective_id=collective_id, has_side_effects=True),
    )(small, proj, out)


def mix_kernel(
    x_ref,
    before_ref,
    coeff_ref,
    norm_ref,
    down_ref,
    up_ref,
    decay_down_ref,
    decay_up_ref,
    base_ref,
    mixed_ref,
    hidden_ref,
    decay_ref,
    log_ref,
):
    length, columns = x_ref.shape[1:]
    ranks = up_ref.shape[0] // 5
    strips = columns // STRIP
    x = x_ref[0].astype(jnp.float32)
    mean = jnp.mean(x, axis=-1, keepdims=True)
    variance = jnp.mean((x - mean) * (x - mean), axis=-1, keepdims=True)
    scale = lax.rsqrt(variance + NORM_EPS)

    def normed_and_diff(strip):
        at = pl.ds(pl.multiple_of(strip * STRIP, STRIP), STRIP)
        hat = (x_ref[0, :, at].astype(jnp.float32) - mean) * scale
        normed = hat * norm_ref[0:1, at] + norm_ref[1:2, at]
        earlier = pltpu.roll(normed, 1, 0)
        earlier = jnp.where(iota(normed.shape, 0) == 0, before_ref[0, :, at], earlier)
        return at, normed, earlier - normed

    def first(strip, hidden):
        at, normed, diff = normed_and_diff(strip)
        return hidden + halves_dot(normed + diff * coeff_ref[0:1, at], down_ref[:, at], ((1,), (1,)))

    hidden = lax.fori_loop(0, strips, first, jnp.zeros(hidden_ref.shape, jnp.float32))
    hidden = jnp.tanh(hidden)
    hidden_ref[...] = hidden
    hidden = hidden.astype(jnp.bfloat16)

    def second(strip, decay):
        at, normed, diff = normed_and_diff(strip)
        for branch in range(5):
            rows = slice(branch * ranks, (branch + 1) * ranks)
            weight = coeff_ref[1 + branch : 2 + branch, at] + halves_dot(
                hidden[:, rows], up_ref[rows, at], ((1,), (0,))
            )
            mixed = (normed + diff * weight).astype(jnp.bfloat16)
            if branch == 0:
                decay += halves_dot(mixed, decay_down_ref[:, at], ((1,), (1,)))
            else:
                mixed_ref[BRANCHES.index(branch), :, at] = mixed
        return decay

    decay = lax.fori_loop(0, strips, second, jnp.zeros(decay_ref.shape, jnp.float32))
    decay = jnp.tanh(decay)
    decay_ref[...] = decay
    log_ref[...] = base_ref[...] + halves_dot(decay, decay_up_ref[...], ((1,), (0,)))


def mix_forward(block_input, before, coeffs, norm, down, up, decay_down, decay_up, base):
    sequences, length, columns = block_input.shape
    heads, tokens = decay_up.shape[1], sequences * length
    args = (block_input, before, coeffs, norm, down, up, decay_down, decay_up, base)

    def rows(wide):
        return pl.BlockSpec((length, wide), lambda s: (s, 0))

    outs = [(down.shape[0], jnp.float32), (decay_up.shape[0], jnp.float32), (heads, jnp.float32)]
    return pl.pallas_call(
        mix_kernel,
        grid=(sequences,),
        in_specs=[
            pl.BlockSpec((1, length, columns), lambda s: (s, 0, 0)),
            pl.BlockSpec((1, 1, columns), lambda s: (s, 0, 0)),
        ]
        + [pl.BlockSpec(array.shape, lambda s: (0, 0)) for array in args[2:]],
        out_specs=[pl.BlockSpec((4, length, columns), lambda s: (0, s, 0))]
        + [rows(wide) for wide, _ in outs],
        out_shape=[jax.ShapeDtypeStruct((4, tokens, columns), jnp.bfloat16)]
        + [jax.ShapeDtypeStruct((tokens, wide), kind) for wide, kind in outs],
        compiler_params=pltpu.CompilerParams(vmem_limit_bytes=40 * 2**20),
        cost_estimate=pl.CostEstimate(
            flops=2 * 10**9, bytes_accessed=16 * 2**20, transcendentals=10**5
        ),
    )(*args)


def per_device(
    block_input,
    initial_state,
    norm_gains,
    norm_biases,
    mixing_coefficients,
    mix_down,
    mixing_up_weight,
    decay_down,
    decay_up,
    proj_weights,
    out_weight,
    time_decay,
    time_first,
    group_gain,
    group_bias,
    channel_key,
    channel_value,
    channel_recept,
    out_grad,
):
    blocks, place = lax.axis_size("seq"), lax.axis_index("seq")
    half = lax.axis_index("tp")
    sizes = (lax.axis_size("dp"), blocks)
    width = norm_gains.shape[1]
    heads_here, each = time_decay.shape
    head_size = initial_state.shape[-1]
    head_cols = heads_here * head_size
    ranks, decay_ranks = mix_down.shape[1], decay_down.shape[1]

    def narrow_rows(part):
        part = part.reshape(-1, heads_here * each)
        return jnp.pad(part, ((0, 0), (0, width - part.shape[1])))

    up_at = 16
    down_at = up_at + ranks
    decay_at = down_at + ranks
    narrow_at = decay_at + decay_ranks
    top_rows = jnp.concatenate(
        [norm_gains, norm_biases, mixing_coefficients, jnp.zeros((4, width), jnp.bfloat16)]
    )
    low_rows = jnp.concatenate(
        [
            narrow_rows(time_decay),
            narrow_rows(time_first),
            narrow_rows(group_gain),
            narrow_rows(group_bias),
            jnp.zeros((12, width), jnp.bfloat16),
        ]
    )
    top_rows, low_rows = lax.optimization_barrier((top_rows, low_rows))
    own_rows = jnp.concatenate(
        [
            top_rows,
            mixing_up_weight,
            mix_down.T,
            decay_down.T,
            narrow_rows(decay_up),
            low_rows,
        ]
    )
    spread_rows, projections, out_proj = gather_weights(
        own_rows, proj_weights, out_weight, sizes, 1
    )
    channel = jnp.arange(head_cols)
    lane = (channel % head_size) // each * width + channel // head_size * each + channel % each
    choose = (jnp.arange(spread_rows.shape[1])[:, None] == lane[None, :]).astype(jnp.bfloat16)
    narrow_all = jnp.dot(
        spread_rows[narrow_at:], choose, preferred_element_type=jnp.float32
    )
    gains_all, biases_all = (spread_rows[k : k + 2].astype(jnp.float32) for k in (0, 2))
    shift_coefficient = spread_rows[4:12].astype(jnp.float32)
    lowrank_up = spread_rows[up_at:down_at]
    lowrank_down = spread_rows[down_at:decay_at]
    decay_projection = spread_rows[decay_at:narrow_at]
    lift_rows = narrow_all[:decay_ranks].astype(jnp.bfloat16)
    base_row, bonus, group_scale, group_shift = (
        narrow_all[decay_ranks + k : decay_ranks + k + 1] for k in range(4)
    )
    seq_count, length, feature_columns = block_input.shape
    tokens = seq_count * length
    own_cols = channel_recept.shape[1]

    def both_halves(own):
        other = other_half(own)
        low = jnp.where(half == 0, own, other)
        high = jnp.where(half == 0, other, own)
        return jnp.concatenate([low, high], axis=-1)

    def own_half(rows):
        return lax.dynamic_slice_in_dim(rows, half * own_cols, own_cols, rows.ndim - 1)

    def add_last(rows, last):
        at_last = jnp.arange(length)[None, :, None] == length - 1
        return rows + jnp.where(at_last, last[:, None, :], 0.0)

    full_out = both_halves(out_grad)
    last_input = block_input[:, -1].astype(jnp.float32)
    last_one = layer_norm(last_input, gains_all[0], biases_all[0])
    preceding_first = from_behind(last_one.astype(jnp.bfloat16), "seq", 1)
    preceding_first = preceding_first.astype(jnp.float32)[:, None, :]
    norm_one = jnp.stack([gains_all[0], biases_all[0]])
    stacked, hidden_mixture, hidden_decay, log_flat = mix_forward(
        block_input,
        preceding_first,
        shift_coefficient,
        norm_one,
        lowrank_down,
        lowrank_up,
        decay_projection,
        lift_rows,
        base_row,
    )
    projected = jnp.einsum("ntd,nde->nte", stacked, projections, preferred_element_type=jnp.float32)
    recurrence = Recurrence(seq_count, length, head_cols)
    where_here = place.astype(jnp.int32).reshape(1)
    all_packed = lax.all_gather(recurrence.totals(projected, log_flat), "seq")
    inner, decayed = recurrence.inner(projected, log_flat, bonus)
    inner, full_out = lax.optimization_barrier((inner, full_out))
    wkv, mixer_rows, state, decay_range = recurrence.join(
        where_here,
        inner,
        decayed,
        projected,
        all_packed,
        initial_state,
        group_scale,
        group_shift,
    )
    mixer_in = mixer_rows.reshape(seq_count, length, head_cols)
    decay_range = decay_range[:, :2].reshape(seq_count, 2, heads_here, head_size)
    total_least = jnp.min(decay_range[:, 0], axis=-1)
    total_most = jnp.max(decay_range[:, 1], axis=-1)
    mixer_part = jnp.einsum("std,de->ste", mixer_in, out_proj, preferred_element_type=jnp.float32)
    late_input, mixer_part = lax.optimization_barrier((block_input, mixer_part))
    residual = (
        late_input.astype(jnp.float32) + mixer_part + other_half(mixer_part.astype(jnp.bfloat16)).astype(jnp.float32)
    )
    normed_two, norm_two_back = jax.vjp(layer_norm, residual, gains_all[1], biases_all[1])
    prev_two = from_behind(normed_two[:, -1, :].astype(jnp.bfloat16), "seq", 1).astype(jnp.float32)
    chan_key, chan_recept = channel_mix(normed_two, prev_two, shift_coefficient)
    chan_key_b = chan_key.astype(jnp.bfloat16)
    chan_recept_b = chan_recept.astype(jnp.bfloat16)
    recept_pre = jnp.einsum(
        "std,de->ste", chan_recept_b, channel_recept, preferred_element_type=jnp.float32
    )
    gate_chan = jax.nn.sigmoid(recept_pre)
    grad_out = out_grad.astype(jnp.float32)
    grad_value = (grad_out * gate_chan).astype(jnp.bfloat16)
    chan_key_b, grad_value = lax.optimization_barrier((chan_key_b, grad_value))
    full_value = both_halves(grad_value)
    key_pre = jnp.einsum("std,df->stf", chan_key_b, channel_key, preferred_element_type=jnp.float32)
    hidden = jnp.square(jnp.maximum(key_pre, 0.0)).astype(jnp.bfloat16)
    own_value, sent_value = (
        lax.dynamic_slice_in_dim(channel_value, which * own_cols, own_cols, 1)
        for which in (half, 1 - half)
    )
    sent_part = jnp.einsum("stf,fd->std", hidden, sent_value, preferred_element_type=jnp.float32)
    hidden, sent_part = lax.optimization_barrier((hidden, sent_part.astype(jnp.bfloat16)))
    other_part = other_half(sent_part).astype(jnp.float32)
    own_part = jnp.einsum("stf,fd->std", hidden, own_value, preferred_element_type=jnp.float32)

    def weight_terms(left, right):
        return jnp.einsum(
            "td,tf->df", left, right, preferred_element_type=jnp.float32
        ).astype(jnp.bfloat16)

    def scattered(whole):
        return lax.psum_scatter(whole, ("dp", "seq"), scatter_dimension=0, tiled=True).astype(
            jnp.float32
        )

    flat_value, flat_hidden = full_value.reshape(tokens, -1), hidden.reshape(tokens, -1)
    value_cut = flat_hidden.shape[1] * 5 // 7
    full_value, own_part, value_whole = lax.optimization_barrier(
        (full_value, own_part, weight_terms(flat_value, flat_hidden[:, :value_cut]))
    )
    value_sum = scattered(value_whole)
    grad_hidden = jnp.einsum(
        "std,fd->stf", full_value, channel_value, preferred_element_type=jnp.float32
    )
    grad_key = (grad_hidden * 2.0 * jnp.maximum(key_pre, 0.0)).astype(jnp.bfloat16)
    grad_key, own_part = lax.optimization_barrier((grad_key, own_part))
    kv_rows = own_part + other_part
    output = (own_half(residual) + gate_chan * kv_rows).astype(jnp.bfloat16)
    grad_recept = (grad_out * kv_rows * gate_chan * (1.0 - gate_chan)).astype(jnp.bfloat16)
    grad_normed_two, grad_coeffs_chan = [], []
    for k in range(2):
        at = slice(k * own_cols, (k + 1) * own_cols)
        part_key = jnp.einsum(
            "stf,df->std", grad_key, channel_key[at], preferred_element_type=jnp.float32
        )
        part_recept = jnp.einsum(
            "ste,de->std", grad_recept, channel_recept[at], preferred_element_type=jnp.float32
        )
        _, chan_back = jax.vjp(
            channel_mix, normed_two[..., at], prev_two[..., at], shift_coefficient[:, at]
        )
        part_two, part_prev_two, coeffs = chan_back((part_key, part_recept))
        grad_coeffs_chan.append(coeffs)
        sent_two = part_two.astype(jnp.bfloat16)
        grad_key, sent_two = lax.optimization_barrier((grad_key, sent_two))
        other_two = other_half(sent_two).astype(jnp.float32)
        from_next_two = from_behind(for_sending(part_prev_two), "seq", -1)
        from_next_two = from_next_two.astype(jnp.float32) + other_half(from_next_two).astype(
            jnp.float32
        )
        grad_normed_two.append(add_last(part_two + other_two, from_next_two))
    grad_coeffs_chan = jnp.concatenate(grad_coeffs_chan, axis=1)
    grad_normed_two = jnp.concatenate(grad_normed_two, axis=-1)
    flat_key, flat_grad_key = chan_key_b.reshape(tokens, -1), grad_key.reshape(tokens, -1)
    key_cut = flat_grad_key.shape[1] * 5 // 7
    key_whole = weight_terms(flat_key, flat_grad_key[:, :key_cut])
    grad_residual, grad_gain_two, grad_bias_two = norm_two_back(grad_normed_two)
    grad_residual = grad_residual + full_out.astype(jnp.float32)
    grad_residual, key_whole = lax.optimization_barrier((grad_residual, key_whole))
    grad_branch = grad_residual.astype(jnp.bfloat16)
    grad_mixer = jnp.einsum(
        "ste,de->std", grad_branch, out_proj, preferred_element_type=jnp.float32
    )
    grad_wkv, grad_gate, block_term, group_sums = recurrence.back_join(
        grad_mixer.reshape(tokens, head_cols), wkv, projected, decayed, group_scale, group_shift
    )
    all_terms = lax.all_gather(block_term, "seq")
    grad_wkv, value_sum, key_whole = lax.optimization_barrier((grad_wkv, value_sum, key_whole))
    key_sum = scattered(key_whole)
    grad_receive, near_key, near_value, running, bonus_sums = recurrence.back_inner(
        projected, log_flat, bonus, grad_wkv, state
    )
    grad_keys, grad_values, grad_log, state_grad, rate_sums = recurrence.back_outer(
        where_here,
        projected,
        log_flat,
        near_key,
        near_value,
        running,
        state,
        all_packed,
        all_terms,
    )

    grad_proj = jnp.stack([grad_receive, grad_keys, grad_values, grad_gate])
    part_block, edge, small_rows, lift_grad = mix_back(
        block_input,
        preceding_first,
        grad_proj,
        grad_log,
        hidden_mixture,
        hidden_decay,
        projections,
        shift_coefficient,
        norm_one,
        lowrank_down,
        lowrank_up,
        decay_projection,
        lift_rows,
        narrow_at + 112,
    )
    from_next_one = from_behind(edge[:, 0].astype(jnp.bfloat16), "seq", -1).astype(jnp.float32)
    _, last_back = jax.vjp(layer_norm, last_input, gains_all[0], biases_all[0])
    part_last, gain_last, bias_last = last_back(from_next_one)
    part_block = add_last(part_block, part_last)
    head_rows = jnp.concatenate(
        [
            lift_grad,
            jnp.sum(rate_sums[:, :1], axis=0),
            jnp.sum(bonus_sums[:, :1], axis=0),
            jnp.sum(group_sums[:, :2], axis=0),
            jnp.zeros((12, head_cols), jnp.float32),
        ]
    )
    thirds = []
    for _ in range(3):
        thirds.append(head_rows.astype(jnp.bfloat16))
        head_rows = head_rows - lax.optimization_barrier(thirds[-1]).astype(jnp.float32)
    head_rows = jnp.sum(
        lax.dot_general(
            jnp.stack(thirds),
            choose,
            (((2,), (1,)), ((), ())),
            preferred_element_type=jnp.float32,
        ),
        axis=0,
    )
    other_rows = jnp.concatenate(
        [
            grad_coeffs_chan[6:],
            jnp.stack([0.5 * grad_gain_two, 0.5 * grad_bias_two, gain_last, bias_last]),
            jnp.zeros((2, feature_columns), jnp.float32),
        ]
    )
    small_rows = lax.dynamic_update_slice(small_rows, other_rows, (8, 0))
    small_rows = lax.dynamic_update_slice(small_rows, head_rows, (narrow_at, 0))
    sent_block = lax.dynamic_slice_in_dim(part_block, (1 - half) * own_cols, own_cols, 2)
    *proj_sums, out_sum, recept_sum, key_rest, value_rest, small_sums, other_block = ring_sums(
        [(stacked, grad_proj, (branch,)) for branch in range(4)]
        + [
            (grad_branch.reshape(tokens, -1), mixer_in.reshape(tokens, -1), ()),
            (chan_recept_b.reshape(tokens, -1), grad_recept.reshape(tokens, -1), ()),
            (flat_key, flat_grad_key[:, key_cut:], ()),
            (flat_value, flat_hidden[:, value_cut:], ()),
        ],
        small_rows,
        sent_block.astype(jnp.bfloat16),
        sizes,
        0,
    )
    small_sums = small_sums.T
    input_grad = own_half(grad_residual) + own_half(part_block) + other_block.astype(jnp.float32)
    shared = small_sums[:narrow_at] + other_half(small_sums[:narrow_at])
    narrow = small_sums[narrow_at:, : heads_here * each]
    head_sums = [
        narrow[decay_ranks + k].reshape(heads_here, each) for k in range(4)
    ]
    return (
        output,
        input_grad,
        state_grad,
        jnp.stack([shared[6] + shared[12], shared[10]]),
        jnp.stack([shared[7] + shared[13], shared[11]]),
        jnp.concatenate([shared[:1], shared[2:6], shared[8:10]], axis=0),
        shared[1:2],
        shared[down_at:decay_at].T,
        shared[up_at:down_at],
        shared[decay_at:].T,
        narrow[:decay_ranks].reshape(decay_ranks, heads_here, each),
        jnp.stack(proj_sums),
        out_sum.T,
        *head_sums,
        jnp.concatenate([key_sum, key_rest], axis=1),
        jnp.concatenate([value_sum, value_rest], axis=1).T,
        recept_sum,
        total_least,
        total_most,
    )


def solution(mesh):
    return jax.shard_map(
        per_device,
        mesh=mesh,
        in_specs=(
            P("dp", "seq", None),
            P("dp", "tp", None, None),
            P(None, ("dp", "seq")),
            P(None, ("dp", "seq")),
            P(None, ("dp", "seq")),
            P(("dp", "seq"), None),
            P(None, ("dp", "seq")),
            P(("dp", "seq"), None),
            P(None, "tp", ("dp", "seq")),
            P(None, ("dp", "seq"), "tp"),
            P("tp", ("dp", "seq")),
            P("tp", ("dp", "seq")),
            P("tp", ("dp", "seq")),
            P("tp", ("dp", "seq")),
            P("tp", ("dp", "seq")),
            P(None, "tp"),
            P("tp", None),
            P(None, "tp"),
            P("dp", "seq", "tp"),
        ),
        out_specs=(
            P("dp", "seq", "tp"),
            P("dp", "seq", "tp"),
            P("dp", "tp", None, None),
            P(None, ("dp", "seq")),
            P(None, ("dp", "seq")),
            P(None, ("dp", "seq")),
            P(None, ("dp", "seq")),
            P(("dp", "seq"), None),
            P(None, ("dp", "seq")),
            P(("dp", "seq"), None),
            P(None, "tp", ("dp", "seq")),
            P(None, ("dp", "seq"), "tp"),
            P("tp", ("dp", "seq")),
            P("tp", ("dp", "seq")),
            P("tp", ("dp", "seq")),
            P("tp", ("dp", "seq")),
            P("tp", ("dp", "seq")),
            P(("dp", "seq"), "tp"),
            P("tp", ("dp", "seq")),
            P(("dp", "seq"), "tp"),
            P("dp", "tp"),
            P("dp", "tp"),
        ),
        check_vma=False,
    )
```
